32 devices in a mesh: dp: 8 (over y, x, core), mp: 4 (over z).
Axes of the slice: x: 2, y: 2, z: 4, core: 2. Of those that a mesh axis runs over, the one named last changes fastest.
Arguments:
- tokens: bfloat16 [16384, 768], P(('dp', 'mp')), may hold values from -6 to 6
- segment_ids: int32 [16384], P('dp'), may hold values from 0 to 1663, as said below
- w_query: bfloat16 [768, 768], P(None, 'mp'), may hold values from -0.21875 to 0.21875
- b_query: float32 [768], P('mp'), may hold values from -3 to 3
- w_key: bfloat16 [768, 768], P(None, 'mp'), may hold values from -0.21875 to 0.21875
- w_value: bfloat16 [768, 768], P(None, 'mp'), may hold values from -0.21875 to 0.21875
- b_value: float32 [768], P('mp'), may hold values from -3 to 3
- w_out: bfloat16 [768, 768], P('mp'), may hold values from -1.75 to 1.75
- b_out: float32 [768], replicated, may hold values from -3 to 3
- gain_one: float32 [768], replicated, may hold values from 0.5 to 1.5
- shift_one: float32 [768], replicated, may hold values from -3 to 3
- w_up: bfloat16 [768, 3072], P(None, 'mp'), may hold values from -0.21875 to 0.21875
- b_up: float32 [3072], P('mp'), may hold values from -3 to 3
- w_down: bfloat16 [3072, 768], P('mp'), may hold values from -0.109375 to 0.109375
- b_down: float32 [768], replicated, may hold values from -3 to 3
- gain_two: float32 [768], replicated, may hold values from 0.5 to 1.5
- shift_two: float32 [768], replicated, may hold values from -3 to 3
- cotangent: bfloat16 [16384, 768], P(('dp', 'mp')), may hold values from -6 to 6
Outputs:
- output: bfloat16 [16384, 768], P(('dp', 'mp'))
- grad_tokens: float32 [16384, 768], P(('dp', 'mp'))
- grad_w_query: float32 [768, 768], P(None, 'mp')
- grad_b_query: float32 [768], P('mp')
- grad_w_key: float32 [768, 768], P(None, 'mp')
- grad_w_value: float32 [768, 768], P(None, 'mp')
- grad_b_value: float32 [768], P('mp')
- grad_w_out: float32 [768, 768], P('mp')
- grad_b_out: float32 [768], replicated
- grad_gain_one: float32 [768], replicated
- grad_shift_one: float32 [768], replicated
- grad_w_up: float32 [768, 3072], P(None, 'mp')
- grad_b_up: float32 [3072], P('mp')
- grad_w_down: float32 [3072, 768], P('mp')
- grad_b_down: float32 [768], replicated
- grad_gain_two: float32 [768], replicated
- grad_shift_two: float32 [768], replicated
The draws below stay inside these ranges and needn't reach their ends.
Inputs may be any that keep to these rules, and one draw needn't show every extreme that they name: `segment_ids`: never falling along the tokens, rising by one at each fragment start; fragments never cross the edge of a packed row of 512 tokens, a fragment starts at every multiple of 128, each fragment covers 1 to 128 consecutive tokens, each packed row has one of exactly 128 and holds exactly 4 + 3 * (16) fragments.
All inputs are finite; a program needn't handle non-finite values.
Results may differ from the reference program's by a relative error of at most 0.012.
Values may be sent and summed in bfloat16 or wider, within the bound.
A program may use at most 128 MiB of HBM per device.

```python
import jax
import jax.numpy as jnp
from jax import lax

D = 768
HEADS = 12
HD = 64
FF = 3072
SEQ = 512
TOKENS = 16384


def draw_segment_ids(key, part):
    key = jax.random.fold_in(key, 11)
    row_total = TOKENS // SEQ
    quarter = SEQ // 4
    picked_count = SEQ // 32
    first_key, second_key = jax.random.split(key)
    position = jnp.arange(quarter, dtype=jnp.int32)
    scores = jax.random.randint(first_key, (row_total, 4, quarter), 0, 1 << 20).astype(jnp.int32) * quarter + position[None, None, :]
    scores = jnp.where(position[None, None, :] == 0, (1 << 20) * quarter + quarter, scores)
    order = jnp.argsort(scores, axis=-1)
    ranks = jnp.argsort(order, axis=-1)
    extra = ranks < picked_count
    drawn = jax.random.randint(second_key, (row_total,), 0, 4)
    keep = jnp.arange(4, dtype=jnp.int32)[None, :] != drawn[:, None]
    first = position == 0
    starts = first[None, None, :] | extra & keep[:, :, None]
    flat = starts.reshape(-1).astype(jnp.int32)
    return (jnp.cumsum(flat) - 1).astype(jnp.int32)


def level_of(rng, dims, cuts, low, top_value):
    def one(dim, blocks):
        heights = jax.random.uniform(jax.random.fold_in(jax.random.fold_in(rng, 6), dim), (blocks,), jnp.float32, low / len(cuts), top_value / len(cuts))
        return jnp.repeat(jnp.exp(heights), dims[dim] // blocks).reshape((-1,) + (1,) * (len(dims) - dim - 1))

    factor_of = one(*cuts[0])
    for cut in cuts[1:]:
        factor_of = factor_of * one(*cut)
    return factor_of


def centred(key, extent, width, reach, cuts=(), kind=jnp.bfloat16):
    entries = jax.random.normal(key, extent, jnp.float32) * width
    if len(cuts) > 0:
        entries = level_of(key, extent, cuts, -0.22, 0.18) * entries
    return jnp.clip(entries, min=-reach, max=reach).astype(kind)


def setup_inputs(seed: int = 0) -> dict:
    key_of = jax.random.split(jax.random.key(seed), 19)
    return {
        "tokens": centred(key_of[0], (TOKENS, D), 1.0, 6.0, ((0, 32),)),
        "segment_ids": draw_segment_ids(jax.random.fold_in(key_of[18], 71), 0),
        "w_query": centred(key_of[2], (D, D), D ** -0.5, 0.21875, ((1, 4),)),
        "b_query": centred(key_of[3], (D,), 0.5, 3.0, ((0, 4),), jnp.float32),
        "w_key": centred(key_of[4], (D, D), D ** -0.5, 0.21875, ((1, 4),)),
        "w_value": centred(key_of[5], (D, D), D ** -0.5, 0.21875, ((1, 4),)),
        "b_value": centred(key_of[6], (D,), 0.5, 3.0, ((0, 4),), jnp.float32),
        "w_out": centred(key_of[7], (D, D), (D // 64) ** -0.5, 1.75, ((0, 4),)),
        "b_out": centred(key_of[8], (D,), 0.5, 3.0, (), jnp.float32),
        "gain_one": jnp.clip(1.0 + 0.1 * jax.random.normal(key_of[9], (D,), jnp.float32), 0.5, 1.5),
        "shift_one": centred(key_of[10], (D,), 0.5, 3.0, (), jnp.float32),
        "w_up": centred(key_of[11], (D, FF), D ** -0.5, 0.21875, ((1, 4),)),
        "b_up": centred(key_of[12], (FF,), 0.5, 3.0, ((0, 4),), jnp.float32),
        "w_down": centred(key_of[13], (FF, D), FF ** -0.5, 0.109375, ((0, 4),)),
        "b_down": centred(key_of[14], (D,), 0.5, 3.0, (), jnp.float32),
        "gain_two": jnp.clip(1.0 + 0.1 * jax.random.normal(key_of[15], (D,), jnp.float32), 0.5, 1.5),
        "shift_two": centred(key_of[16], (D,), 0.5, 3.0, (), jnp.float32),
        "cotangent": centred(key_of[17], (TOKENS, D), 1.0, 6.0, ((0, 32),)),
    }


@jax.custom_vjp
def low(v):
    return lax.optimization_barrier(v.astype(jnp.bfloat16)).astype(jnp.float32)

@jax.custom_vjp
def low_back(v):
    return v

def low_keep(v):
    return (low(v), None)

def low_pass(kept, grad):
    return (grad,)

def back_keep(v):
    return (v, None)

def back_low(kept, grad):
    return (low(grad),)
low.defvjp(low_keep, low_pass)
low_back.defvjp(back_keep, back_low)
HIGH = lax.Precision.HIGHEST

def matmul(left, right):
    return jnp.dot(left, right, precision=HIGH, preferred_element_type=jnp.float32)

def layer_norm(value, gain, shift):
    center = value - lax.optimization_barrier(jnp.mean(value, axis=-1, keepdims=True))
    variance = lax.optimization_barrier(jnp.mean(center * center, axis=-1, keepdims=True))
    return center * lax.rsqrt(variance + 1e-05) * gain + shift

def attend_row(inputs):
    query, key, value, segment = inputs
    score = jnp.einsum('qhd,khd->hqk', query, key, precision=HIGH) * HD ** (-0.5)
    score = low_back(score)
    same = segment[:, None] == segment[None, :]
    score = jnp.where(same[None], score, -1000000000.0)
    top = lax.optimization_barrier(jnp.max(score, axis=-1, keepdims=True))
    expo = jnp.exp(score - top)
    prob = low(expo / lax.optimization_barrier(jnp.sum(expo, axis=-1, keepdims=True)))
    return jnp.einsum('hqk,khd->qhd', prob, value, precision=HIGH)

def forward(params, inputs):
    w_query, b_query, w_key, w_value, b_value, w_out, b_out, gain_one, shift_one, w_up, b_up, w_down, b_down, gain_two, shift_two = params
    tokens, segment_ids = inputs
    x_low = low(tokens)
    query = low(low_back(matmul(x_low, w_query) + b_query))
    key = low(low_back(matmul(x_low, w_key)))
    value = low(low_back(matmul(x_low, w_value) + b_value))
    row_count = tokens.shape[0] // SEQ
    shape4 = (row_count, SEQ, HEADS, HD)
    context = lax.map(jax.checkpoint(attend_row), (query.reshape(shape4), key.reshape(shape4), value.reshape(shape4), segment_ids.reshape(row_count, SEQ)))
    context = low(low_back(context.reshape(tokens.shape[0], D)))
    attn = low_back(matmul(context, w_out))
    normed_one = layer_norm(tokens + attn + b_out, gain_one, shift_one)
    up = low_back(matmul(low(normed_one), w_up) + b_up)
    act = low(jax.nn.gelu(up, approximate=True))
    ffn = low_back(matmul(act, w_down))
    return layer_norm(normed_one + ffn + b_down, gain_two, shift_two)

def reference(tokens, segment_ids, w_query, b_query, w_key, w_value, b_value, w_out, b_out, gain_one, shift_one, w_up, b_up, w_down, b_down, gain_two, shift_two, cotangent):
    params = tuple((p.astype(jnp.float32) for p in (w_query, b_query, w_key, w_value, b_value, w_out, b_out, gain_one, shift_one, w_up, b_up, w_down, b_down, gain_two, shift_two)))
    x_full = tokens.astype(jnp.float32)

    def run(params, x_full):
        return forward(params, (x_full, segment_ids))
    output, pull = jax.vjp(run, params, x_full)
    grads, grad_tokens = pull(cotangent.astype(jnp.float32))
    g_wq, g_bq, g_wk, g_wv, g_bv, g_wo, g_bo, g_g1, g_s1, g_wu, g_bu, g_wd, g_bd, g_g2, g_s2 = grads
    return (output.astype(jnp.bfloat16), grad_tokens, g_wq, g_bq, g_wk, g_wv, g_bv, g_wo, g_bo, g_g1, g_s1, g_wu, g_bu, g_wd, g_bd, g_g2, g_s2)
```

```python
from functools import partial

import jax
import jax.numpy as jnp
from jax import lax
from jax.sharding import PartitionSpec as P

HD = 64
BLOCK = 128


def matmul(left, right):
    return jnp.dot(left, right, preferred_element_type=jnp.float32)


def rows_product(left, right):
    return lax.dot_general(
        left, right, (((0,), (0,)), ((), ())), preferred_element_type=jnp.float32
    )


def times_transpose(left, right):
    return lax.dot_general(
        left, right, (((1,), (1,)), ((), ())), preferred_element_type=jnp.float32
    )


def norm_forward(value, gain, shift):
    center = value - jnp.mean(value, axis=-1, keepdims=True)
    variance = jnp.mean(center * center, axis=-1, keepdims=True)
    inverse = lax.rsqrt(variance + 1e-05)
    unit = center * inverse
    return (unit * gain + shift, unit, inverse)


def norm_backward(grad, unit, inverse, gain):
    scaled = grad * gain
    inner = (
        scaled
        - jnp.mean(scaled, axis=-1, keepdims=True)
        - unit * jnp.mean(scaled * unit, axis=-1, keepdims=True)
    )
    return (inverse * inner, jnp.sum(grad * unit, axis=0), jnp.sum(grad, axis=0))


def einsum(spec, left, right):
    return jnp.einsum(spec, left, right, preferred_element_type=jnp.float32)


def per_device(
    tokens,
    segment_ids,
    w_query,
    b_query,
    w_key,
    w_value,
    b_value,
    w_out,
    b_out,
    gain_one,
    shift_one,
    w_up,
    b_up,
    w_down,
    b_down,
    gain_two,
    shift_two,
    cotangent,
):
    rows, width = tokens.shape
    heads = width // HD
    blocks = rows // BLOCK
    low = jnp.bfloat16

    def whole(array, axis):
        return lax.all_gather(array, "mp", axis=axis, tiled=True)

    w_query, w_key, w_value = whole(w_query, 1), whole(w_key, 1), whole(w_value, 1)
    b_query, b_value, b_up = whole(b_query, 0), whole(b_value, 0), whole(b_up, 0)
    w_out, w_up, w_down = whole(w_out, 0), whole(w_up, 1), whole(w_down, 0)

    segment = lax.dynamic_slice(segment_ids, (lax.axis_index("mp") * rows,), (rows,))
    segment = segment.reshape(blocks, BLOCK)
    shape4 = (blocks, BLOCK, heads, HD)
    query = (matmul(tokens, w_query) + b_query).astype(low).reshape(shape4)
    key = matmul(tokens, w_key).astype(low).reshape(shape4)
    value = (matmul(tokens, w_value) + b_value).astype(low).reshape(shape4)
    score = einsum("bqhd,bkhd->bhqk", query, key) * HD ** (-0.5)
    same = segment[:, :, None] == segment[:, None, :]
    score = jnp.where(same[:, None], score, -1000000000.0)
    expo = jnp.exp(score - jnp.max(score, axis=-1, keepdims=True))
    prob = expo / jnp.sum(expo, axis=-1, keepdims=True)
    prob_low = prob.astype(low)
    context = einsum("bhqk,bkhd->bqhd", prob_low, value).astype(low).reshape(rows, width)
    normed_one, unit_one, inverse_one = norm_forward(
        tokens.astype(jnp.float32) + matmul(context, w_out) + b_out, gain_one, shift_one
    )
    normed_low = normed_one.astype(low)
    up_value = matmul(normed_low, w_up) + b_up
    act_low = jax.nn.gelu(up_value, approximate=True).astype(low)
    out_value, unit_two, inverse_two = norm_forward(
        normed_one + matmul(act_low, w_down) + b_down, gain_two, shift_two
    )
    grad_resid_two, grad_gain_two, grad_shift_two = norm_backward(
        cotangent.astype(jnp.float32), unit_two, inverse_two, gain_two
    )
    grad_b_down = jnp.sum(grad_resid_two, axis=0)
    grad_two_low = grad_resid_two.astype(low)
    grad_w_down = rows_product(act_low, grad_two_low)
    grad_act = times_transpose(grad_two_low, w_down)
    unused, gelu_pull = jax.vjp(partial(jax.nn.gelu, approximate=True), up_value)
    grad_up = gelu_pull(grad_act)[0].astype(low)
    grad_b_up = jnp.sum(grad_up.astype(jnp.float32), axis=0)
    grad_w_up = rows_product(normed_low, grad_up)
    grad_normed_one = grad_resid_two + times_transpose(grad_up, w_up)
    grad_resid_one, grad_gain_one, grad_shift_one = norm_backward(
        grad_normed_one, unit_one, inverse_one, gain_one
    )
    grad_b_out = jnp.sum(grad_resid_one, axis=0)
    grad_one_low = grad_resid_one.astype(low)
    grad_w_out = rows_product(context, grad_one_low)
    grad_context = times_transpose(grad_one_low, w_out).astype(low).reshape(shape4)
    grad_prob = einsum("bqhd,bkhd->bhqk", grad_context, value)
    grad_value = einsum("bhqk,bqhd->bkhd", prob_low, grad_context).astype(low)
    grad_score = prob * (grad_prob - jnp.sum(grad_prob * prob, axis=-1, keepdims=True))
    grad_score = grad_score.astype(low)
    grad_query = (einsum("bhqk,bkhd->bqhd", grad_score, key) * HD ** (-0.5)).astype(low)
    grad_key = (einsum("bhqk,bqhd->bkhd", grad_score, query) * HD ** (-0.5)).astype(low)
    grad_query = grad_query.reshape(rows, width)
    grad_key = grad_key.reshape(rows, width)
    grad_value = grad_value.reshape(rows, width)
    grad_w_query = rows_product(tokens, grad_query)
    grad_w_key = rows_product(tokens, grad_key)
    grad_w_value = rows_product(tokens, grad_value)
    grad_b_query = jnp.sum(grad_query.astype(jnp.float32), axis=0)
    grad_b_value = jnp.sum(grad_value.astype(jnp.float32), axis=0)
    grad_tokens = (
        grad_resid_one
        + times_transpose(grad_query, w_query)
        + times_transpose(grad_key, w_key)
        + times_transpose(grad_value, w_value)
    )

    def share(array, axis):
        part = lax.psum_scatter(
            array.astype(low), "mp", scatter_dimension=axis, tiled=True
        )
        return lax.psum(part, "dp").astype(jnp.float32)

    def share_small(array):
        return lax.psum_scatter(array, "mp", scatter_dimension=0, tiled=True)

    grad_w_down = share(grad_w_down, 0)
    grad_w_up = share(grad_w_up, 1)
    grad_w_out = share(grad_w_out, 0)
    grad_w_query = share(grad_w_query, 1)
    grad_w_key = share(grad_w_key, 1)
    grad_w_value = share(grad_w_value, 1)
    grad_b_query, grad_b_value, grad_b_up = lax.psum(
        (share_small(grad_b_query), share_small(grad_b_value), share_small(grad_b_up)), "dp"
    )
    grad_b_out, grad_gain_one, grad_shift_one, grad_b_down, grad_gain_two, grad_shift_two = (
        lax.psum(
            (grad_b_out, grad_gain_one, grad_shift_one, grad_b_down, grad_gain_two, grad_shift_two),
            ("dp", "mp"),
        )
    )
    return (
        out_value.astype(low),
        grad_tokens,
        grad_w_query,
        grad_b_query,
        grad_w_key,
        grad_w_value,
        grad_b_value,
        grad_w_out,
        grad_b_out,
        grad_gain_one,
        grad_shift_one,
        grad_w_up,
        grad_b_up,
        grad_w_down,
        grad_b_down,
        grad_gain_two,
        grad_shift_two,
    )


def solution(mesh):
    return jax.shard_map(
        per_device,
        mesh=mesh,
        in_specs=(
            P(("dp", "mp"), None),
            P("dp"),
            P(None, "mp"),
            P("mp"),
            P(None, "mp"),
            P(None, "mp"),
            P("mp"),
            P("mp", None),
            P(),
            P(),
            P(),
            P(None, "mp"),
            P("mp"),
            P("mp", None),
            P(),
            P(),
            P(),
            P(("dp", "mp"), None),
        ),
        out_specs=(
            P(("dp", "mp"), None),
            P(("dp", "mp"), None),
            P(None, "mp"),
            P("mp"),
            P(None, "mp"),
            P(None, "mp"),
            P("mp"),
            P("mp", None),
            P(),
            P(),
            P(),
            P(None, "mp"),
            P("mp"),
            P("mp", None),
            P(),
            P(),
            P(),
        ),
        check_vma=False,
    )
```

```python
import functools

import jax
import jax.numpy as jnp
from jax import lax
from jax.experimental import pallas as pl
from jax.experimental.pallas import tpu as pltpu
from jax.sharding import PartitionSpec as P

HD = 64
BLOCK = 128
TILE = 256
ROWS = 64
PLANE = 8
MASKED = -1000000000.0
MESH = pl.DeviceIdType.MESH
F32 = jnp.float32
LOW = jnp.bfloat16


def dot(left, right):
    return jnp.dot(left, right, preferred_element_type=F32)


def dot_nt(left, right):
    return lax.dot_general(left, right, (((1,), (1,)), ((), ())), preferred_element_type=F32)


def mean(value):
    return jnp.mean(value, axis=-1, keepdims=True)


def total(value):
    return jnp.sum(value, axis=0, keepdims=True)


def at(start, size, unit):
    return pl.ds(pl.multiple_of(start, unit), size)


def loop(count, body, unroll=1):
    def step(index, carry):
        body(index)
        return carry

    lax.fori_loop(0, count, step, 0, unroll=unroll)


class Links:
    def __init__(self, send, recv):
        self.send, self.recv = send, recv
        self.names = {}
        self.open = []

    def index(self, name):
        return self.names.setdefault(name, len(self.names))

    def copy(self, name, src, dst, device):
        k = self.index(name)
        return pltpu.make_async_remote_copy(
            src_ref=src,
            dst_ref=dst,
            send_sem=self.send.at[k],
            recv_sem=self.recv.at[k],
            device_id=device,
            device_id_type=MESH,
        )

    def start(self, name, src, dst, device):
        copy = self.copy(name, src, dst, device)
        copy.start()
        self.open.append(copy)

    def wait(self, name, dst, device):
        self.copy(name, dst, dst, device).wait_recv()

    def drain(self):
        for copy in self.open:
            copy.wait_send()
        self.open = []


def layer_kernel(
    n_mp,
    tok,
    cot,
    seg,
    w_query,
    w_key,
    w_value,
    b_query,
    b_value,
    b_up,
    b_out,
    gain_one,
    shift_one,
    b_down,
    gain_two,
    shift_two,
    w_out,
    w_up,
    w_down,
    out,
    grad_tok,
    grad_w,
    grad_small,
    w,
    half_in,
    quarter_in,
    eighth_in,
    plane_in,
    qkv,
    grad_qkv_t,
    prob,
    ctx,
    ctx_t,
    unit_one,
    inv_one,
    normed,
    normed_t,
    acc,
    grad_low,
    act,
    act_t,
    slope,
    up_tmp,
    mask,
    bias_in,
    qkv_bias,
    up_bias,
    small,
    small_in,
    small_up,
    small_plane,
    local_sem,
    send_sem,
    recv_sem,
):
    rows, d = tok.shape
    group = n_mp * d
    shard = d // n_mp
    piece = d // 16
    tiles = d // TILE
    pairs = d // BLOCK
    blocks = rows // BLOCK

    dp, me = lax.axis_index("dp"), lax.axis_index("mp")
    c, x, y = dp % 2, dp // 2 % 2, dp // 4 % 2
    core = (dp + 1 - 2 * c, me)
    x_side = (dp + 2 - 4 * x, me)
    y_side = (dp + 4 - 8 * y, me)

    def plane(step):
        return (me + step) % n_mp

    def rows_of(start, size):
        return at(start, size, 16)

    local = [
        pltpu.make_async_copy(w_out, w.at[rows_of(3 * d + me * shard, shard)], local_sem.at[0]),
        pltpu.make_async_copy(w_up, w.at[rows_of(group + me * d, d)], local_sem.at[1]),
        pltpu.make_async_copy(w_down, w.at[rows_of(2 * group + me * d, d)], local_sem.at[2]),
    ]
    for copy in local:
        copy.start()

    barrier = pltpu.get_barrier_semaphore()
    partners = [core, x_side, y_side] + [(dp, plane(s)) for s in range(1, n_mp)]
    for partner in partners:
        pl.semaphore_signal(barrier, inc=1, device_id=partner, device_id_type=MESH)

    for kind, ref in enumerate((w_query, w_key, w_value)):
        w[rows_of(kind * d + me * shard, shard), :] = ref[...].T

    pad = jnp.zeros((1, d - shard), F32)
    for k, ref in enumerate((b_query, b_value)):
        placed = jnp.broadcast_to(jnp.concatenate([ref[...], pad], axis=1), (8, d))
        bias_in[me, k : k + 1, :] = pltpu.roll(placed, me * shard, 1)[0:1, :]
    bias_in[me, 2:3, :] = b_up[...]

    pl.semaphore_wait(barrier, len(partners))
    for copy in local:
        copy.wait()

    links = Links(send_sem, recv_sem)

    def region(g, m, core_of, side):
        if g == 0:
            return (2 * core_of + side) * d + m * shard
        return g * group + m * d + core_of * (d // 2) + side * (d // 4)

    class Gather:
        def __init__(self, name, ref, mine, theirs):
            self.name, self.ref = name, ref
            self.mine, self.theirs = mine, theirs

        def at(self, start, size):
            return self.ref.at[rows_of(start, size)]

        def one(self):
            a = self.at(self.mine[0] + (2 * x + y) * piece, piece)
            b = self.at(self.mine[1] + (2 * y + x) * piece, piece)
            links.start((self.name, 1, 0), a, a, y_side)
            links.start((self.name, 1, 1), b, b, x_side)

        def two(self):
            links.wait(
                (self.name, 1, 0), self.at(self.mine[0] + (2 * x + 1 - y) * piece, piece), y_side
            )
            a = self.at(self.mine[0] + 2 * x * piece, 2 * piece)
            links.start((self.name, 2, 0), a, a, x_side)
            links.wait(
                (self.name, 1, 1), self.at(self.mine[1] + (2 * y + 1 - x) * piece, piece), x_side
            )
            b = self.at(self.mine[1] + 2 * y * piece, 2 * piece)
            links.start((self.name, 2, 1), b, b, y_side)

        def three(self):
            links.wait(
                (self.name, 2, 0), self.at(self.mine[0] + 2 * (1 - x) * piece, 2 * piece), x_side
            )
            a = self.at(self.mine[0], 4 * piece)
            links.start((self.name, 3, 0), a, a, core)
            links.wait(
                (self.name, 2, 1), self.at(self.mine[1] + 2 * (1 - y) * piece, 2 * piece), y_side
            )
            b = self.at(self.mine[1], 4 * piece)
            links.start((self.name, 3, 1), b, b, core)

        def done(self):
            for side in range(2):
                links.wait((self.name, 3, side), self.at(self.theirs[side], 4 * piece), core)

    for s in range(1, n_mp):
        links.start(("bias", s), bias_in.at[me], bias_in.at[me], (dp, plane(s)))
    for g in range(3):
        for s in range(1, n_mp):
            a = w.at[rows_of(region(g, me, c, 0) + (2 * x + y) * piece, piece)]
            b = w.at[rows_of(region(g, me, c, 1) + (2 * y + x) * piece, piece)]
            links.start(("w", g, s, 0), a, a, (dp, plane(s)))
            links.start(("w", g, s, 1), b, b, (dp, plane(s)))

    gathers = {}
    for g in range(3):
        for s in range(1, n_mp):
            m = plane(n_mp - s)
            gathers[g, s] = Gather(
                ("in", g, s),
                w,
                [region(g, m, c, side) for side in range(2)],
                [region(g, m, 1 - c, side) for side in range(2)],
            )

    def arrive(g, s):
        m = plane(n_mp - s)
        from_plane = (dp, m)
        a = w.at[rows_of(region(g, m, c, 0) + (2 * x + y) * piece, piece)]
        b = w.at[rows_of(region(g, m, c, 1) + (2 * y + x) * piece, piece)]
        links.wait(("w", g, s, 0), a, from_plane)
        links.wait(("w", g, s, 1), b, from_plane)
        gathers[g, s].one()

    keys = list(gathers)
    ticks = []
    for t in range(len(keys) + 3):
        step = []
        if t < len(keys):
            step.append(functools.partial(arrive, *keys[t]))
        if 0 <= t - 1 < len(keys):
            step.append(gathers[keys[t - 1]].two)
        if 0 <= t - 2 < len(keys):
            step.append(gathers[keys[t - 2]].three)
        if 0 <= t - 3 < len(keys):
            step.append(gathers[keys[t - 3]].done)
        ticks.append(step)

    def tick(count):
        for _ in range(count):
            for action in ticks.pop(0):
                action()

    for b in range(blocks):
        line = seg[pl.ds(me * blocks + b, 1), :]
        across = jnp.broadcast_to(line, (BLOCK, BLOCK))
        mask[b] = jnp.where(across == across.T, 0.0, MASKED)

    tick(3)
    bias_all = jnp.zeros((8, d), F32)
    for s in range(1, n_mp):
        m = plane(n_mp - s)
        links.wait(("bias", s), bias_in.at[m], (dp, m))
    row_b = jnp.zeros((2, d), F32)
    for m in range(n_mp):
        row_b = row_b + bias_in[m, 0:2, :]
    for t in range(tiles):
        columns = slice(t * TILE, (t + 1) * TILE)
        qkv_bias[t] = row_b[0:1, columns]
        qkv_bias[tiles + t] = jnp.zeros((1, TILE), F32)
        qkv_bias[2 * tiles + t] = row_b[1:2, columns]
        for m in range(n_mp):
            up_bias[m * tiles + t] = bias_in[m, 2:3, columns]
    tick(3)

    def project(n):
        part = dot_nt(tok[...], w[at(n * TILE, TILE, TILE), :]) + qkv_bias[n]
        qkv[2 * n] = part[:, :BLOCK].astype(LOW)
        qkv[2 * n + 1] = part[:, BLOCK:].astype(LOW)

    loop(3 * tiles, project)

    lane = lax.broadcasted_iota(jnp.int32, (1, BLOCK), 1)
    first = jnp.where(lane < HD, 1.0, 0.0).astype(LOW)
    second = jnp.where(lane < HD, 0.0, 1.0).astype(LOW)

    def two_heads(value):
        return jnp.concatenate([value * first, value * second], axis=0)

    def softmax(score):
        expo = jnp.exp(score - jnp.max(score, axis=-1, keepdims=True))
        return expo / jnp.sum(expo, axis=-1, keepdims=True)

    def attend(index):
        b, p = index // pairs, index % pairs
        here = at(b * BLOCK, BLOCK, BLOCK)
        query = qkv[p, here, :]
        key = qkv[pairs + p, here, :]
        value = qkv[2 * pairs + p, here, :]
        score = dot_nt(query, two_heads(key)) * HD**-0.5
        hidden = mask[b]
        both = jnp.concatenate(
            [softmax(score[:, :BLOCK] + hidden), softmax(score[:, BLOCK:] + hidden)], axis=1
        ).astype(LOW)
        prob[index] = both
        context = dot(both, two_heads(value)).astype(LOW)
        ctx[here, at(p * BLOCK, BLOCK, BLOCK)] = context
        ctx_t[at(p * BLOCK, BLOCK, BLOCK), here] = context.T

    for _ in range(3):
        base = _ * (blocks * pairs // 3)
        loop(blocks * pairs // 3, lambda i, base=base: attend(base + i), unroll=2)
        tick(1)

    def attn_out(n):
        columns = at(n * TILE, TILE, TILE)
        acc[:, columns] = dot(ctx[...], w[3 * d : 4 * d, columns])

    loop(tiles, attn_out)

    def norm_one(r):
        here = at(r * ROWS, ROWS, ROWS)
        value = tok[here, :].astype(F32) + acc[here, :] + b_out[...]
        center = value - mean(value)
        inverse = lax.rsqrt(mean(center * center) + 1e-05)
        unit = center * inverse
        unit_one[here, :] = unit
        inv_one[here, :] = jnp.broadcast_to(inverse, (ROWS, BLOCK))
        normed[here, :] = (unit * gain_one[...] + shift_one[...]).astype(LOW)

    loop(rows // ROWS, norm_one)

    def turn(r):
        here = at(r * BLOCK, BLOCK, BLOCK)
        normed_t[:, here] = normed[here, :].T

    loop(blocks, turn)

    def feed_up(m):
        def one(n):
            t = m * tiles + n
            weight = w[rows_of(group + m * d, d), at(n * TILE, TILE, TILE)]
            up_tmp[...] = dot(normed[...], weight) + up_bias[t]

            def gelu(r):
                here = at(r * ROWS, ROWS, ROWS)
                u = up_tmp[here, :]
                square = u * u
                inner = jnp.tanh(0.7978845608028654 * (u + 0.044715 * (square * u)))
                cdf = 0.5 + 0.5 * inner
                act[t, here, :] = (u * cdf).astype(LOW)
                slope_in = 0.7978845608028654 + (3 * 0.044715 * 0.7978845608028654) * square
                slope[t, here, :] = (cdf + 0.5 * u * (1.0 - inner * inner) * slope_in).astype(LOW)

            loop(rows // ROWS, gelu)
            for k in range(TILE // BLOCK):
                act_t[t, k * BLOCK : (k + 1) * BLOCK, :] = act[
                    t, :, k * BLOCK : (k + 1) * BLOCK
                ].T

        loop(tiles, one)

    def columns_of(m):
        return jnp.concatenate([act[m * tiles + t] for t in range(tiles)], axis=1)

    def feed_down(m, opening):
        whole = columns_of(m)

        def one(n):
            columns = at(n * TILE, TILE, TILE)
            part = dot(whole, w[rows_of(2 * group + m * d, d), columns])
            acc[:, columns] = part if opening else acc[:, columns] + part

        loop(tiles, one)

    feed_up(me)
    for s in range(1, n_mp):
        if len(ticks) > 3:
            tick(1)
        feed_up(plane(n_mp - s))
    feed_down(me, True)
    for s in range(1, n_mp):
        while len(ticks) > n_mp - 1 - s:
            tick(1)
        feed_down(plane(n_mp - s), False)
    links.drain()

    small[...] = jnp.zeros(small.shape, F32)

    def add_small(row, value):
        small[0, row : row + 1, :] = small[0, row : row + 1, :] + value

    def norm_two(r):
        here = at(r * ROWS, ROWS, ROWS)
        unit = unit_one[here, :]
        value = unit * gain_one[...] + shift_one[...] + acc[here, :] + b_down[...]
        center = value - mean(value)
        inverse = lax.rsqrt(mean(center * center) + 1e-05)
        unit = center * inverse
        out[here, :] = (unit * gain_two[...] + shift_two[...]).astype(LOW)
        grad = cot[here, :].astype(F32)
        scaled = grad * gain_two[...]
        grad_resid = inverse * (scaled - mean(scaled) - unit * mean(scaled * unit))
        acc[here, :] = grad_resid
        grad_low[here, :] = grad_resid.astype(LOW)
        add_small(5, total(grad_resid))
        add_small(6, total(grad * unit))
        add_small(7, total(grad))

    loop(rows // ROWS, norm_two)

    def block_of(g, s):
        return g * n_mp + s

    def add_rows(start, source, offset, size):
        def one(k):
            here = rows_of(start + k * 16, 16)
            there = rows_of(offset + k * 16, 16)
            w[here, :] = (w[here, :].astype(F32) + source[there, :].astype(F32)).astype(LOW)

        loop(size // 16, one)

    def halve(g, s):
        m, k = plane(s), block_of(g, s)
        for side in range(2):
            links.start(
                ("half", k, side),
                w.at[rows_of(region(g, m, 1 - c, side), 4 * piece)],
                half_in.at[k, side],
                core,
            )

    def quarter(g, s):
        m, k = plane(s), block_of(g, s)
        for side, (bit, device) in enumerate(((x, x_side), (y, y_side))):
            start = region(g, m, c, side)
            links.wait(("half", k, side), half_in.at[k, side], core)
            other = 2 * (1 - bit) * piece
            add_rows(start + other, half_in.at[k, side], other, 2 * piece)
            links.start(
                ("quarter", k, side),
                w.at[rows_of(start + other, 2 * piece)],
                quarter_in.at[k, side],
                device,
            )
        for side, bit in enumerate((x, y)):
            start = region(g, m, c, side)
            own = 2 * bit * piece
            add_rows(start + own, half_in.at[k, side], own, 2 * piece)

    def eighth(g, s):
        m, k = plane(s), block_of(g, s)
        sides = ((x, y, x_side, y_side), (y, x, y_side, x_side))
        for side, (high, bit, before, device) in enumerate(sides):
            start = region(g, m, c, side) + 2 * high * piece
            links.wait(("quarter", k, side), quarter_in.at[k, side], before)
            other = (1 - bit) * piece
            add_rows(start + other, quarter_in.at[k, side], other, piece)
            links.start(
                ("eighth", k, side),
                w.at[rows_of(start + other, piece)],
                eighth_in.at[k, side],
                device,
            )
        for side, (high, bit, before, device) in enumerate(sides):
            start = region(g, m, c, side) + 2 * high * piece
            own = bit * piece
            add_rows(start + own, quarter_in.at[k, side], own, piece)

    def to_plane(g, s):
        m, k = plane(s), block_of(g, s)
        for side, (first_bit, bit, device) in enumerate(((x, y, y_side), (y, x, x_side))):
            start = region(g, m, c, side) + (2 * first_bit + bit) * piece
            links.wait(("eighth", k, side), eighth_in.at[k, side], device)
            add_rows(start, eighth_in.at[k, side], 0, piece)
            if s:
                links.start(
                    ("plane", g, s, side),
                    w.at[rows_of(start, piece)],
                    plane_in.at[g, s - 1, side],
                    (dp, m),
                )

    outs = [
        Gather(
            ("out", g),
            grad_w.at[g],
            [c * (d // 2) + side * (d // 4) for side in range(2)],
            [(1 - c) * (d // 2) + side * (d // 4) for side in range(2)],
        )
        for g in range(3)
    ]

    def finish(g):
        for side, (first_bit, bit) in enumerate(((x, y), (y, x))):
            start = region(g, me, c, side) + (2 * first_bit + bit) * piece
            goal = c * (d // 2) + side * (d // 4) + (2 * first_bit + bit) * piece
            for s in range(1, n_mp):
                links.wait(
                    ("plane", g, s, side), plane_in.at[g, s - 1, side], (dp, plane(n_mp - s))
                )

            def one(k):
                value = w[rows_of(start + k * 16, 16), :].astype(F32)
                for s in range(1, n_mp):
                    value = value + plane_in[g, s - 1, side, rows_of(k * 16, 16), :].astype(F32)
                grad_w[g, rows_of(goal + k * 16, 16), :] = value.astype(LOW)

            loop(piece // 16, one)
        outs[g].one()

    order = [s for s in range(1, n_mp)] + [0]
    queue = []

    def advance(count):
        for _ in range(min(count, len(queue))):
            queue.pop(0)()

    def down_back(m):
        def one(n):
            t = m * tiles + n
            here = rows_of(2 * group + t * TILE, TILE)
            grad = grad_low[...]
            grad_up = (dot_nt(grad, w[here, :]) * slope[t].astype(F32)).astype(LOW)
            act[t] = grad_up
            small_up[t] = total(grad_up.astype(F32))
            w[here, :] = dot(act_t[t], grad).astype(LOW)

        loop(tiles, one)

    def up_back(m):
        whole = columns_of(m)

        def one(n):
            here = rows_of(group + m * d + n * TILE, TILE)
            columns = at(n * TILE, TILE, TILE)
            acc[:, columns] = acc[:, columns] + dot_nt(whole, w[here, :])
            w[here, :] = dot(normed_t[columns, :], whole).astype(LOW)

        loop(tiles, one)

    for s in order:
        down_back(plane(s))
        halve(2, s)
        advance(1)
        queue.append(functools.partial(quarter, 2, s))
    for k, s in enumerate(order):
        up_back(plane(s))
        halve(1, s)
        advance(1)
        queue.append(functools.partial(quarter, 1, s))
    queue.extend(functools.partial(eighth, 2, s) for s in order)
    queue.extend(functools.partial(to_plane, 2, s) for s in order)

    def norm_one_back(r):
        here = at(r * ROWS, ROWS, ROWS)
        grad = acc[here, :]
        unit = unit_one[here, :]
        scaled = grad * gain_one[...]
        inverse = inv_one[here, 0:1]
        grad_resid = inverse * (scaled - mean(scaled) - unit * mean(scaled * unit))
        grad_tok[here, :] = grad_resid
        grad_low[here, :] = grad_resid.astype(LOW)
        add_small(2, total(grad_resid))
        add_small(3, total(grad * unit))
        add_small(4, total(grad))

    loop(rows // ROWS, norm_one_back)
    advance(1)

    def out_back(n):
        here = rows_of(3 * d + n * TILE, TILE)
        columns = at(n * TILE, TILE, TILE)
        grad = grad_low[...]
        ctx[:, columns] = dot_nt(grad, w[here, :]).astype(LOW)
        w[here, :] = dot(ctx_t[columns, :], grad).astype(LOW)

    loop(tiles, out_back)
    advance(1)

    def attend_back(index):
        b, p = index // pairs, index % pairs
        here = at(b * BLOCK, BLOCK, BLOCK)
        query = qkv[p, here, :]
        key = qkv[pairs + p, here, :]
        value = qkv[2 * pairs + p, here, :]
        grad = ctx[here, at(p * BLOCK, BLOCK, BLOCK)]
        both = prob[index]
        grad_prob = dot_nt(grad, two_heads(value))
        wide = both.astype(F32)

        def score_back(columns):
            part, grad_part = wide[:, columns], grad_prob[:, columns]
            return part * (grad_part - jnp.sum(part * grad_part, axis=-1, keepdims=True))

        low_score = jnp.concatenate(
            [score_back(slice(0, BLOCK)), score_back(slice(BLOCK, 2 * BLOCK))], axis=1
        ).astype(LOW)

        def turned(pair):
            return jnp.concatenate([pair[:, :BLOCK].T, pair[:, BLOCK:].T], axis=1)

        grads = (
            (dot(low_score, two_heads(key)) * HD**-0.5).astype(LOW),
            (dot(turned(low_score), two_heads(query)) * HD**-0.5).astype(LOW),
            dot(turned(both), two_heads(grad)).astype(LOW),
        )
        for kind, value in enumerate(grads):
            qkv[kind * pairs + p, here, :] = value
            grad_qkv_t[at((kind * pairs + p) * BLOCK, BLOCK, BLOCK), here] = value.T

    parts = 6
    for k in range(parts):
        base = k * (blocks * pairs // parts)
        loop(blocks * pairs // parts, lambda i, base=base: attend_back(base + i), unroll=2)
        advance(2)

    for k in range(pairs):
        columns = slice(k * BLOCK, (k + 1) * BLOCK)
        small[0, 0:1, columns] = total(qkv[k].astype(F32))
        small[0, 1:2, columns] = total(qkv[2 * pairs + k].astype(F32))
    for m in range(n_mp):
        for n in range(tiles):
            small[0, 8 + m : 9 + m, n * TILE : (n + 1) * TILE] = small_up[m * tiles + n]
    links.start(("small", 0), small.at[0], small_in.at[0], core)

    def token_back(kind):
        whole = jnp.concatenate([qkv[kind * pairs + k] for k in range(pairs)], axis=1)

        def one(n):
            columns = at(n * TILE, TILE, TILE)
            grad_tok[:, columns] = grad_tok[:, columns] + dot(
                whole, w[kind * d : (kind + 1) * d, columns]
            )

        loop(tiles, one)

        def weight(n):
            here = rows_of(kind * d + n * TILE, TILE)
            w[here, :] = dot(grad_qkv_t[here, :], tok[...]).astype(LOW)

        loop(tiles, weight)

    for kind in range(3):
        token_back(kind)
        advance(1)
    for s in order:
        halve(0, s)
    queue.extend(functools.partial(quarter, 0, s) for s in order)
    advance(len(queue))

    for k, (before, device) in enumerate(((core, x_side), (x_side, y_side), (y_side, None))):
        links.wait(("small", k), small_in.at[k], before)
        if device is None:
            small_plane[me] = small[k] + small_in[k]
        else:
            small[k + 1] = small[k] + small_in[k]
            links.start(("small", k + 1), small.at[k + 1], small_in.at[k + 1], device)
    for s in range(1, n_mp):
        links.start(("small plane", s), small_plane.at[me], small_plane.at[me], (dp, plane(s)))

    for s in order:
        eighth(1, s)
    for s in order:
        to_plane(1, s)
    for s in order:
        eighth(0, s)
    finish(2)
    outs[2].two()
    for s in order:
        to_plane(0, s)
    finish(1)
    outs[1].two()
    outs[2].three()
    finish(0)
    outs[0].two()
    outs[1].three()
    outs[0].three()

    for s in range(1, n_mp):
        m = plane(n_mp - s)
        links.wait(("small plane", s), small_plane.at[m], (dp, m))
    value = small_plane[0]
    for m in range(1, n_mp):
        value = value + small_plane[m]
    grad_small[...] = value
    ups = value[8:16, :]
    own = total(jnp.where(lax.broadcasted_iota(jnp.int32, ups.shape, 0) == me, ups, 0.0))
    grad_small[8:9, :] = own
    turned = pltpu.roll(value[0:8, :], (n_mp - me) % n_mp * shard, 1)
    grad_small[0:2, :] = turned[0:2, :]

    for gather in outs:
        gather.done()
    links.drain()


def run_kernel(n_mp, tokens, cotangent, segments, weights, vectors, big):
    rows, d = tokens.shape
    vmem = pl.BlockSpec(memory_space=pltpu.VMEM)
    blocks = rows // BLOCK
    pairs = d // BLOCK
    tiles = d // TILE
    ff_tiles = n_mp * tiles
    piece = d // 16
    low = lambda *shape: pltpu.VMEM(shape, LOW)
    full = lambda *shape: pltpu.VMEM(shape, F32)
    block_count = 3 * n_mp
    names = 512
    flops = 2 * rows * d * d * 12 * 3
    return pl.pallas_call(
        functools.partial(layer_kernel, n_mp),
        out_shape=(
            jax.ShapeDtypeStruct((rows, d), LOW),
            jax.ShapeDtypeStruct((rows, d), F32),
            jax.ShapeDtypeStruct((3, d, d), LOW),
            jax.ShapeDtypeStruct((16, d), F32),
        ),
        in_specs=[vmem] * (3 + len(weights) + len(vectors))
        + [pl.BlockSpec(memory_space=pl.ANY)] * len(big),
        out_specs=(vmem,) * 4,
        scratch_shapes=[
            low(3 * n_mp * d, d),
            low(block_count, 2, 4 * piece, d),
            low(block_count, 2, 2 * piece, d),
            low(block_count, 2, piece, d),
            low(3, n_mp - 1, 2, piece, d),
            low(3 * pairs, rows, BLOCK),
            low(3 * d, rows),
            low(blocks * pairs, BLOCK, 2 * BLOCK),
            low(rows, d),
            low(d, rows),
            full(rows, d),
            full(rows, BLOCK),
            low(rows, d),
            low(d, rows),
            full(rows, d),
            low(rows, d),
            low(ff_tiles, rows, TILE),
            low(ff_tiles, TILE, rows),
            low(ff_tiles, rows, TILE),
            full(rows, TILE),
            full(blocks, BLOCK, BLOCK),
            full(n_mp, 8, d),
            full(3 * tiles, 1, TILE),
            full(ff_tiles, 1, TILE),
            full(3, 16, d),
            full(3, 16, d),
            full(ff_tiles, 1, TILE),
            full(n_mp, 16, d),
            pltpu.SemaphoreType.DMA((3,)),
            pltpu.SemaphoreType.DMA((names,)),
            pltpu.SemaphoreType.DMA((names,)),
        ],
        compiler_params=pltpu.CompilerParams(
            collective_id=0, has_side_effects=True, vmem_limit_bytes=63 << 20
        ),
        cost_estimate=pl.CostEstimate(flops=flops, bytes_accessed=1 << 24, transcendentals=1 << 21),
    )(tokens, cotangent, segments, *weights, *vectors, *big)


def per_device(
    n_dp,
    n_mp,
    tokens,
    segment_ids,
    w_query,
    b_query,
    w_key,
    w_value,
    b_value,
    w_out,
    b_out,
    gain_one,
    shift_one,
    w_up,
    b_up,
    w_down,
    b_down,
    gain_two,
    shift_two,
    cotangent,
):
    d = tokens.shape[1]
    shard = d // n_mp
    vectors = (b_query, b_value, b_up, b_out, gain_one, shift_one, b_down, gain_two, shift_two)
    out, grad_tokens, grad_w, small = run_kernel(
        n_mp,
        tokens,
        cotangent,
        segment_ids.reshape(-1, BLOCK),
        (w_query, w_key, w_value),
        tuple(v.reshape(1, -1) for v in vectors),
        (w_out, w_up, w_down),
    )
    grad_w = grad_w.astype(F32)
    if n_dp > PLANE:
        groups = [[k + PLANE * h for h in range(n_dp // PLANE)] for k in range(PLANE)]
        grad_w, small = lax.psum((grad_w, small), "dp", axis_index_groups=groups)
    return (
        out,
        grad_tokens,
        grad_w[0, :shard].T,
        small[0, :shard],
        grad_w[0, shard : 2 * shard].T,
        grad_w[0, 2 * shard : 3 * shard].T,
        small[1, :shard],
        grad_w[0, 3 * shard :],
        small[2],
        small[3],
        small[4],
        grad_w[1],
        small[8],
        grad_w[2],
        small[5],
        small[6],
        small[7],
    )


def solution(mesh):
    n_dp, n_mp = mesh.shape["dp"], mesh.shape["mp"]
    return jax.shard_map(
        functools.partial(per_device, n_dp, n_mp),
        mesh=mesh,
        in_specs=(
            P(("dp", "mp"), None),
            P("dp"),
            P(None, "mp"),
            P("mp"),
            P(None, "mp"),
            P(None, "mp"),
            P("mp"),
            P("mp", None),
            P(),
            P(),
            P(),
            P(None, "mp"),
            P("mp"),
            P("mp", None),
            P(),
            P(),
            P(),
            P(("dp", "mp"), None),
        ),
        out_specs=(
            P(("dp", "mp"), None),
            P(("dp", "mp"), None),
            P(None, "mp"),
            P("mp"),
            P(None, "mp"),
            P(None, "mp"),
            P("mp"),
            P("mp", None),
            P(),
            P(),
            P(),
            P(None, "mp"),
            P("mp"),
            P("mp", None),
            P(),
            P(),
            P(),
        ),
        check_vma=False,
    )
```

```python
import functools

import jax
import jax.numpy as jnp
from jax import lax
from jax.experimental import pallas as pl
from jax.experimental.pallas import tpu as pltpu
from jax.sharding import PartitionSpec as P

HD = 64
BLOCK = 128
TILE = 256
ROWS = 64
PLANE = 8
MASKED = -1000000000.0
MESH = pl.DeviceIdType.MESH
F32 = jnp.float32
LOW = jnp.bfloat16


def dot(left, right):
    return jnp.dot(left, right, preferred_element_type=F32)


def dot_nt(left, right):
    return lax.dot_general(left, right, (((1,), (1,)), ((), ())), preferred_element_type=F32)


def mean(value):
    return jnp.mean(value, axis=-1, keepdims=True)


def total(value):
    return jnp.sum(value, axis=0, keepdims=True)


def at(start, size, unit):
    return pl.ds(pl.multiple_of(start, unit), size)


def loop(count, body, unroll=1):
    def step(index, carry):
        body(index)
        return carry

    lax.fori_loop(0, count, step, 0, unroll=unroll)


class Links:
    def __init__(self, send, recv):
        self.send, self.recv = send, recv
        self.names = {}
        self.open = []

    def index(self, name):
        return self.names.setdefault(name, len(self.names))

    def copy(self, name, src, dst, device):
        k = self.index(name)
        return pltpu.make_async_remote_copy(
            src_ref=src,
            dst_ref=dst,
            send_sem=self.send.at[k],
            recv_sem=self.recv.at[k],
            device_id=device,
            device_id_type=MESH,
        )

    def start(self, name, src, dst, device):
        copy = self.copy(name, src, dst, device)
        copy.start()
        self.open.append(copy)

    def wait(self, name, dst, device):
        self.copy(name, dst, dst, device).wait_recv()

    def drain(self):
        for copy in self.open:
            copy.wait_send()
        self.open = []


def layer_kernel(
    n_mp,
    tok_in,
    cot_in,
    seg_in,
    w_query,
    w_key,
    w_value,
    w_out,
    w_up,
    w_down,
    b_query_in,
    b_value_in,
    *refs,
):
    vectors_in, refs = refs[:7], refs[7:]
    (
        out_to,
        grad_tok_to,
        grad_w_to,
        grad_small_to,
        tok,
        cot,
        seg,
        b_query,
        b_value,
        vectors,
        lines,
        out,
        grad_tok,
        grad_w,
        grad_small,
        w,
        half_in,
        quarter_in,
        eighth_in,
        plane_in,
        qkv,
        grad_qkv_t,
        prob,
        ctx,
        ctx_t,
        unit_one,
        inv_one,
        normed,
        normed_t,
        acc,
        grad_low,
        act,
        act_t,
        slope,
        up_tmp,
        mask,
        bias_in,
        qkv_bias,
        up_bias,
        small,
        small_in,
        small_up,
        small_plane,
        local_sem,
        send_sem,
        recv_sem,
    ) = refs
    b_up, b_out, gain_one, shift_one, b_down, gain_two, shift_two = [lines.at[k] for k in range(7)]
    rows, d = tok.shape
    group = n_mp * d
    shard = d // n_mp
    piece = d // 16
    tiles = d // TILE
    pairs = d // BLOCK
    blocks = rows // BLOCK

    dp, me = lax.axis_index("dp"), lax.axis_index("mp")
    c, x, y = dp % 2, dp // 2 % 2, dp // 4 % 2
    core = (dp + 1 - 2 * c, me)
    x_side = (dp + 2 - 4 * x, me)
    y_side = (dp + 4 - 8 * y, me)

    def plane(step):
        return (me + step) % n_mp

    def rows_of(start, size):
        return at(start, size, 16)

    count = 0

    def fetch(src, dst):
        nonlocal count
        copy = pltpu.make_async_copy(src, dst, local_sem.at[count])
        count += 1
        copy.start()
        return copy

    own_w = [
        fetch(ref, w.at[rows_of(kind * d + me * shard, shard)])
        for kind, ref in enumerate((w_query, w_key, w_value, w_out))
    ]
    own_b = [fetch(b_query_in, b_query), fetch(b_value_in, b_value)]
    own_b += [fetch(ref, vectors.at[k]) for k, ref in enumerate(vectors_in)]
    own_w.append(fetch(w_up, w.at[rows_of(group + me * d, d)]))
    own_w.append(fetch(w_down, w.at[rows_of(2 * group + me * d, d)]))
    own_rows = [fetch(seg_in, seg), fetch(tok_in, tok), fetch(cot_in, cot)]

    barrier = pltpu.get_barrier_semaphore()
    partners = [core, x_side, y_side] + [(dp, plane(s)) for s in range(1, n_mp)]
    for partner in partners:
        pl.semaphore_signal(barrier, inc=1, device_id=partner, device_id_type=MESH)

    for copy in own_b:
        copy.wait()
    for k in range(len(vectors_in)):
        parts = [vectors[k, j : j + 1, :] for j in range(d // BLOCK)]
        lines[k] = jnp.concatenate(parts, axis=1)
    pad = jnp.zeros((1, d - shard), F32)
    for k, ref in enumerate((b_query, b_value)):
        placed = jnp.broadcast_to(jnp.concatenate([ref[...], pad], axis=1), (8, d))
        bias_in[me, k : k + 1, :] = pltpu.roll(placed, me * shard, 1)[0:1, :]
    bias_in[me, 2:3, :] = b_up[...]

    for copy in own_w:
        copy.wait()
    pl.semaphore_wait(barrier, len(partners))

    links = Links(send_sem, recv_sem)

    def region(g, m, core_of, side):
        if g == 0:
            return (2 * core_of + side) * d + m * shard
        return g * group + m * d + core_of * (d // 2) + side * (d // 4)

    class Gather:
        def __init__(self, name, ref, mine, theirs):
            self.name, self.ref = name, ref
            self.mine, self.theirs = mine, theirs

        def at(self, start, size):
            return self.ref.at[rows_of(start, size)]

        def one(self):
            a = self.at(self.mine[0] + (2 * x + y) * piece, piece)
            b = self.at(self.mine[1] + (2 * y + x) * piece, piece)
            links.start((self.name, 1, 0), a, a, y_side)
            links.start((self.name, 1, 1), b, b, x_side)

        def two(self):
            links.wait(
                (self.name, 1, 0), self.at(self.mine[0] + (2 * x + 1 - y) * piece, piece), y_side
            )
            a = self.at(self.mine[0] + 2 * x * piece, 2 * piece)
            links.start((self.name, 2, 0), a, a, x_side)
            links.wait(
                (self.name, 1, 1), self.at(self.mine[1] + (2 * y + 1 - x) * piece, piece), x_side
            )
            b = self.at(self.mine[1] + 2 * y * piece, 2 * piece)
            links.start((self.name, 2, 1), b, b, y_side)

        def three(self):
            links.wait(
                (self.name, 2, 0), self.at(self.mine[0] + 2 * (1 - x) * piece, 2 * piece), x_side
            )
            a = self.at(self.mine[0], 4 * piece)
            links.start((self.name, 3, 0), a, a, core)
            links.wait(
                (self.name, 2, 1), self.at(self.mine[1] + 2 * (1 - y) * piece, 2 * piece), y_side
            )
            b = self.at(self.mine[1], 4 * piece)
            links.start((self.name, 3, 1), b, b, core)

        def done(self):
            for side in range(2):
                links.wait((self.name, 3, side), self.at(self.theirs[side], 4 * piece), core)

    for s in range(1, n_mp):
        links.start(("bias", s), bias_in.at[me], bias_in.at[me], (dp, plane(s)))
    for g in range(3):
        for s in range(1, n_mp):
            a = w.at[rows_of(region(g, me, c, 0) + (2 * x + y) * piece, piece)]
            b = w.at[rows_of(region(g, me, c, 1) + (2 * y + x) * piece, piece)]
            links.start(("w", g, s, 0), a, a, (dp, plane(s)))
            links.start(("w", g, s, 1), b, b, (dp, plane(s)))

    gathers = {}
    for g in range(3):
        for s in range(1, n_mp):
            m = plane(n_mp - s)
            gathers[g, s] = Gather(
                ("in", g, s),
                w,
                [region(g, m, c, side) for side in range(2)],
                [region(g, m, 1 - c, side) for side in range(2)],
            )

    def arrive(g, s):
        m = plane(n_mp - s)
        from_plane = (dp, m)
        a = w.at[rows_of(region(g, m, c, 0) + (2 * x + y) * piece, piece)]
        b = w.at[rows_of(region(g, m, c, 1) + (2 * y + x) * piece, piece)]
        links.wait(("w", g, s, 0), a, from_plane)
        links.wait(("w", g, s, 1), b, from_plane)
        gathers[g, s].one()

    keys = list(gathers)
    ticks = []
    for t in range(len(keys) + 3):
        step = []
        if t < len(keys):
            step.append(functools.partial(arrive, *keys[t]))
        if 0 <= t - 1 < len(keys):
            step.append(gathers[keys[t - 1]].two)
        if 0 <= t - 2 < len(keys):
            step.append(gathers[keys[t - 2]].three)
        if 0 <= t - 3 < len(keys):
            step.append(gathers[keys[t - 3]].done)
        ticks.append(step)

    def tick(count):
        for _ in range(count):
            for action in ticks.pop(0):
                action()

    for copy in own_rows:
        copy.wait()

    for b in range(blocks):
        line = seg[pl.ds(me * blocks + b, 1), :]
        across = jnp.broadcast_to(line, (BLOCK, BLOCK))
        mask[b] = jnp.where(across == across.T, 0.0, MASKED)

    tick(3)
    bias_all = jnp.zeros((8, d), F32)
    for s in range(1, n_mp):
        m = plane(n_mp - s)
        links.wait(("bias", s), bias_in.at[m], (dp, m))
    row_b = jnp.zeros((2, d), F32)
    for m in range(n_mp):
        row_b = row_b + bias_in[m, 0:2, :]
    for t in range(tiles):
        columns = slice(t * TILE, (t + 1) * TILE)
        qkv_bias[t] = row_b[0:1, columns]
        qkv_bias[tiles + t] = jnp.zeros((1, TILE), F32)
        qkv_bias[2 * tiles + t] = row_b[1:2, columns]
        for m in range(n_mp):
            up_bias[m * tiles + t] = bias_in[m, 2:3, columns]
    tick(3)

    def project(n):
        part = dot_nt(tok[...], w[at(n * TILE, TILE, TILE), :]) + qkv_bias[n]
        qkv[2 * n] = part[:, :BLOCK].astype(LOW)
        qkv[2 * n + 1] = part[:, BLOCK:].astype(LOW)

    loop(3 * tiles, project)

    lane = lax.broadcasted_iota(jnp.int32, (1, BLOCK), 1)
    first = jnp.where(lane < HD, 1.0, 0.0).astype(LOW)
    second = jnp.where(lane < HD, 0.0, 1.0).astype(LOW)

    def two_heads(value):
        return jnp.concatenate([value * first, value * second], axis=0)

    def softmax(score):
        expo = jnp.exp(score - jnp.max(score, axis=-1, keepdims=True))
        return expo / jnp.sum(expo, axis=-1, keepdims=True)

    def attend(index):
        b, p = index // pairs, index % pairs
        here = at(b * BLOCK, BLOCK, BLOCK)
        query = qkv[p, here, :]
        key = qkv[pairs + p, here, :]
        value = qkv[2 * pairs + p, here, :]
        score = dot_nt(query, two_heads(key)) * HD**-0.5
        hidden = mask[b]
        both = jnp.concatenate(
            [softmax(score[:, :BLOCK] + hidden), softmax(score[:, BLOCK:] + hidden)], axis=1
        ).astype(LOW)
        prob[index] = both
        context = dot(both, two_heads(value)).astype(LOW)
        ctx[here, at(p * BLOCK, BLOCK, BLOCK)] = context
        ctx_t[at(p * BLOCK, BLOCK, BLOCK), here] = context.T

    for _ in range(3):
        base = _ * (blocks * pairs // 3)
        loop(blocks * pairs // 3, lambda i, base=base: attend(base + i), unroll=2)
        tick(1)

    def attn_out(n):
        columns = at(n * TILE, TILE, TILE)
        acc[:, columns] = dot(ctx[...], w[3 * d : 4 * d, columns])

    loop(tiles, attn_out)

    def norm_one(r):
        here = at(r * ROWS, ROWS, ROWS)
        value = tok[here, :].astype(F32) + acc[here, :] + b_out[...]
        center = value - mean(value)
        inverse = lax.rsqrt(mean(center * center) + 1e-05)
        unit = center * inverse
        unit_one[here, :] = unit
        inv_one[here, :] = jnp.broadcast_to(inverse, (ROWS, BLOCK))
        normed[here, :] = (unit * gain_one[...] + shift_one[...]).astype(LOW)

    loop(rows // ROWS, norm_one)

    def turn(r):
        here = at(r * BLOCK, BLOCK, BLOCK)
        normed_t[:, here] = normed[here, :].T

    loop(blocks, turn)

    def feed_up(m):
        def one(n):
            t = m * tiles + n
            weight = w[rows_of(group + m * d, d), at(n * TILE, TILE, TILE)]
            up_tmp[...] = dot(normed[...], weight) + up_bias[t]

            def gelu(r):
                here = at(r * ROWS, ROWS, ROWS)
                u = up_tmp[here, :]
                square = u * u
                inner = jnp.tanh(0.7978845608028654 * (u + 0.044715 * (square * u)))
                cdf = 0.5 + 0.5 * inner
                act[t, here, :] = (u * cdf).astype(LOW)
                slope_in = 0.7978845608028654 + (3 * 0.044715 * 0.7978845608028654) * square
                slope[t, here, :] = (cdf + 0.5 * u * (1.0 - inner * inner) * slope_in).astype(LOW)

            loop(rows // ROWS, gelu)
            for k in range(TILE // BLOCK):
                act_t[t, k * BLOCK : (k + 1) * BLOCK, :] = act[
                    t, :, k * BLOCK : (k + 1) * BLOCK
                ].T

        loop(tiles, one)

    def columns_of(m):
        return jnp.concatenate([act[m * tiles + t] for t in range(tiles)], axis=1)

    def feed_down(m, opening):
        whole = columns_of(m)

        def one(n):
            columns = at(n * TILE, TILE, TILE)
            part = dot(whole, w[rows_of(2 * group + m * d, d), columns])
            acc[:, columns] = part if opening else acc[:, columns] + part

        loop(tiles, one)

    feed_up(me)
    for s in range(1, n_mp):
        if len(ticks) > 3:
            tick(1)
        feed_up(plane(n_mp - s))
    feed_down(me, True)
    for s in range(1, n_mp):
        while len(ticks) > n_mp - 1 - s:
            tick(1)
        feed_down(plane(n_mp - s), False)
    links.drain()

    small[...] = jnp.zeros(small.shape, F32)

    def add_small(row, value):
        small[0, row : row + 1, :] = small[0, row : row + 1, :] + value

    def norm_two(r):
        here = at(r * ROWS, ROWS, ROWS)
        unit = unit_one[here, :]
        value = unit * gain_one[...] + shift_one[...] + acc[here, :] + b_down[...]
        center = value - mean(value)
        inverse = lax.rsqrt(mean(center * center) + 1e-05)
        unit = center * inverse
        out[here, :] = (unit * gain_two[...] + shift_two[...]).astype(LOW)
        grad = cot[here, :].astype(F32)
        scaled = grad * gain_two[...]
        grad_resid = inverse * (scaled - mean(scaled) - unit * mean(scaled * unit))
        acc[here, :] = grad_resid
        grad_low[here, :] = grad_resid.astype(LOW)
        add_small(5, total(grad_resid))
        add_small(6, total(grad * unit))
        add_small(7, total(grad))

    loop(rows // ROWS, norm_two)
    leaving = [fetch(out, out_to)]

    def block_of(g, s):
        return g * n_mp + s

    def add_rows(start, source, offset, size):
        def one(k):
            here = rows_of(start + k * 16, 16)
            there = rows_of(offset + k * 16, 16)
            w[here, :] = (w[here, :].astype(F32) + source[there, :].astype(F32)).astype(LOW)

        loop(size // 16, one)

    def halve(g, s):
        m, k = plane(s), block_of(g, s)
        for side in range(2):
            links.start(
                ("half", k, side),
                w.at[rows_of(region(g, m, 1 - c, side), 4 * piece)],
                half_in.at[k, side],
                core,
            )

    def quarter(g, s):
        m, k = plane(s), block_of(g, s)
        for side, (bit, device) in enumerate(((x, x_side), (y, y_side))):
            start = region(g, m, c, side)
            links.wait(("half", k, side), half_in.at[k, side], core)
            other = 2 * (1 - bit) * piece
            add_rows(start + other, half_in.at[k, side], other, 2 * piece)
            links.start(
                ("quarter", k, side),
                w.at[rows_of(start + other, 2 * piece)],
                quarter_in.at[k, side],
                device,
            )
        for side, bit in enumerate((x, y)):
            start = region(g, m, c, side)
            own = 2 * bit * piece
            add_rows(start + own, half_in.at[k, side], own, 2 * piece)

    def eighth(g, s):
        m, k = plane(s), block_of(g, s)
        sides = ((x, y, x_side, y_side), (y, x, y_side, x_side))
        for side, (high, bit, before, device) in enumerate(sides):
            start = region(g, m, c, side) + 2 * high * piece
            links.wait(("quarter", k, side), quarter_in.at[k, side], before)
            other = (1 - bit) * piece
            add_rows(start + other, quarter_in.at[k, side], other, piece)
            links.start(
                ("eighth", k, side),
                w.at[rows_of(start + other, piece)],
                eighth_in.at[k, side],
                device,
            )
        for side, (high, bit, before, device) in enumerate(sides):
            start = region(g, m, c, side) + 2 * high * piece
            own = bit * piece
            add_rows(start + own, quarter_in.at[k, side], own, piece)

    def to_plane(g, s):
        m, k = plane(s), block_of(g, s)
        for side, (first_bit, bit, device) in enumerate(((x, y, y_side), (y, x, x_side))):
            start = region(g, m, c, side) + (2 * first_bit + bit) * piece
            links.wait(("eighth", k, side), eighth_in.at[k, side], device)
            add_rows(start, eighth_in.at[k, side], 0, piece)
            if s:
                links.start(
                    ("plane", g, s, side),
                    w.at[rows_of(start, piece)],
                    plane_in.at[g, s - 1, side],
                    (dp, m),
                )

    outs = [
        Gather(
            ("out", g),
            grad_w.at[g],
            [c * (d // 2) + side * (d // 4) for side in range(2)],
            [(1 - c) * (d // 2) + side * (d // 4) for side in range(2)],
        )
        for g in range(3)
    ]

    def finish(g):
        for side, (first_bit, bit) in enumerate(((x, y), (y, x))):
            start = region(g, me, c, side) + (2 * first_bit + bit) * piece
            goal = c * (d // 2) + side * (d // 4) + (2 * first_bit + bit) * piece
            for s in range(1, n_mp):
                links.wait(
                    ("plane", g, s, side), plane_in.at[g, s - 1, side], (dp, plane(n_mp - s))
                )

            def one(k):
                value = w[rows_of(start + k * 16, 16), :].astype(F32)
                for s in range(1, n_mp):
                    value = value + plane_in[g, s - 1, side, rows_of(k * 16, 16), :].astype(F32)
                grad_w[g, rows_of(goal + k * 16, 16), :] = value.astype(LOW)

            loop(piece // 16, one)
        outs[g].one()

    order = [s for s in range(1, n_mp)] + [0]
    queue = []

    def advance(count):
        for _ in range(min(count, len(queue))):
            queue.pop(0)()

    def down_back(m):
        def one(n):
            t = m * tiles + n
            here = rows_of(2 * group + t * TILE, TILE)
            grad = grad_low[...]
            grad_up = (dot_nt(grad, w[here, :]) * slope[t].astype(F32)).astype(LOW)
            act[t] = grad_up
            small_up[t] = total(grad_up.astype(F32))
            w[here, :] = dot(act_t[t], grad).astype(LOW)

        loop(tiles, one)

    def up_back(m):
        whole = columns_of(m)

        def one(n):
            here = rows_of(group + m * d + n * TILE, TILE)
            columns = at(n * TILE, TILE, TILE)
            acc[:, columns] = acc[:, columns] + dot_nt(whole, w[here, :])
            w[here, :] = dot(normed_t[columns, :], whole).astype(LOW)

        loop(tiles, one)

    for s in order:
        down_back(plane(s))
        halve(2, s)
        advance(1)
        queue.append(functools.partial(quarter, 2, s))
    for k, s in enumerate(order):
        up_back(plane(s))
        halve(1, s)
        advance(1)
        queue.append(functools.partial(quarter, 1, s))
    queue.extend(functools.partial(eighth, 2, s) for s in order)
    queue.extend(functools.partial(to_plane, 2, s) for s in order)

    def norm_one_back(r):
        here = at(r * ROWS, ROWS, ROWS)
        grad = acc[here, :]
        unit = unit_one[here, :]
        scaled = grad * gain_one[...]
        inverse = inv_one[here, 0:1]
        grad_resid = inverse * (scaled - mean(scaled) - unit * mean(scaled * unit))
        grad_tok[here, :] = grad_resid
        grad_low[here, :] = grad_resid.astype(LOW)
        add_small(2, total(grad_resid))
        add_small(3, total(grad * unit))
        add_small(4, total(grad))

    loop(rows // ROWS, norm_one_back)
    advance(1)

    def out_back(n):
        here = rows_of(3 * d + n * TILE, TILE)
        columns = at(n * TILE, TILE, TILE)
        grad = grad_low[...]
        ctx[:, columns] = dot_nt(grad, w[here, :]).astype(LOW)
        w[here, :] = dot(ctx_t[columns, :], grad).astype(LOW)

    loop(tiles, out_back)
    advance(1)

    def attend_back(index):
        b, p = index // pairs, index % pairs
        here = at(b * BLOCK, BLOCK, BLOCK)
        query = qkv[p, here, :]
        key = qkv[pairs + p, here, :]
        value = qkv[2 * pairs + p, here, :]
        grad = ctx[here, at(p * BLOCK, BLOCK, BLOCK)]
        both = prob[index]
        grad_prob = dot_nt(grad, two_heads(value))
        wide = both.astype(F32)

        def score_back(columns):
            part, grad_part = wide[:, columns], grad_prob[:, columns]
            return part * (grad_part - jnp.sum(part * grad_part, axis=-1, keepdims=True))

        low_score = jnp.concatenate(
            [score_back(slice(0, BLOCK)), score_back(slice(BLOCK, 2 * BLOCK))], axis=1
        ).astype(LOW)

        def turned(pair):
            return jnp.concatenate([pair[:, :BLOCK].T, pair[:, BLOCK:].T], axis=1)

        grads = (
            (dot(low_score, two_heads(key)) * HD**-0.5).astype(LOW),
            (dot(turned(low_score), two_heads(query)) * HD**-0.5).astype(LOW),
            dot(turned(both), two_heads(grad)).astype(LOW),
        )
        for kind, value in enumerate(grads):
            qkv[kind * pairs + p, here, :] = value
            grad_qkv_t[at((kind * pairs + p) * BLOCK, BLOCK, BLOCK), here] = value.T

    parts = 6
    for k in range(parts):
        base = k * (blocks * pairs // parts)
        loop(blocks * pairs // parts, lambda i, base=base: attend_back(base + i), unroll=2)
        advance(2)

    for k in range(pairs):
        columns = slice(k * BLOCK, (k + 1) * BLOCK)
        small[0, 0:1, columns] = total(qkv[k].astype(F32))
        small[0, 1:2, columns] = total(qkv[2 * pairs + k].astype(F32))
    for m in range(n_mp):
        for n in range(tiles):
            small[0, 8 + m : 9 + m, n * TILE : (n + 1) * TILE] = small_up[m * tiles + n]
    links.start(("small", 0), small.at[0], small_in.at[0], core)

    def token_back(kind):
        whole = jnp.concatenate([qkv[kind * pairs + k] for k in range(pairs)], axis=1)

        def one(n):
            columns = at(n * TILE, TILE, TILE)
            grad_tok[:, columns] = grad_tok[:, columns] + dot(
                whole, w[kind * d : (kind + 1) * d, columns]
            )

        loop(tiles, one)

        def weight(n):
            here = rows_of(kind * d + n * TILE, TILE)
            w[here, :] = dot(grad_qkv_t[here, :], tok[...]).astype(LOW)

        loop(tiles, weight)

    for kind in range(3):
        token_back(kind)
        advance(1)
    leaving.append(fetch(grad_tok, grad_tok_to))
    for s in order:
        halve(0, s)
    queue.extend(functools.partial(quarter, 0, s) for s in order)
    advance(len(queue))

    for k, (before, device) in enumerate(((core, x_side), (x_side, y_side), (y_side, None))):
        links.wait(("small", k), small_in.at[k], before)
        if device is None:
            small_plane[me] = small[k] + small_in[k]
        else:
            small[k + 1] = small[k] + small_in[k]
            links.start(("small", k + 1), small.at[k + 1], small_in.at[k + 1], device)
    for s in range(1, n_mp):
        links.start(("small plane", s), small_plane.at[me], small_plane.at[me], (dp, plane(s)))

    for s in order:
        eighth(1, s)
    for s in order:
        to_plane(1, s)
    for s in order:
        eighth(0, s)
    finish(2)
    outs[2].two()
    for s in order:
        to_plane(0, s)
    finish(1)
    outs[1].two()
    outs[2].three()
    finish(0)
    outs[0].two()
    outs[1].three()
    outs[0].three()

    for s in range(1, n_mp):
        m = plane(n_mp - s)
        links.wait(("small plane", s), small_plane.at[m], (dp, m))
    value = small_plane[0]
    for m in range(1, n_mp):
        value = value + small_plane[m]
    grad_small[...] = value
    ups = value[8:16, :]
    own = total(jnp.where(lax.broadcasted_iota(jnp.int32, ups.shape, 0) == me, ups, 0.0))
    grad_small[8:9, :] = own
    turned = pltpu.roll(value[0:8, :], (n_mp - me) % n_mp * shard, 1)
    grad_small[0:2, :] = turned[0:2, :]

    leaving.append(fetch(grad_small, grad_small_to))
    for g in (2, 1, 0):
        outs[g].done()
        leaving.append(fetch(grad_w.at[g], grad_w_to.at[g]))
    links.drain()
    for copy in leaving:
        copy.wait()


def run_kernel(n_mp, tokens, cotangent, segments, weights, shards, vectors):
    rows, d = tokens.shape
    anywhere = pl.BlockSpec(memory_space=pl.ANY)
    blocks = rows // BLOCK
    pairs = d // BLOCK
    tiles = d // TILE
    ff_tiles = n_mp * tiles
    piece = d // 16
    low = lambda *shape: pltpu.VMEM(shape, LOW)
    full = lambda *shape: pltpu.VMEM(shape, F32)
    block_count = 3 * n_mp
    names = 256
    flops = 2 * rows * d * d * 12 * 3
    operands = (tokens, cotangent, segments, *weights, *shards, *vectors)
    return pl.pallas_call(
        functools.partial(layer_kernel, n_mp),
        out_shape=(
            jax.ShapeDtypeStruct((rows, d), LOW),
            jax.ShapeDtypeStruct((rows, d), F32),
            jax.ShapeDtypeStruct((3, d, d), LOW),
            jax.ShapeDtypeStruct((16, d), F32),
        ),
        in_specs=[anywhere] * len(operands),
        out_specs=(anywhere,) * 4,
        scratch_shapes=[
            low(rows, d),
            low(rows, d),
            pltpu.VMEM(segments.shape, jnp.int32),
            full(*shards[0].shape),
            full(*shards[1].shape),
            full(len(vectors), *vectors[0].shape),
            full(len(vectors), 1, d),
            low(rows, d),
            full(rows, d),
            low(3, d, d),
            full(16, d),
            low(3 * n_mp * d, d),
            low(block_count, 2, 4 * piece, d),
            low(block_count, 2, 2 * piece, d),
            low(block_count, 2, piece, d),
            low(3, n_mp - 1, 2, piece, d),
            low(3 * pairs, rows, BLOCK),
            low(3 * d, rows),
            low(blocks * pairs, BLOCK, 2 * BLOCK),
            low(rows, d),
            low(d, rows),
            full(rows, d),
            full(rows, BLOCK),
            low(rows, d),
            low(d, rows),
            full(rows, d),
            low(rows, d),
            low(ff_tiles, rows, TILE),
            low(ff_tiles, TILE, rows),
            low(ff_tiles, rows, TILE),
            full(rows, TILE),
            full(blocks, BLOCK, BLOCK),
            full(n_mp, 8, d),
            full(3 * tiles, 1, TILE),
            full(ff_tiles, 1, TILE),
            full(3, 16, d),
            full(3, 16, d),
            full(ff_tiles, 1, TILE),
            full(n_mp, 16, d),
            pltpu.SemaphoreType.DMA((32,)),
            pltpu.SemaphoreType.DMA((names,)),
            pltpu.SemaphoreType.DMA((names,)),
        ],
        compiler_params=pltpu.CompilerParams(
            collective_id=0, has_side_effects=True, vmem_limit_bytes=63 << 20
        ),
        cost_estimate=pl.CostEstimate(flops=flops, bytes_accessed=1 << 24, transcendentals=1 << 21),
    )(*operands)


def finish_kernel(
    out,
    grad_tok,
    grad_w,
    small,
    out_to,
    grad_tok_to,
    query_to,
    key_to,
    value_to,
    attn_to,
    up_to,
    down_to,
    b_query_to,
    b_value_to,
    *refs,

):
    vectors_to, refs = refs[:7], refs[7:]
    held, wide, lines, parts, vectors, low_rows, full_rows, sems = refs
    d = held.shape[-1]
    shard = query_to.shape[0]
    pieces = d // shard
    count = 0

    def fetch(src, dst):
        nonlocal count
        copy = pltpu.make_async_copy(src, dst, sems.at[count])
        count += 1
        copy.start()
        return copy

    first = fetch(small, lines)
    loads = {}
    for g in range(3):
        for k in range(pieces):
            here = pl.ds(k * shard, shard)
            loads[g, k] = fetch(grad_w.at[g, here], held.at[g, here])
    passing = [fetch(out, low_rows), fetch(grad_tok, full_rows)]
    first.wait()
    for k in range(2):
        parts[k] = lines[k : k + 1, :shard]
    for k in range(vectors.shape[0]):
        for j in range(d // BLOCK):
            vectors[k, j : j + 1, :] = lines[2 + k : 3 + k, j * BLOCK : (j + 1) * BLOCK]
    stores = [fetch(parts.at[0], b_query_to), fetch(parts.at[1], b_value_to)]
    stores += [fetch(vectors.at[k], ref) for k, ref in enumerate(vectors_to)]
    for g in range(3):
        for k in range(pieces):
            loads[g, k].wait()

            def widen(r, g=g, k=k):
                here = at(k * shard + r * 16, 16, 16)
                wide[g, here, :] = held[g, here, :].astype(F32)

            loop(shard // 16, widen, unroll=2)
            here = pl.ds(k * shard, shard)
            if g == 0:
                stores.append(fetch(wide.at[0, here], (query_to, key_to, value_to, attn_to)[k]))
            else:
                stores.append(fetch(wide.at[g, here], (up_to, down_to)[g - 1].at[here]))
        if g == 0:
            for copy in passing:
                copy.wait()
            stores += [fetch(low_rows, out_to), fetch(full_rows, grad_tok_to)]
    for copy in stores:
        copy.wait()


def run_finish(shard, out, grad_tok, grad_w, small):
    d = out.shape[1]
    anywhere = pl.BlockSpec(memory_space=pl.ANY)
    full = lambda *shape: jax.ShapeDtypeStruct(shape, F32)
    shapes = (
        [jax.ShapeDtypeStruct(out.shape, LOW), full(*grad_tok.shape)]
        + [full(shard, d)] * 4
        + [full(d, d)] * 2
        + [full(1, shard)] * 2
        + [full(d // BLOCK, BLOCK)] * 7
    )
    return pl.pallas_call(
        finish_kernel,
        out_shape=tuple(shapes),
        in_specs=[anywhere] * 4,
        out_specs=(anywhere,) * len(shapes),
        scratch_shapes=[
            pltpu.VMEM(grad_w.shape, grad_w.dtype),
            pltpu.VMEM(grad_w.shape, F32),
            pltpu.VMEM(small.shape, F32),
            pltpu.VMEM((2, 1, shard), F32),
            pltpu.VMEM((7, d // BLOCK, BLOCK), F32),
            pltpu.VMEM(out.shape, LOW),
            pltpu.VMEM(grad_tok.shape, F32),
            pltpu.SemaphoreType.DMA((64,)),
        ],
        compiler_params=pltpu.CompilerParams(vmem_limit_bytes=60 << 20),
        cost_estimate=pl.CostEstimate(flops=0, bytes_accessed=1 << 24, transcendentals=0),
    )(out, grad_tok, grad_w, small)


def per_device(
    n_dp,
    n_mp,
    tokens,
    segment_ids,
    w_query,
    b_query,
    w_key,
    w_value,
    b_value,
    w_out,
    b_out,
    gain_one,
    shift_one,
    w_up,
    b_up,
    w_down,
    b_down,
    gain_two,
    shift_two,
    cotangent,
):
    d = tokens.shape[1]
    shard = d // n_mp
    vectors = (b_up, b_out, gain_one, shift_one, b_down, gain_two, shift_two)
    out, grad_tokens, grad_w, small = run_kernel(
        n_mp,
        tokens,
        cotangent,
        segment_ids.reshape(-1, BLOCK),
        (w_query.T, w_key.T, w_value.T, w_out, w_up, w_down),
        (b_query.reshape(1, -1), b_value.reshape(1, -1)),
        tuple(v.reshape(-1, BLOCK) for v in vectors),
    )
    if n_dp > PLANE:
        groups = [[k + PLANE * h for h in range(n_dp // PLANE)] for k in range(PLANE)]
        grad_w, small = lax.psum(
            (grad_w.astype(F32), small), "dp", axis_index_groups=groups
        )
    (
        out,
        grad_tokens,
        grad_w_query,
        grad_w_key,
        grad_w_value,
        grad_w_out,
        grad_w_up,
        grad_w_down,
        grad_b_query,
        grad_b_value,
        *grad_vectors,
    ) = run_finish(shard, out, grad_tokens, grad_w, small)
    grad_b_out, grad_gain_one, grad_shift_one, grad_b_down, grad_gain_two, grad_shift_two = [
        grad_vectors[k].reshape(-1) for k in range(6)
    ]
    return (
        out,
        grad_tokens,
        grad_w_query.T,
        grad_b_query.reshape(-1),
        grad_w_key.T,
        grad_w_value.T,
        grad_b_value.reshape(-1),
        grad_w_out,
        grad_b_out,
        grad_gain_one,
        grad_shift_one,
        grad_w_up,
        grad_vectors[6].reshape(-1),
        grad_w_down,
        grad_b_down,
        grad_gain_two,
        grad_shift_two,
    )


def solution(mesh):
    n_dp, n_mp = mesh.shape["dp"], mesh.shape["mp"]
    return jax.shard_map(
        functools.partial(per_device, n_dp, n_mp),
        mesh=mesh,
        in_specs=(
            P(("dp", "mp"), None),
            P("dp"),
            P(None, "mp"),
            P("mp"),
            P(None, "mp"),
            P(None, "mp"),
            P("mp"),
            P("mp", None),
            P(),
            P(),
            P(),
            P(None, "mp"),
            P("mp"),
            P("mp", None),
            P(),
            P(),
            P(),
            P(("dp", "mp"), None),
        ),
        out_specs=(
            P(("dp", "mp"), None),
            P(("dp", "mp"), None),
            P(None, "mp"),
            P("mp"),
            P(None, "mp"),
            P(None, "mp"),
            P("mp"),
            P("mp", None),
            P(),
            P(),
            P(),
            P(None, "mp"),
            P("mp"),
            P("mp", None),
            P(),
            P(),
            P(),
        ),
        check_vma=False,
    )
```

```python
import functools

import jax
import jax.numpy as jnp
from jax import lax
from jax.experimental import pallas as pl
from jax.experimental.pallas import tpu as pltpu
from jax.sharding import PartitionSpec as P

HD = 64
BLOCK = 128
TILE = 256
ROWS = 64
PLANE = 8
ATTEND_PARTS = 2
ATTEND_BACK_PARTS = 6
DOUBLED = (1, 2)
GELU = 0.7978845608028654
FORWARD = (
    ("send", 0), ("masks",), ("one", 0, 0), ("send", 1), ("two", 0, 0), ("one", 0, 1),
    ("biases",), ("three", 0, 0), ("two", 0, 1), ("done", 0, 0), ("project", 0), ("one", 0, 2),
    ("attend", 0, 0), ("attend", 0, 1), ("three", 0, 1), ("two", 0, 2), ("done", 0, 1),
    ("two", 1, 0), ("send", 2), ("three", 0, 2), ("one", 1, 1), ("done", 0, 2), ("project", 1),
    ("three", 1, 0), ("one", 1, 2), ("attend", 1, 0), ("two", 1, 1), ("attend", 1, 1),
    ("done", 1, 0), ("two", 1, 2), ("attn_out",), ("norm_one",), ("three", 1, 1), ("two", 2, 0),
    ("up", 3), ("up", 0), ("done", 1, 1), ("three", 1, 2), ("one", 2, 1), ("up", 1),
    ("three", 2, 0), ("one", 2, 2), ("done", 1, 2), ("up", 2), ("two", 2, 1), ("down", 3),
    ("done", 2, 0), ("two", 2, 2), ("down", 0), ("three", 2, 1), ("done", 2, 1), ("down", 1),
    ("three", 2, 2), ("done", 2, 2), ("down", 2),
)
BACKWARD = (
    ("down", 1), ("halve", 2, 1), ("down", 0), ("halve", 2, 0), ("down", 2), ("quarter", 2, 1),
    ("halve", 2, 2), ("down", 3), ("quarter", 2, 0), ("halve", 2, 3), ("up", 1),
    ("eighth", 2, 1), ("halve", 1, 1), ("quarter", 2, 2), ("up", 0), ("halve", 1, 0), ("up", 2),
    ("plane", 2, 1), ("eighth", 2, 0), ("quarter", 1, 1), ("halve", 1, 2), ("up", 3),
    ("halve", 1, 3), ("norm",), ("eighth", 2, 2), ("plane", 2, 0), ("out",), ("quarter", 1, 0),
    ("attend", 0), ("eighth", 1, 1), ("attend", 1), ("plane", 2, 2), ("quarter", 1, 2),
    ("attend", 2), ("attend", 3), ("eighth", 1, 0), ("attend", 4), ("plane", 1, 1),
    ("quarter", 1, 3), ("attend", 5), ("small_send",), ("token",), ("small_next", 0),
    ("plane", 1, 0), ("eighth", 1, 2), ("quarter", 2, 3), ("project",), ("small_next", 1),
    ("plane", 1, 2), ("eighth", 1, 3), ("halve", 0, 1), ("halve", 0, 0), ("halve", 0, 2),
    ("halve", 0, 3), ("quarter", 0, 1), ("small_next", 2), ("eighth", 2, 3), ("quarter", 0, 0),
    ("eighth", 0, 1), ("quarter", 0, 2), ("small_done",), ("eighth", 0, 0), ("plane", 0, 1),
    ("quarter", 0, 3), ("eighth", 0, 2), ("plane", 0, 0), ("finish", 1), ("finish", 2),
    ("eighth", 0, 3), ("plane", 0, 2), ("two", 1), ("two", 2), ("three", 1), ("finish", 0),
    ("done", 1), ("three", 2), ("two", 0), ("done", 2), ("three", 0), ("done", 0),
)
MASKED = -1000000000.0
MESH = pl.DeviceIdType.MESH
F32 = jnp.float32
LOW = jnp.bfloat16


def dot(left, right):
    return jnp.dot(left, right, preferred_element_type=F32)


def dot_nt(left, right):
    return lax.dot_general(left, right, (((1,), (1,)), ((), ())), preferred_element_type=F32)


def mean(value):
    return jnp.mean(value, axis=-1, keepdims=True)


def total(value):
    return jnp.sum(value, axis=0, keepdims=True)


def at(start, size, unit):
    return pl.ds(pl.multiple_of(start, unit), size)


def loop(count, body, unroll=1):
    def step(index, carry):
        body(index)
        return carry

    lax.fori_loop(0, count, step, 0, unroll=unroll)


class Links:
    def __init__(self, send, recv):
        self.send, self.recv = send, recv
        self.names = {}
        self.used = 0
        self.open = []

    def index(self, name, width):
        if name not in self.names:
            self.names[name] = self.used
            self.used += width
        return self.names[name]

    def copy(self, name, src, dst, device, there=None, here=None):
        first = self.index(name, 1 if there is None else 4)
        going, coming = (first, first) if there is None else (first + there, first + here)
        return pltpu.make_async_remote_copy(
            src_ref=src,
            dst_ref=dst,
            send_sem=self.send.at[going],
            recv_sem=self.recv.at[coming],
            device_id=device,
            device_id_type=MESH,
        )

    def start(self, *args):
        copy = self.copy(*args)
        copy.start()
        self.open.append(copy)

    def wait(self, name, dst, device, there=None):
        self.copy(name, dst, dst, device, there, there).wait_recv()

    def drain(self):
        for copy in self.open:
            copy.wait_send()
        self.open = []


def layer_kernel(
    n_mp,
    tok_in,
    cot_in,
    seg_in,
    w_query,
    w_key,
    w_value,
    w_out,
    w_up,
    w_down,
    b_query_in,
    b_value_in,
    *refs,
):
    vectors_in, refs = refs[:7], refs[7:]
    (
        out_to,
        grad_tok_to,
        grad_w_to,
        grad_small_to,
        tok,
        cot,
        seg,
        b_query,
        b_value,
        vectors,
        lines,
        out,
        grad_tok,
        grad_w,
        grad_small,
        w,
        half_in,
        quarter_in,
        eighth_in,
        plane_in,
        qkv,
        grad_qkv_t,
        prob,
        ctx,
        ctx_t,
        unit_one,
        inv_one,
        normed,
        normed_t,
        acc,
        grad_low,
        act,
        act_t,
        slope,
        mask,
        bias_in,
        qkv_bias,
        small,
        small_in,
        small_up,
        small_plane,
        local_sem,
        send_sem,
        recv_sem,
    ) = refs
    b_up, b_out, gain_one, shift_one, b_down, gain_two, shift_two = [lines.at[k] for k in range(7)]
    rows, d = tok.shape
    group = n_mp * d
    shard = d // n_mp
    piece = d // 16
    pairs = d // BLOCK
    blocks = rows // BLOCK

    dp, me = lax.axis_index("dp"), lax.axis_index("mp")
    c, x, y = dp % 2, dp // 2 % 2, dp // 4 % 2
    core = (dp + 1 - 2 * c, me)
    x_side = (dp + 2 - 4 * x, me)
    y_side = (dp + 4 - 8 * y, me)

    ranks = (me + 1 - 2 * (me % 2), 2 - me // 2, 3 - 3 * (me // 2), me)
    others = range(n_mp - 1)

    def rows_of(start, size):
        return at(start, size, 16)

    count = 0

    def fetch(src, dst):
        nonlocal count
        copy = pltpu.make_async_copy(src, dst, local_sem.at[count])
        count += 1
        copy.start()
        return copy

    own_w = [
        fetch(ref, w.at[rows_of(kind * d + me * shard, shard)])
        for kind, ref in enumerate((w_query, w_key, w_value, w_out))
    ]
    own_b = [fetch(b_query_in, b_query), fetch(b_value_in, b_value)]
    own_b += [fetch(ref, vectors.at[k]) for k, ref in enumerate(vectors_in)]
    own_w.append(fetch(w_up, w.at[rows_of(group + me * d, d)]))
    own_w.append(fetch(w_down, w.at[rows_of(2 * group + me * d, d)]))
    own_rows = [fetch(seg_in, seg), fetch(tok_in, tok), fetch(cot_in, cot)]

    barrier = pltpu.get_barrier_semaphore()
    partners = [core, x_side, y_side] + [(dp, ranks[k]) for k in others]
    for partner in partners:
        pl.semaphore_signal(barrier, inc=1, device_id=partner, device_id_type=MESH)

    for copy in own_b:
        copy.wait()
    for k in range(len(vectors_in)):
        parts = [vectors[k, j : j + 1, :] for j in range(d // BLOCK)]
        lines[k] = jnp.concatenate(parts, axis=1)
    pad = jnp.zeros((1, d - shard), F32)
    for k, ref in enumerate((b_query, b_value)):
        placed = jnp.broadcast_to(jnp.concatenate([ref[...], pad], axis=1), (8, d))
        bias_in[me, k : k + 1, :] = pltpu.roll(placed, me * shard, 1)[0:1, :]
    bias_in[me, 2:3, :] = b_up[...]

    for copy in own_w:
        copy.wait()
    pl.semaphore_wait(barrier, len(partners))

    links = Links(send_sem, recv_sem)

    def region(g, m, core_of, side):
        if g == 0:
            return (2 * core_of + side) * d + m * shard
        return g * group + m * d + core_of * (d // 2) + side * (d // 4)

    class Gather:
        def __init__(self, name, ref, mine, theirs):
            self.name, self.ref = name, ref
            self.mine, self.theirs = mine, theirs

        def at(self, start, size):
            return self.ref.at[rows_of(start, size)]

        def one(self):
            a = self.at(self.mine[0] + (2 * x + y) * piece, piece)
            b = self.at(self.mine[1] + (2 * y + x) * piece, piece)
            links.start((self.name, 1, 0), a, a, y_side)
            links.start((self.name, 1, 1), b, b, x_side)

        def joined(self, side):
            if side == 0:
                start, device = self.mine[0] + (2 * x + 1 - y) * piece, y_side
            else:
                start, device = self.mine[1] + (2 * y + 1 - x) * piece, x_side
            links.wait((self.name, 1, side), self.at(start, piece), device)

        def two(self, joined=None):
            (joined or self.joined)(0)
            a = self.at(self.mine[0] + 2 * x * piece, 2 * piece)
            links.start((self.name, 2, 0), a, a, x_side)
            (joined or self.joined)(1)
            b = self.at(self.mine[1] + 2 * y * piece, 2 * piece)
            links.start((self.name, 2, 1), b, b, y_side)

        def three(self):
            links.wait(
                (self.name, 2, 0), self.at(self.mine[0] + 2 * (1 - x) * piece, 2 * piece), x_side
            )
            a = self.at(self.mine[0], 4 * piece)
            links.start((self.name, 3, 0), a, a, core)
            links.wait(
                (self.name, 2, 1), self.at(self.mine[1] + 2 * (1 - y) * piece, 2 * piece), y_side
            )
            b = self.at(self.mine[1], 4 * piece)
            links.start((self.name, 3, 1), b, b, core)

        def done(self):
            for side in range(2):
                links.wait((self.name, 3, side), self.at(self.theirs[side], 4 * piece), core)

    for k in others:
        m = ranks[k]
        links.start("bias", bias_in.at[me], bias_in.at[me], (dp, m), m, me)

    def share(g, k, m, side):
        start = region(g, m, c, side)
        high, bit = (x, y) if side == 0 else (y, x)
        if k == 0 and g in DOUBLED:
            return w.at[rows_of(start + 2 * high * piece, 2 * piece)]
        return w.at[rows_of(start + (2 * high + bit) * piece, piece)]

    def send(g):
        for k in others:
            for side in range(2):
                rows_in = share(g, k, me, side)
                links.start(("w", g, side), rows_in, rows_in, (dp, ranks[k]), ranks[k], me)

    gathers = {}
    for g in range(3):
        for k in others:
            m = ranks[k]
            gathers[g, k] = Gather(
                ("in", g, k),
                w,
                [region(g, m, c, side) for side in range(2)],
                [region(g, m, 1 - c, side) for side in range(2)],
            )

    def landed(g, k, side):
        m = ranks[k]
        links.wait(("w", g, side), share(g, k, m, side), (dp, m), m)

    def one(g, k):
        for side in range(2):
            landed(g, k, side)
        gathers[g, k].one()

    def two(g, k):
        whole = k == 0 and g in DOUBLED
        gathers[g, k].two(functools.partial(landed, g, k) if whole else None)

    def three(g, k):
        gathers[g, k].three()

    def done(g, k):
        gathers[g, k].done()

    def masks():
        for copy in own_rows:
            copy.wait()
        for b in range(blocks):
            line = seg[pl.ds(me * blocks + b, 1), :]
            across = jnp.broadcast_to(line, (BLOCK, BLOCK))
            mask[b] = jnp.where(across == across.T, 0.0, MASKED)

    def biases():
        for k in others:
            m = ranks[k]
            links.wait("bias", bias_in.at[m], (dp, m), m)
        row = jnp.zeros((2, d), F32)
        for m in range(n_mp):
            row = row + bias_in[m, 0:2, :]
        for h in range(2):
            columns = slice(h * (d // 2), (h + 1) * (d // 2))
            qkv_bias[h] = row[0:1, columns]
            qkv_bias[2 + h] = jnp.zeros((1, d // 2), F32)
            qkv_bias[4 + h] = row[1:2, columns]

    half_pairs = pairs // 2

    def half_of(k):
        return me // 2 if k == 0 else 1 - me // 2

    def project(k):
        half = half_of(k)

        def one_kind(kind):
            here = rows_of(kind * d + half * (d // 2), d // 2)
            part = dot_nt(tok[...], w[here, :]) + qkv_bias[2 * kind + half]
            for j in range(half_pairs):
                columns = part[:, j * BLOCK : (j + 1) * BLOCK]
                qkv[kind * pairs + half * half_pairs + j] = columns.astype(LOW)

        loop(3, one_kind)

    lane = lax.broadcasted_iota(jnp.int32, (1, BLOCK), 1)
    first = jnp.where(lane < HD, 1.0, 0.0).astype(LOW)
    second = jnp.where(lane < HD, 0.0, 1.0).astype(LOW)
    none = jnp.zeros((HD, BLOCK), LOW)

    def two_heads(value):
        return jnp.concatenate([value * first, value * second], axis=0)

    def two_heads_t(value):
        turned = value.T
        upper = jnp.concatenate([turned[:HD], none], axis=1)
        lower = jnp.concatenate([none, turned[HD:]], axis=1)
        return jnp.concatenate([upper, lower], axis=0)

    def softmax(score):
        expo = jnp.exp(score - jnp.max(score, axis=0, keepdims=True))
        return expo * (1.0 / jnp.sum(expo, axis=0, keepdims=True))

    def attend(b, p):
        here = at(b * BLOCK, BLOCK, BLOCK)
        columns = at(p * BLOCK, BLOCK, BLOCK)
        query = qkv[p, here, :]
        key = qkv[pairs + p, here, :]
        value = qkv[2 * pairs + p, here, :]
        score = dot_nt(two_heads(key), query) * HD**-0.5
        hidden = mask[b]
        both = jnp.concatenate(
            [softmax(score[:BLOCK] + hidden), softmax(score[BLOCK:] + hidden)], axis=0
        ).astype(LOW)
        prob[b * pairs + p] = both
        context = dot(two_heads_t(value), both).astype(LOW)
        ctx_t[columns, here] = context
        ctx[here, columns] = context.T

    def attend_part(k, part):
        count = blocks * half_pairs // ATTEND_PARTS

        def step(i):
            i = i + part * count
            attend(i % blocks, half_of(k) * half_pairs + i // blocks)

        loop(count, step, unroll=2)

    def attn_out():
        acc[...] = dot(ctx[...], w[3 * d : 4 * d, :])

    def norm_one():
        def step(r):
            here = at(r * ROWS, ROWS, ROWS)
            value = tok[here, :].astype(F32) + acc[here, :] + b_out[...]
            center = value - mean(value)
            inverse = lax.rsqrt(mean(center * center) + 1e-05)
            unit = center * inverse
            unit_one[here, :] = unit
            inv_one[here, :] = jnp.broadcast_to(inverse, (ROWS, BLOCK))
            normed[here, :] = (unit * gain_one[...] + shift_one[...]).astype(LOW)

        loop(rows // ROWS, step)

        def turn(r):
            here = at(r * BLOCK, BLOCK, BLOCK)
            normed_t[:, here] = normed[here, :].T

        loop(blocks, turn)

    def feed_up(k):
        m = ranks[k]
        acc[...] = dot(normed[...], w[rows_of(group + m * d, d), :]) + bias_in[m, 2:3, :]

        def gelu(r):
            here = at(r * 16, 16, 16)
            u = acc[here, :]
            square = u * u
            inner = jnp.tanh(u * (GELU + GELU * 0.044715 * square))
            cdf = 0.5 + 0.5 * inner
            act[m, here, :] = (u * cdf).astype(LOW)
            slope_in = 0.5 * GELU + (1.5 * 0.044715 * GELU) * square
            slope[m, here, :] = (cdf + u * (1.0 - inner * inner) * slope_in).astype(LOW)

        loop(rows // 16, gelu)

        def turn(r):
            here = at(r * BLOCK, BLOCK, BLOCK)
            act_t[m, :, here] = act[m, here, :].T

        loop(blocks, turn)

    def feed_down(k):
        m = ranks[k]
        part = dot(act[m], w[rows_of(2 * group + m * d, d), :])
        acc[...] = part if k == n_mp - 1 else acc[...] + part

    forward = {
        "send": send,
        "one": one,
        "two": two,
        "three": three,
        "done": done,
        "masks": masks,
        "biases": biases,
        "project": project,
        "attend": attend_part,
        "attn_out": attn_out,
        "norm_one": norm_one,
        "up": feed_up,
        "down": feed_down,
    }
    for name, *args in FORWARD:
        forward[name](*args)
    links.drain()

    small[...] = jnp.zeros(small.shape, F32)

    def add_small(row, value):
        small[0, row : row + 1, :] = small[0, row : row + 1, :] + value

    def norm_two(r):
        here = at(r * ROWS, ROWS, ROWS)
        unit = unit_one[here, :]
        value = unit * gain_one[...] + shift_one[...] + acc[here, :] + b_down[...]
        center = value - mean(value)
        inverse = lax.rsqrt(mean(center * center) + 1e-05)
        unit = center * inverse
        out[here, :] = (unit * gain_two[...] + shift_two[...]).astype(LOW)
        grad = cot[here, :].astype(F32)
        scaled = grad * gain_two[...]
        grad_resid = inverse * (scaled - mean(scaled) - unit * mean(scaled * unit))
        acc[here, :] = grad_resid
        grad_low[here, :] = grad_resid.astype(LOW)
        add_small(5, total(grad_resid))
        add_small(6, total(grad * unit))
        add_small(7, total(grad))

    loop(rows // ROWS, norm_two)
    leaving = [fetch(out, out_to)]

    def block_of(g, s):
        return g * n_mp + s

    def add_rows(start, source, offset, size):
        def one(k):
            here = rows_of(start + k * 16, 16)
            there = rows_of(offset + k * 16, 16)
            w[here, :] = (w[here, :].astype(F32) + source[there, :].astype(F32)).astype(LOW)

        loop(size // 16, one)

    def halve(g, s):
        m, k = ranks[s], block_of(g, s)
        for side in range(2):
            links.start(
                ("half", k, side),
                w.at[rows_of(region(g, m, 1 - c, side), 4 * piece)],
                half_in.at[k, side],
                core,
            )

    def quarter(g, s):
        m, k = ranks[s], block_of(g, s)
        for side, (bit, device) in enumerate(((x, x_side), (y, y_side))):
            start = region(g, m, c, side)
            links.wait(("half", k, side), half_in.at[k, side], core)
            other = 2 * (1 - bit) * piece
            add_rows(start + other, half_in.at[k, side], other, 2 * piece)
            links.start(
                ("quarter", k, side),
                w.at[rows_of(start + other, 2 * piece)],
                quarter_in.at[k, side],
                device,
            )
        for side, bit in enumerate((x, y)):
            start = region(g, m, c, side)
            own = 2 * bit * piece
            add_rows(start + own, half_in.at[k, side], own, 2 * piece)

    def eighth(g, s):
        m, k = ranks[s], block_of(g, s)
        sides = ((x, y, x_side, y_side), (y, x, y_side, x_side))
        for side, (high, bit, before, device) in enumerate(sides):
            start = region(g, m, c, side) + 2 * high * piece
            links.wait(("quarter", k, side), quarter_in.at[k, side], before)
            other = (1 - bit) * piece
            add_rows(start + other, quarter_in.at[k, side], other, piece)
            links.start(
                ("eighth", k, side),
                w.at[rows_of(start + other, piece)],
                eighth_in.at[k, side],
                device,
            )
        for side, (high, bit, before, device) in enumerate(sides):
            start = region(g, m, c, side) + 2 * high * piece
            own = bit * piece
            add_rows(start + own, quarter_in.at[k, side], own, piece)

    def to_plane(g, s):
        m, k = ranks[s], block_of(g, s)
        for side, (high, bit, device) in enumerate(((x, y, y_side), (y, x, x_side))):
            start = region(g, m, c, side) + (2 * high + bit) * piece
            links.wait(("eighth", k, side), eighth_in.at[k, side], device)
            add_rows(start, eighth_in.at[k, side], 0, piece)
            if s < n_mp - 1:
                links.start(
                    ("plane", g, side),
                    w.at[rows_of(start, piece)],
                    plane_in.at[g, me, side],
                    (dp, m),
                    m,
                    me,
                )

    outs = [
        Gather(
            ("out", g),
            grad_w.at[g],
            [c * (d // 2) + side * (d // 4) for side in range(2)],
            [(1 - c) * (d // 2) + side * (d // 4) for side in range(2)],
        )
        for g in range(3)
    ]

    def finish(g):
        to_plane(g, n_mp - 1)
        for side, (high, bit) in enumerate(((x, y), (y, x))):
            start = region(g, me, c, side) + (2 * high + bit) * piece
            goal = c * (d // 2) + side * (d // 4) + (2 * high + bit) * piece
            for k in others:
                m = ranks[k]
                links.wait(("plane", g, side), plane_in.at[g, m, side], (dp, m), m)

            def step(k):
                value = w[rows_of(start + k * 16, 16), :].astype(F32)
                for s in others:
                    value = value + plane_in[g, ranks[s], side, rows_of(k * 16, 16), :].astype(F32)
                grad_w[g, rows_of(goal + k * 16, 16), :] = value.astype(LOW)

            loop(piece // 16, step)
        outs[g].one()

    def spread(g):
        outs[g].two()

    def pair(g):
        outs[g].three()

    def leave(g):
        outs[g].done()
        leaving.append(fetch(grad_w.at[g], grad_w_to.at[g]))

    def down_back(k):
        m = ranks[k]
        here = rows_of(2 * group + m * d, d)
        small_up[m] = jnp.zeros((1, d), F32)

        def step(r):
            tile = rows_of(r * TILE, TILE)
            grad_up = dot_nt(grad_low[tile, :], w[here, :]) * slope[m, tile, :].astype(F32)
            act[m, tile, :] = grad_up.astype(LOW)
            small_up[m] = small_up[m] + total(grad_up)

        loop(rows // TILE, step)

        def weight(r):
            tile = rows_of(r * (d // 2), d // 2)
            there = rows_of(2 * group + m * d + r * (d // 2), d // 2)
            w[there, :] = dot(act_t[m, tile, :], grad_low[...]).astype(LOW)

        loop(2, weight)

    def up_back(k):
        m = ranks[k]
        here = rows_of(group + m * d, d)

        def step(r):
            tile = rows_of(r * TILE, TILE)
            acc[tile, :] = acc[tile, :] + dot_nt(act[m, tile, :], w[here, :])

        loop(rows // TILE, step)

        def weight(r):
            tile = rows_of(r * (d // 2), d // 2)
            there = rows_of(group + m * d + r * (d // 2), d // 2)
            w[there, :] = dot(normed_t[tile, :], act[m]).astype(LOW)

        loop(2, weight)

    def norm_back():
        def step(r):
            here = at(r * ROWS, ROWS, ROWS)
            grad = acc[here, :]
            unit = unit_one[here, :]
            scaled = grad * gain_one[...]
            inverse = inv_one[here, 0:1]
            grad_resid = inverse * (scaled - mean(scaled) - unit * mean(scaled * unit))
            grad_tok[here, :] = grad_resid
            grad_low[here, :] = grad_resid.astype(LOW)
            add_small(2, total(grad_resid))
            add_small(3, total(grad * unit))
            add_small(4, total(grad))

        loop(rows // ROWS, step)

    def out_back():
        def step(r):
            tile = rows_of(r * TILE, TILE)
            ctx[tile, :] = dot_nt(grad_low[tile, :], w[3 * d : 4 * d, :]).astype(LOW)

        loop(rows // TILE, step)

        def weight(r):
            tile = rows_of(r * (d // 2), d // 2)
            there = rows_of(3 * d + r * (d // 2), d // 2)
            w[there, :] = dot(ctx_t[tile, :], grad_low[...]).astype(LOW)

        loop(2, weight)

    def attend_back(index):
        b, p = index // pairs, index % pairs
        here = at(b * BLOCK, BLOCK, BLOCK)
        query = qkv[p, here, :]
        key = qkv[pairs + p, here, :]
        value = qkv[2 * pairs + p, here, :]
        grad = ctx[here, at(p * BLOCK, BLOCK, BLOCK)]
        both = prob[index]
        grad_prob = dot_nt(two_heads(value), grad)
        wide = both.astype(F32)

        def score_back(part, grad_part):
            return part * (grad_part - jnp.sum(part * grad_part, axis=0, keepdims=True))

        low_score = jnp.concatenate(
            [
                score_back(wide[:BLOCK], grad_prob[:BLOCK]),
                score_back(wide[BLOCK:], grad_prob[BLOCK:]),
            ],
            axis=0,
        ).astype(LOW)

        def beside(stack):
            return jnp.concatenate([stack[:BLOCK], stack[BLOCK:]], axis=1)

        def keep(kind, natural, turned):
            qkv[kind * pairs + p, here, :] = natural
            grad_qkv_t[at((kind * pairs + p) * BLOCK, BLOCK, BLOCK), here] = turned

        grad_query = (dot(two_heads_t(key), low_score) * HD**-0.5).astype(LOW)
        grad_key = (dot(beside(low_score), two_heads(query)) * HD**-0.5).astype(LOW)
        grad_value = dot(beside(both), two_heads(grad)).astype(LOW)
        keep(0, grad_query.T, grad_query)
        keep(1, grad_key, grad_key.T)
        keep(2, grad_value, grad_value.T)

    def attend_back_part(part):
        count = blocks * pairs // ATTEND_BACK_PARTS
        loop(count, lambda i: attend_back(part * count + i), unroll=2)

    def small_send():
        for k in range(pairs):
            columns = slice(k * BLOCK, (k + 1) * BLOCK)
            small[0, 0:1, columns] = total(qkv[k].astype(F32))
            small[0, 1:2, columns] = total(qkv[2 * pairs + k].astype(F32))
        for m in range(n_mp):
            small[0, 8 + m : 9 + m, :] = small_up[m]
        links.start(("small", 0), small.at[0], small_in.at[0], core)

    def small_next(k):
        before, device = ((core, x_side), (x_side, y_side), (y_side, None))[k]
        links.wait(("small", k), small_in.at[k], before)
        if device is None:
            small_plane[me] = small[k] + small_in[k]
            for s in others:
                m = ranks[s]
                links.start("small", small_plane.at[me], small_plane.at[me], (dp, m), m, me)
        else:
            small[k + 1] = small[k] + small_in[k]
            links.start(("small", k + 1), small.at[k + 1], small_in.at[k + 1], device)

    def small_done():
        for s in others:
            m = ranks[s]
            links.wait("small", small_plane.at[m], (dp, m), m)
        value = small_plane[0]
        for m in range(1, n_mp):
            value = value + small_plane[m]
        grad_small[...] = value
        ups = value[8:16, :]
        own = total(jnp.where(lax.broadcasted_iota(jnp.int32, ups.shape, 0) == me, ups, 0.0))
        grad_small[8:9, :] = own
        turned = pltpu.roll(value[0:8, :], (n_mp - me) % n_mp * shard, 1)
        grad_small[0:2, :] = turned[0:2, :]
        leaving.append(fetch(grad_small, grad_small_to))

    def token_back():
        def step(kind):
            whole = jnp.concatenate([qkv[kind * pairs + k] for k in range(pairs)], axis=1)
            grad_tok[...] = grad_tok[...] + dot(whole, w[rows_of(kind * d, d), :])

        loop(3, step)
        leaving.append(fetch(grad_tok, grad_tok_to))

    def project_back():
        def step(r):
            here = rows_of(r * (d // 2), d // 2)
            w[here, :] = dot(grad_qkv_t[here, :], tok[...]).astype(LOW)

        loop(6, step)

    backward = {
        "down": down_back,
        "up": up_back,
        "norm": norm_back,
        "out": out_back,
        "attend": attend_back_part,
        "token": token_back,
        "project": project_back,
        "halve": halve,
        "quarter": quarter,
        "eighth": eighth,
        "plane": to_plane,
        "finish": finish,
        "two": spread,
        "three": pair,
        "done": leave,
        "small_send": small_send,
        "small_next": small_next,
        "small_done": small_done,
    }
    for name, *args in BACKWARD:
        backward[name](*args)
    links.drain()
    for copy in leaving:
        copy.wait()


def run_kernel(n_mp, tokens, cotangent, segments, weights, shards, vectors):
    rows, d = tokens.shape
    anywhere = pl.BlockSpec(memory_space=pl.ANY)
    blocks = rows // BLOCK
    pairs = d // BLOCK
    piece = d // 16
    low = lambda *shape: pltpu.VMEM(shape, LOW)
    full = lambda *shape: pltpu.VMEM(shape, F32)
    block_count = 3 * n_mp
    names = 256
    flops = 2 * rows * d * d * 12 * 3
    operands = (tokens, cotangent, segments, *weights, *shards, *vectors)
    return pl.pallas_call(
        functools.partial(layer_kernel, n_mp),
        out_shape=(
            jax.ShapeDtypeStruct((rows, d), LOW),
            jax.ShapeDtypeStruct((rows, d), F32),
            jax.ShapeDtypeStruct((3, d, d), LOW),
            jax.ShapeDtypeStruct((16, d), F32),
        ),
        in_specs=[anywhere] * len(operands),
        out_specs=(anywhere,) * 4,
        scratch_shapes=[
            low(rows, d),
            low(rows, d),
            pltpu.VMEM(segments.shape, jnp.int32),
            full(*shards[0].shape),
            full(*shards[1].shape),
            full(len(vectors), *vectors[0].shape),
            full(len(vectors), 1, d),
            low(rows, d),
            full(rows, d),
            low(3, d, d),
            full(16, d),
            low(3 * n_mp * d, d),
            low(block_count, 2, 4 * piece, d),
            low(block_count, 2, 2 * piece, d),
            low(block_count, 2, piece, d),
            low(3, n_mp, 2, piece, d),
            low(3 * pairs, rows, BLOCK),
            low(3 * d, rows),
            low(blocks * pairs, 2 * BLOCK, BLOCK),
            low(rows, d),
            low(d, rows),
            full(rows, d),
            full(rows, BLOCK),
            low(rows, d),
            low(d, rows),
            full(rows, d),
            low(rows, d),
            low(n_mp, rows, d),
            low(n_mp, d, rows),
            low(n_mp, rows, d),
            full(blocks, BLOCK, BLOCK),
            full(n_mp, 8, d),
            full(6, 1, d // 2),
            full(3, 16, d),
            full(3, 16, d),
            full(n_mp, 1, d),
            full(n_mp, 16, d),
            pltpu.SemaphoreType.DMA((32,)),
            pltpu.SemaphoreType.DMA((names,)),
            pltpu.SemaphoreType.DMA((names,)),
        ],
        compiler_params=pltpu.CompilerParams(
            collective_id=0, has_side_effects=True, vmem_limit_bytes=63 << 20
        ),
        cost_estimate=pl.CostEstimate(flops=flops, bytes_accessed=1 << 24, transcendentals=1 << 21),
    )(*operands)


def finish_kernel(
    out,
    grad_tok,
    grad_w,
    small,
    out_to,
    grad_tok_to,
    query_to,
    key_to,
    value_to,
    attn_to,
    up_to,
    down_to,
    b_query_to,
    b_value_to,
    *refs,

):
    vectors_to, refs = refs[:7], refs[7:]
    held, wide, lines, parts, vectors, low_rows, full_rows, sems = refs
    d = held.shape[-1]
    shard = query_to.shape[0]
    pieces = d // shard
    count = 0

    def fetch(src, dst):
        nonlocal count
        copy = pltpu.make_async_copy(src, dst, sems.at[count])
        count += 1
        copy.start()
        return copy

    first = fetch(small, lines)
    loads = {}
    for g in range(3):
        for k in range(pieces):
            here = pl.ds(k * shard, shard)
            loads[g, k] = fetch(grad_w.at[g, here], held.at[g, here])
    passing = [fetch(out, low_rows), fetch(grad_tok, full_rows)]
    first.wait()
    for k in range(2):
        parts[k] = lines[k : k + 1, :shard]
    for k in range(vectors.shape[0]):
        for j in range(d // BLOCK):
            vectors[k, j : j + 1, :] = lines[2 + k : 3 + k, j * BLOCK : (j + 1) * BLOCK]
    stores = [fetch(parts.at[0], b_query_to), fetch(parts.at[1], b_value_to)]
    stores += [fetch(vectors.at[k], ref) for k, ref in enumerate(vectors_to)]
    for g in range(3):
        for k in range(pieces):
            loads[g, k].wait()

            def widen(r, g=g, k=k):
                here = at(k * shard + r * 16, 16, 16)
                wide[g, here, :] = held[g, here, :].astype(F32)

            loop(shard // 16, widen, unroll=2)
            here = pl.ds(k * shard, shard)
            if g == 0:
                stores.append(fetch(wide.at[0, here], (query_to, key_to, value_to, attn_to)[k]))
            else:
                stores.append(fetch(wide.at[g, here], (up_to, down_to)[g - 1].at[here]))
        if g == 0:
            for copy in passing:
                copy.wait()
            stores += [fetch(low_rows, out_to), fetch(full_rows, grad_tok_to)]
    for copy in stores:
        copy.wait()


def run_finish(shard, out, grad_tok, grad_w, small):
    d = out.shape[1]
    anywhere = pl.BlockSpec(memory_space=pl.ANY)
    full = lambda *shape: jax.ShapeDtypeStruct(shape, F32)
    shapes = (
        [jax.ShapeDtypeStruct(out.shape, LOW), full(*grad_tok.shape)]
        + [full(shard, d)] * 4
        + [full(d, d)] * 2
        + [full(1, shard)] * 2
        + [full(d // BLOCK, BLOCK)] * 7
    )
    return pl.pallas_call(
        finish_kernel,
        out_shape=tuple(shapes),
        in_specs=[anywhere] * 4,
        out_specs=(anywhere,) * len(shapes),
        scratch_shapes=[
            pltpu.VMEM(grad_w.shape, grad_w.dtype),
            pltpu.VMEM(grad_w.shape, F32),
            pltpu.VMEM(small.shape, F32),
            pltpu.VMEM((2, 1, shard), F32),
            pltpu.VMEM((7, d // BLOCK, BLOCK), F32),
            pltpu.VMEM(out.shape, LOW),
            pltpu.VMEM(grad_tok.shape, F32),
            pltpu.SemaphoreType.DMA((64,)),
        ],
        compiler_params=pltpu.CompilerParams(vmem_limit_bytes=60 << 20),
        cost_estimate=pl.CostEstimate(flops=0, bytes_accessed=1 << 24, transcendentals=0),
    )(out, grad_tok, grad_w, small)


def per_device(
    n_dp,
    n_mp,
    tokens,
    segment_ids,
    w_query,
    b_query,
    w_key,
    w_value,
    b_value,
    w_out,
    b_out,
    gain_one,
    shift_one,
    w_up,
    b_up,
    w_down,
    b_down,
    gain_two,
    shift_two,
    cotangent,
):
    d = tokens.shape[1]
    shard = d // n_mp
    vectors = (b_up, b_out, gain_one, shift_one, b_down, gain_two, shift_two)
    out, grad_tokens, grad_w, small = run_kernel(
        n_mp,
        tokens,
        cotangent,
        segment_ids.reshape(-1, BLOCK),
        (w_query.T, w_key.T, w_value.T, w_out, w_up, w_down),
        (b_query.reshape(1, -1), b_value.reshape(1, -1)),
        tuple(v.reshape(-1, BLOCK) for v in vectors),
    )
    if n_dp > PLANE:
        groups = [[k + PLANE * h for h in range(n_dp // PLANE)] for k in range(PLANE)]
        grad_w, small = lax.psum(
            (grad_w.astype(F32), small), "dp", axis_index_groups=groups
        )
    (
        out,
        grad_tokens,
        grad_w_query,
        grad_w_key,
        grad_w_value,
        grad_w_out,
        grad_w_up,
        grad_w_down,
        grad_b_query,
        grad_b_value,
        *grad_vectors,
    ) = run_finish(shard, out, grad_tokens, grad_w, small)
    grad_b_out, grad_gain_one, grad_shift_one, grad_b_down, grad_gain_two, grad_shift_two = [
        grad_vectors[k].reshape(-1) for k in range(6)
    ]
    return (
        out,
        grad_tokens,
        grad_w_query.T,
        grad_b_query.reshape(-1),
        grad_w_key.T,
        grad_w_value.T,
        grad_b_value.reshape(-1),
        grad_w_out,
        grad_b_out,
        grad_gain_one,
        grad_shift_one,
        grad_w_up,
        grad_vectors[6].reshape(-1),
        grad_w_down,
        grad_b_down,
        grad_gain_two,
        grad_shift_two,
    )


def solution(mesh):
    n_dp, n_mp = mesh.shape["dp"], mesh.shape["mp"]
    return jax.shard_map(
        functools.partial(per_device, n_dp, n_mp),
        mesh=mesh,
        in_specs=(
            P(("dp", "mp"), None),
            P("dp"),
            P(None, "mp"),
            P("mp"),
            P(None, "mp"),
            P(None, "mp"),
            P("mp"),
            P("mp", None),
            P(),
            P(),
            P(),
            P(None, "mp"),
            P("mp"),
            P("mp", None),
            P(),
            P(),
            P(),
            P(("dp", "mp"), None),
        ),
        out_specs=(
            P(("dp", "mp"), None),
            P(("dp", "mp"), None),
            P(None, "mp"),
            P("mp"),
            P(None, "mp"),
            P(None, "mp"),
            P("mp"),
            P("mp", None),
            P(),
            P(),
            P(),
            P(None, "mp"),
            P("mp"),
            P("mp", None),
            P(),
            P(),
            P(),
        ),
        check_vma=False,
    )
```

```python
import functools

import jax
import jax.numpy as jnp
from jax import lax
from jax.experimental import pallas as pl
from jax.experimental.pallas import tpu as pltpu
from jax.sharding import PartitionSpec as P

HD = 64
BLOCK = 128
TILE = 256
ROWS = 64
PLANE = 8
ATTEND_PARTS = 2
ATTEND_BACK_PARTS = 6
DOUBLED = (1, 2)
SENDS = ((0, 2, 1), (0, 1, 2), (0, 1, 2))
NEAR = (2,)
GELU = 0.7978845608028654
FORWARD = (
    ("send", 0), ("one", 0, 0), ("one", 0, 1), ("masks",), ("send", 1), ("biases",),
    ("two", 0, 0), ("two", 0, 1), ("one", 0, 2), ("two", 1, 0), ("three", 0, 0), ("one", 1, 1),
    ("send", 2), ("two", 0, 2), ("done", 0, 0), ("three", 1, 0), ("one", 1, 2), ("three", 0, 1),
    ("two", 1, 1), ("project", 0), ("attend", 0, 0), ("three", 0, 2), ("done", 0, 1),
    ("attend", 0, 1), ("two", 1, 2), ("done", 0, 2), ("done", 1, 0), ("project", 1),
    ("two", 2, 0), ("attend", 1, 0), ("attend", 1, 1), ("attn_out",), ("one", 2, 1),
    ("three", 1, 2), ("three", 1, 1), ("norm_one",), ("one", 2, 2), ("up", 3), ("done", 1, 1),
    ("two", 2, 1), ("up", 0), ("two", 2, 2), ("three", 2, 0), ("up", 1), ("done", 1, 2),
    ("up", 2), ("done", 2, 0), ("three", 2, 1), ("down", 3), ("down", 0), ("three", 2, 2),
    ("done", 2, 1), ("down", 1), ("done", 2, 2), ("down", 2),
)
BACKWARD = (
    ("down", 2), ("halve", 2, 2), ("down", 1), ("quarter", 2, 2), ("halve", 2, 1), ("down", 0),
    ("halve", 2, 0), ("quarter", 2, 1), ("down", 3), ("up", 1), ("near", 2), ("eighth", 2, 2),
    ("halve", 1, 1), ("up", 2), ("eighth", 2, 1), ("halve", 1, 2), ("quarter", 1, 1), ("up", 3),
    ("halve", 2, 3), ("up", 0), ("quarter", 1, 2), ("halve", 1, 0), ("norm",), ("out",),
    ("attend", 0), ("eighth", 1, 1), ("halve", 1, 3), ("quarter", 1, 0), ("attend", 1),
    ("plane", 2, 1), ("attend", 2), ("quarter", 1, 3), ("eighth", 1, 2), ("attend", 3),
    ("attend", 4), ("quarter", 2, 3), ("attend", 5), ("eighth", 1, 0), ("plane", 1, 1),
    ("token",), ("project",), ("plane", 2, 2), ("halve", 0, 2), ("eighth", 1, 3),
    ("small_send",), ("halve", 0, 1), ("quarter", 0, 2), ("small_next", 0), ("plane", 1, 2),
    ("halve", 0, 3), ("halve", 0, 0), ("quarter", 0, 1), ("eighth", 0, 2), ("quarter", 0, 0),
    ("eighth", 0, 1), ("plane", 1, 0), ("plane", 0, 2), ("eighth", 2, 3), ("eighth", 0, 0),
    ("quarter", 0, 3), ("finish", 2), ("plane", 0, 1), ("plane", 0, 0), ("finish", 1),
    ("eighth", 0, 3), ("two", 2), ("small_next", 1), ("finish", 0), ("two", 1), ("two", 0),
    ("small_next", 2), ("three", 2), ("three", 1), ("done", 1), ("done", 2), ("three", 0),
    ("small_done",), ("done", 0),
)
MASKED = -1000000000.0
MESH = pl.DeviceIdType.MESH
F32 = jnp.float32
LOW = jnp.bfloat16


def dot(left, right):
    return jnp.dot(left, right, preferred_element_type=F32)


def dot_nt(left, right):
    return lax.dot_general(left, right, (((1,), (1,)), ((), ())), preferred_element_type=F32)


def mean(value):
    return jnp.mean(value, axis=-1, keepdims=True)


def total(value):
    return jnp.sum(value, axis=0, keepdims=True)


def at(start, size, unit):
    return pl.ds(pl.multiple_of(start, unit), size)


def loop(count, body, unroll=1):
    def step(index, carry):
        body(index)
        return carry

    lax.fori_loop(0, count, step, 0, unroll=unroll)


class Links:
    def __init__(self, send, recv):
        self.send, self.recv = send, recv
        self.names = {}
        self.used = 0
        self.open = []

    def index(self, name, width):
        if name not in self.names:
            self.names[name] = self.used
            self.used += width
        return self.names[name]

    def copy(self, name, src, dst, device, there=None, here=None):
        first = self.index(name, 1 if there is None else 4)
        going, coming = (first, first) if there is None else (first + there, first + here)
        return pltpu.make_async_remote_copy(
            src_ref=src,
            dst_ref=dst,
            send_sem=self.send.at[going],
            recv_sem=self.recv.at[coming],
            device_id=device,
            device_id_type=MESH,
        )

    def start(self, *args):
        copy = self.copy(*args)
        copy.start()
        self.open.append(copy)

    def wait(self, name, dst, device, there=None):
        self.copy(name, dst, dst, device, there, there).wait_recv()

    def drain(self):
        for copy in self.open:
            copy.wait_send()
        self.open = []


def layer_kernel(
    n_mp,
    tok_in,
    cot_in,
    seg_in,
    w_query,
    w_key,
    w_value,
    w_out,
    w_up,
    w_down,
    b_query_in,
    b_value_in,
    *refs,
):
    vectors_in, refs = refs[:7], refs[7:]
    (
        out_to,
        grad_tok_to,
        grad_w_to,
        grad_small_to,
        tok,
        cot,
        seg,
        b_query,
        b_value,
        vectors,
        lines,
        out,
        grad_tok,
        grad_w,
        grad_small,
        w,
        half_in,
        quarter_in,
        eighth_in,
        plane_in,
        near_in,
        qkv,
        grad_qkv_t,
        prob,
        ctx,
        ctx_t,
        unit_one,
        inv_one,
        normed,
        normed_t,
        acc,
        grad_low,
        act,
        act_t,
        slope,
        mask,
        bias_in,
        qkv_bias,
        small,
        small_in,
        small_up,
        small_plane,
        local_sem,
        send_sem,
        recv_sem,
    ) = refs
    b_up, b_out, gain_one, shift_one, b_down, gain_two, shift_two = [lines.at[k] for k in range(7)]
    rows, d = tok.shape
    group = n_mp * d
    shard = d // n_mp
    piece = d // 16
    pairs = d // BLOCK
    blocks = rows // BLOCK

    dp, me = lax.axis_index("dp"), lax.axis_index("mp")
    c, x, y = dp % 2, dp // 2 % 2, dp // 4 % 2
    core = (dp + 1 - 2 * c, me)
    x_side = (dp + 2 - 4 * x, me)
    y_side = (dp + 4 - 8 * y, me)

    ranks = (me + 1 - 2 * (me % 2), 2 - me // 2, 3 - 3 * (me // 2), me)
    others = range(n_mp - 1)

    def rows_of(start, size):
        return at(start, size, 16)

    count = 0

    def fetch(src, dst):
        nonlocal count
        copy = pltpu.make_async_copy(src, dst, local_sem.at[count])
        count += 1
        copy.start()
        return copy

    own_w = [
        fetch(ref, w.at[rows_of(kind * d + me * shard, shard)])
        for kind, ref in enumerate((w_query, w_key, w_value, w_out))
    ]
    own_b = [fetch(b_query_in, b_query), fetch(b_value_in, b_value)]
    own_b += [fetch(ref, vectors.at[k]) for k, ref in enumerate(vectors_in)]
    own_w.append(fetch(w_up, w.at[rows_of(group + me * d, d)]))
    own_w.append(fetch(w_down, w.at[rows_of(2 * group + me * d, d)]))
    own_rows = [fetch(seg_in, seg), fetch(tok_in, tok), fetch(cot_in, cot)]

    barrier = pltpu.get_barrier_semaphore()
    partners = [core, x_side, y_side] + [(dp, ranks[k]) for k in others]
    for partner in partners:
        pl.semaphore_signal(barrier, inc=1, device_id=partner, device_id_type=MESH)

    for copy in own_b:
        copy.wait()
    for k in range(len(vectors_in)):
        parts = [vectors[k, j : j + 1, :] for j in range(d // BLOCK)]
        lines[k] = jnp.concatenate(parts, axis=1)
    pad = jnp.zeros((1, d - shard), F32)
    for k, ref in enumerate((b_query, b_value)):
        placed = jnp.broadcast_to(jnp.concatenate([ref[...], pad], axis=1), (8, d))
        bias_in[me, k : k + 1, :] = pltpu.roll(placed, me * shard, 1)[0:1, :]
    bias_in[me, 2:3, :] = b_up[...]

    for copy in own_w:
        copy.wait()
    pl.semaphore_wait(barrier, len(partners))

    links = Links(send_sem, recv_sem)

    def region(g, m, core_of, side):
        if g == 0:
            return (2 * core_of + side) * d + m * shard
        return g * group + m * d + core_of * (d // 2) + side * (d // 4)

    class Gather:
        def __init__(self, name, ref, mine, theirs):
            self.name, self.ref = name, ref
            self.mine, self.theirs = mine, theirs

        def at(self, start, size):
            return self.ref.at[rows_of(start, size)]

        def one(self):
            a = self.at(self.mine[0] + (2 * x + y) * piece, piece)
            b = self.at(self.mine[1] + (2 * y + x) * piece, piece)
            links.start((self.name, 1, 0), a, a, y_side)
            links.start((self.name, 1, 1), b, b, x_side)

        def joined(self, side):
            if side == 0:
                start, device = self.mine[0] + (2 * x + 1 - y) * piece, y_side
            else:
                start, device = self.mine[1] + (2 * y + 1 - x) * piece, x_side
            links.wait((self.name, 1, side), self.at(start, piece), device)

        def two(self, joined=None):
            (joined or self.joined)(0)
            a = self.at(self.mine[0] + 2 * x * piece, 2 * piece)
            links.start((self.name, 2, 0), a, a, x_side)
            (joined or self.joined)(1)
            b = self.at(self.mine[1] + 2 * y * piece, 2 * piece)
            links.start((self.name, 2, 1), b, b, y_side)

        def three(self):
            links.wait(
                (self.name, 2, 0), self.at(self.mine[0] + 2 * (1 - x) * piece, 2 * piece), x_side
            )
            a = self.at(self.mine[0], 4 * piece)
            links.start((self.name, 3, 0), a, a, core)
            links.wait(
                (self.name, 2, 1), self.at(self.mine[1] + 2 * (1 - y) * piece, 2 * piece), y_side
            )
            b = self.at(self.mine[1], 4 * piece)
            links.start((self.name, 3, 1), b, b, core)

        def done(self):
            for side in range(2):
                links.wait((self.name, 3, side), self.at(self.theirs[side], 4 * piece), core)

    for k in others:
        m = ranks[k]
        links.start("bias", bias_in.at[me], bias_in.at[me], (dp, m), m, me)

    def share(g, k, m, side):
        start = region(g, m, c, side)
        high, bit = (x, y) if side == 0 else (y, x)
        if k == 0 and g in DOUBLED:
            return w.at[rows_of(start + 2 * high * piece, 2 * piece)]
        return w.at[rows_of(start + (2 * high + bit) * piece, piece)]

    def send(g):
        for k in SENDS[g]:
            for side in range(2):
                rows_in = share(g, k, me, side)
                links.start(("w", g, side), rows_in, rows_in, (dp, ranks[k]), ranks[k], me)

    gathers = {}
    for g in range(3):
        for k in others:
            m = ranks[k]
            gathers[g, k] = Gather(
                ("in", g, k),
                w,
                [region(g, m, c, side) for side in range(2)],
                [region(g, m, 1 - c, side) for side in range(2)],
            )

    def landed(g, k, side):
        m = ranks[k]
        links.wait(("w", g, side), share(g, k, m, side), (dp, m), m)

    def one(g, k):
        for side in range(2):
            landed(g, k, side)
        gathers[g, k].one()

    def two(g, k):
        whole = k == 0 and g in DOUBLED
        gathers[g, k].two(functools.partial(landed, g, k) if whole else None)

    def three(g, k):
        gathers[g, k].three()

    def done(g, k):
        gathers[g, k].done()

    def masks():
        for copy in own_rows:
            copy.wait()
        for b in range(blocks):
            line = seg[pl.ds(me * blocks + b, 1), :]
            across = jnp.broadcast_to(line, (BLOCK, BLOCK))
            mask[b] = jnp.where(across == across.T, 0.0, MASKED)

    def biases():
        for k in others:
            m = ranks[k]
            links.wait("bias", bias_in.at[m], (dp, m), m)
        row = jnp.zeros((2, d), F32)
        for m in range(n_mp):
            row = row + bias_in[m, 0:2, :]
        for h in range(2):
            columns = slice(h * (d // 2), (h + 1) * (d // 2))
            qkv_bias[h] = row[0:1, columns]
            qkv_bias[2 + h] = jnp.zeros((1, d // 2), F32)
            qkv_bias[4 + h] = row[1:2, columns]

    half_pairs = pairs // 2

    def half_of(k):
        return me // 2 if k == 0 else 1 - me // 2

    def project(k):
        half = half_of(k)

        def one_kind(kind):
            here = rows_of(kind * d + half * (d // 2), d // 2)
            part = dot_nt(tok[...], w[here, :]) + qkv_bias[2 * kind + half]
            for j in range(half_pairs):
                columns = part[:, j * BLOCK : (j + 1) * BLOCK]
                qkv[kind * pairs + half * half_pairs + j] = columns.astype(LOW)

        loop(3, one_kind, unroll=3)

    lane = lax.broadcasted_iota(jnp.int32, (1, BLOCK), 1)
    first = jnp.where(lane < HD, 1.0, 0.0).astype(LOW)
    second = jnp.where(lane < HD, 0.0, 1.0).astype(LOW)
    none = jnp.zeros((HD, BLOCK), LOW)

    def two_heads(value):
        return jnp.concatenate([value * first, value * second], axis=0)

    def two_heads_t(value):
        turned = value.T
        upper = jnp.concatenate([turned[:HD], none], axis=1)
        lower = jnp.concatenate([none, turned[HD:]], axis=1)
        return jnp.concatenate([upper, lower], axis=0)

    def softmax(score):
        expo = jnp.exp(score - jnp.max(score, axis=0, keepdims=True))
        return expo * (1.0 / jnp.sum(expo, axis=0, keepdims=True))

    def attend(b, p):
        here = at(b * BLOCK, BLOCK, BLOCK)
        columns = at(p * BLOCK, BLOCK, BLOCK)
        query = qkv[p, here, :]
        key = qkv[pairs + p, here, :]
        value = qkv[2 * pairs + p, here, :]
        score = dot_nt(two_heads(key), query) * HD**-0.5
        hidden = mask[b]
        both = jnp.concatenate(
            [softmax(score[:BLOCK] + hidden), softmax(score[BLOCK:] + hidden)], axis=0
        ).astype(LOW)
        prob[b * pairs + p] = both
        context = dot(two_heads_t(value), both).astype(LOW)
        ctx_t[columns, here] = context
        ctx[here, columns] = context.T

    def attend_part(k, part):
        count = blocks * half_pairs // ATTEND_PARTS

        def step(i):
            i = i + part * count
            attend(i % blocks, half_of(k) * half_pairs + i // blocks)

        loop(count, step, unroll=count)

    def attn_out():
        acc[...] = dot(ctx[...], w[3 * d : 4 * d, :])

    def norm_one():
        def step(r):
            here = at(r * ROWS, ROWS, ROWS)
            value = tok[here, :].astype(F32) + acc[here, :] + b_out[...]
            center = value - mean(value)
            inverse = lax.rsqrt(mean(center * center) + 1e-05)
            unit = center * inverse
            unit_one[here, :] = unit
            inv_one[here, :] = jnp.broadcast_to(inverse, (ROWS, BLOCK))
            normed[here, :] = (unit * gain_one[...] + shift_one[...]).astype(LOW)

        loop(rows // ROWS, step)

        def turn(r):
            here = at(r * BLOCK, BLOCK, BLOCK)
            normed_t[:, here] = normed[here, :].T

        loop(blocks, turn)

    def feed_up(k):
        m = ranks[k]
        acc[...] = dot(normed[...], w[rows_of(group + m * d, d), :]) + bias_in[m, 2:3, :]

        def gelu(r):
            here = at(r * 16, 16, 16)
            u = acc[here, :]
            square = u * u
            inner = jnp.tanh(u * (GELU + GELU * 0.044715 * square))
            cdf = 0.5 + 0.5 * inner
            act[m, here, :] = (u * cdf).astype(LOW)
            slope_in = 0.5 * GELU + (1.5 * 0.044715 * GELU) * square
            slope[m, here, :] = (cdf + u * (1.0 - inner * inner) * slope_in).astype(LOW)

        loop(rows // 16, gelu)

        def turn(r):
            here = at(r * BLOCK, BLOCK, BLOCK)
            act_t[m, :, here] = act[m, here, :].T

        loop(blocks, turn)

    def feed_down(k):
        m = ranks[k]
        part = dot(act[m], w[rows_of(2 * group + m * d, d), :])
        acc[...] = part if k == n_mp - 1 else acc[...] + part

    forward = {
        "send": send,
        "one": one,
        "two": two,
        "three": three,
        "done": done,
        "masks": masks,
        "biases": biases,
        "project": project,
        "attend": attend_part,
        "attn_out": attn_out,
        "norm_one": norm_one,
        "up": feed_up,
        "down": feed_down,
    }
    for name, *args in FORWARD:
        forward[name](*args)
    links.drain()

    small[...] = jnp.zeros(small.shape, F32)

    def add_small(row, value):
        small[0, row : row + 1, :] = small[0, row : row + 1, :] + value

    def norm_two(r):
        here = at(r * ROWS, ROWS, ROWS)
        unit = unit_one[here, :]
        value = unit * gain_one[...] + shift_one[...] + acc[here, :] + b_down[...]
        center = value - mean(value)
        inverse = lax.rsqrt(mean(center * center) + 1e-05)
        unit = center * inverse
        out[here, :] = (unit * gain_two[...] + shift_two[...]).astype(LOW)
        grad = cot[here, :].astype(F32)
        scaled = grad * gain_two[...]
        grad_resid = inverse * (scaled - mean(scaled) - unit * mean(scaled * unit))
        acc[here, :] = grad_resid
        grad_low[here, :] = grad_resid.astype(LOW)
        add_small(5, total(grad_resid))
        add_small(6, total(grad * unit))
        add_small(7, total(grad))

    loop(rows // ROWS, norm_two)
    leaving = [fetch(out, out_to)]

    def block_of(g, s):
        return g * n_mp + s

    def add_rows(start, sources, offset, size):
        def one(k):
            here = rows_of(start + k * 16, 16)
            there = rows_of(offset + k * 16, 16)
            value = w[here, :].astype(F32)
            for source in sources:
                value = value + source[there, :].astype(F32)
            w[here, :] = value.astype(LOW)

        loop(size // 16, one)

    def halve(g, s):
        m, k = ranks[s], block_of(g, s)
        for side in range(2):
            links.start(
                ("half", k, side),
                w.at[rows_of(region(g, m, 1 - c, side), 4 * piece)],
                half_in.at[k, side],
                core,
            )

    def near(g):
        k = block_of(g, 0)
        for side in range(2):
            start = region(g, ranks[0], c, side)
            links.wait(("half", k, side), half_in.at[k, side], core)
            add_rows(start, (half_in.at[k, side],), 0, 4 * piece)
            links.start(
                ("near", g, side),
                w.at[rows_of(start, 4 * piece)],
                near_in.at[NEAR.index(g), side],
                (dp, ranks[0]),
            )

    def quarter(g, s):
        m, k = ranks[s], block_of(g, s)
        sources = []
        for side, (bit, device) in enumerate(((x, x_side), (y, y_side))):
            start = region(g, m, c, side)
            links.wait(("half", k, side), half_in.at[k, side], core)
            sources.append([half_in.at[k, side]])
            if s == n_mp - 1 and g in NEAR:
                arrived = near_in.at[NEAR.index(g), side]
                links.wait(("near", g, side), arrived, (dp, ranks[0]))
                sources[side].append(arrived)
            other = 2 * (1 - bit) * piece
            add_rows(start + other, sources[side], other, 2 * piece)
            links.start(
                ("quarter", k, side),
                w.at[rows_of(start + other, 2 * piece)],
                quarter_in.at[k, side],
                device,
            )
        for side, bit in enumerate((x, y)):
            start = region(g, m, c, side)
            own = 2 * bit * piece
            add_rows(start + own, sources[side], own, 2 * piece)

    def eighth(g, s):
        m, k = ranks[s], block_of(g, s)
        sides = ((x, y, x_side, y_side), (y, x, y_side, x_side))
        for side, (high, bit, before, device) in enumerate(sides):
            start = region(g, m, c, side) + 2 * high * piece
            links.wait(("quarter", k, side), quarter_in.at[k, side], before)
            other = (1 - bit) * piece
            add_rows(start + other, (quarter_in.at[k, side],), other, piece)
            links.start(
                ("eighth", k, side),
                w.at[rows_of(start + other, piece)],
                eighth_in.at[k, side],
                device,
            )
        for side, (high, bit, before, device) in enumerate(sides):
            start = region(g, m, c, side) + 2 * high * piece
            own = bit * piece
            add_rows(start + own, (quarter_in.at[k, side],), own, piece)

    def to_plane(g, s):
        m, k = ranks[s], block_of(g, s)
        for side, (high, bit, device) in enumerate(((x, y, y_side), (y, x, x_side))):
            start = region(g, m, c, side) + (2 * high + bit) * piece
            links.wait(("eighth", k, side), eighth_in.at[k, side], device)
            add_rows(start, (eighth_in.at[k, side],), 0, piece)
            if s < n_mp - 1:
                links.start(
                    ("plane", g, side),
                    w.at[rows_of(start, piece)],
                    plane_in.at[g, me, side],
                    (dp, m),
                    m,
                    me,
                )

    outs = [
        Gather(
            ("out", g),
            grad_w.at[g],
            [c * (d // 2) + side * (d // 4) for side in range(2)],
            [(1 - c) * (d // 2) + side * (d // 4) for side in range(2)],
        )
        for g in range(3)
    ]

    def finish(g):
        to_plane(g, n_mp - 1)
        senders = [ranks[k] for k in others if k or g not in NEAR]
        for side, (high, bit) in enumerate(((x, y), (y, x))):
            start = region(g, me, c, side) + (2 * high + bit) * piece
            goal = c * (d // 2) + side * (d // 4) + (2 * high + bit) * piece
            for m in senders:
                links.wait(("plane", g, side), plane_in.at[g, m, side], (dp, m), m)

            def step(k):
                value = w[rows_of(start + k * 16, 16), :].astype(F32)
                for m in senders:
                    value = value + plane_in[g, m, side, rows_of(k * 16, 16), :].astype(F32)
                grad_w[g, rows_of(goal + k * 16, 16), :] = value.astype(LOW)

            loop(piece // 16, step)
        outs[g].one()

    def spread(g):
        outs[g].two()

    def pair(g):
        outs[g].three()

    def leave(g):
        outs[g].done()
        leaving.append(fetch(grad_w.at[g], grad_w_to.at[g]))

    def down_back(k):
        m = ranks[k]
        here = rows_of(2 * group + m * d, d)
        small_up[m] = jnp.zeros((1, d), F32)

        def step(r):
            tile = rows_of(r * TILE, TILE)
            grad_up = dot_nt(grad_low[tile, :], w[here, :]) * slope[m, tile, :].astype(F32)
            act[m, tile, :] = grad_up.astype(LOW)
            small_up[m] = small_up[m] + total(grad_up)

        loop(rows // TILE, step, unroll=2)

        def weight(r):
            tile = rows_of(r * (d // 2), d // 2)
            there = rows_of(2 * group + m * d + r * (d // 2), d // 2)
            w[there, :] = dot(act_t[m, tile, :], grad_low[...]).astype(LOW)

        loop(2, weight, unroll=2)

    def up_back(k):
        m = ranks[k]
        here = rows_of(group + m * d, d)

        def step(r):
            tile = rows_of(r * TILE, TILE)
            acc[tile, :] = acc[tile, :] + dot_nt(act[m, tile, :], w[here, :])

        loop(rows // TILE, step, unroll=2)

        def weight(r):
            tile = rows_of(r * (d // 2), d // 2)
            there = rows_of(group + m * d + r * (d // 2), d // 2)
            w[there, :] = dot(normed_t[tile, :], act[m]).astype(LOW)

        loop(2, weight, unroll=2)

    def norm_back():
        def step(r):
            here = at(r * ROWS, ROWS, ROWS)
            grad = acc[here, :]
            unit = unit_one[here, :]
            scaled = grad * gain_one[...]
            inverse = inv_one[here, 0:1]
            grad_resid = inverse * (scaled - mean(scaled) - unit * mean(scaled * unit))
            grad_tok[here, :] = grad_resid
            grad_low[here, :] = grad_resid.astype(LOW)
            add_small(2, total(grad_resid))
            add_small(3, total(grad * unit))
            add_small(4, total(grad))

        loop(rows // ROWS, step)

    def out_back():
        def step(r):
            tile = rows_of(r * TILE, TILE)
            ctx[tile, :] = dot_nt(grad_low[tile, :], w[3 * d : 4 * d, :]).astype(LOW)

        loop(rows // TILE, step, unroll=2)

        def weight(r):
            tile = rows_of(r * (d // 2), d // 2)
            there = rows_of(3 * d + r * (d // 2), d // 2)
            w[there, :] = dot(ctx_t[tile, :], grad_low[...]).astype(LOW)

        loop(2, weight, unroll=2)

    def attend_back(index):
        b, p = index // pairs, index % pairs
        here = at(b * BLOCK, BLOCK, BLOCK)
        query = qkv[p, here, :]
        key = qkv[pairs + p, here, :]
        value = qkv[2 * pairs + p, here, :]
        grad = ctx[here, at(p * BLOCK, BLOCK, BLOCK)]
        both = prob[index]
        grad_prob = dot_nt(two_heads(value), grad)
        wide = both.astype(F32)

        def score_back(part, grad_part):
            return part * (grad_part - jnp.sum(part * grad_part, axis=0, keepdims=True))

        low_score = jnp.concatenate(
            [
                score_back(wide[:BLOCK], grad_prob[:BLOCK]),
                score_back(wide[BLOCK:], grad_prob[BLOCK:]),
            ],
            axis=0,
        ).astype(LOW)

        def beside(stack):
            return jnp.concatenate([stack[:BLOCK], stack[BLOCK:]], axis=1)

        def keep(kind, natural, turned):
            qkv[kind * pairs + p, here, :] = natural
            grad_qkv_t[at((kind * pairs + p) * BLOCK, BLOCK, BLOCK), here] = turned

        grad_query = (dot(two_heads_t(key), low_score) * HD**-0.5).astype(LOW)
        grad_key = (dot(beside(low_score), two_heads(query)) * HD**-0.5).astype(LOW)
        grad_value = dot(beside(both), two_heads(grad)).astype(LOW)
        keep(0, grad_query.T, grad_query)
        keep(1, grad_key, grad_key.T)
        keep(2, grad_value, grad_value.T)

    def attend_back_part(part):
        count = blocks * pairs // ATTEND_BACK_PARTS
        loop(count, lambda i: attend_back(part * count + i), unroll=count)

    def small_send():
        for k in range(pairs):
            columns = slice(k * BLOCK, (k + 1) * BLOCK)
            small[0, 0:1, columns] = total(qkv[k].astype(F32))
            small[0, 1:2, columns] = total(qkv[2 * pairs + k].astype(F32))
        for m in range(n_mp):
            small[0, 8 + m : 9 + m, :] = small_up[m]
        links.start(("small", 0), small.at[0], small_in.at[0], core)

    def small_next(k):
        before, device = ((core, x_side), (x_side, y_side), (y_side, None))[k]
        links.wait(("small", k), small_in.at[k], before)
        if device is None:
            small_plane[me] = small[k] + small_in[k]
            for s in others:
                m = ranks[s]
                links.start("small", small_plane.at[me], small_plane.at[me], (dp, m), m, me)
        else:
            small[k + 1] = small[k] + small_in[k]
            links.start(("small", k + 1), small.at[k + 1], small_in.at[k + 1], device)

    def small_done():
        for s in others:
            m = ranks[s]
            links.wait("small", small_plane.at[m], (dp, m), m)
        value = small_plane[0]
        for m in range(1, n_mp):
            value = value + small_plane[m]
        grad_small[...] = value
        ups = value[8:16, :]
        own = total(jnp.where(lax.broadcasted_iota(jnp.int32, ups.shape, 0) == me, ups, 0.0))
        grad_small[8:9, :] = own
        turned = pltpu.roll(value[0:8, :], (n_mp - me) % n_mp * shard, 1)
        grad_small[0:2, :] = turned[0:2, :]
        leaving.append(fetch(grad_small, grad_small_to))

    def token_back():
        def step(kind):
            whole = jnp.concatenate([qkv[kind * pairs + k] for k in range(pairs)], axis=1)
            grad_tok[...] = grad_tok[...] + dot(whole, w[rows_of(kind * d, d), :])

        loop(3, step)
        leaving.append(fetch(grad_tok, grad_tok_to))

    def project_back():
        def step(r):
            here = rows_of(r * (d // 2), d // 2)
            w[here, :] = dot(grad_qkv_t[here, :], tok[...]).astype(LOW)

        loop(6, step, unroll=2)

    backward = {
        "down": down_back,
        "up": up_back,
        "norm": norm_back,
        "out": out_back,
        "attend": attend_back_part,
        "token": token_back,
        "project": project_back,
        "halve": halve,
        "near": near,
        "quarter": quarter,
        "eighth": eighth,
        "plane": to_plane,
        "finish": finish,
        "two": spread,
        "three": pair,
        "done": leave,
        "small_send": small_send,
        "small_next": small_next,
        "small_done": small_done,
    }
    for name, *args in BACKWARD:
        backward[name](*args)
    links.drain()
    for copy in leaving:
        copy.wait()


def run_kernel(n_mp, tokens, cotangent, segments, weights, shards, vectors):
    rows, d = tokens.shape
    anywhere = pl.BlockSpec(memory_space=pl.ANY)
    blocks = rows // BLOCK
    pairs = d // BLOCK
    piece = d // 16
    low = lambda *shape: pltpu.VMEM(shape, LOW)
    full = lambda *shape: pltpu.VMEM(shape, F32)
    block_count = 3 * n_mp
    names = 256
    flops = 2 * rows * d * d * 12 * 3
    operands = (tokens, cotangent, segments, *weights, *shards, *vectors)
    return pl.pallas_call(
        functools.partial(layer_kernel, n_mp),
        out_shape=(
            jax.ShapeDtypeStruct((rows, d), LOW),
            jax.ShapeDtypeStruct((rows, d), F32),
            jax.ShapeDtypeStruct((3, d, d), LOW),
            jax.ShapeDtypeStruct((16, d), F32),
        ),
        in_specs=[anywhere] * len(operands),
        out_specs=(anywhere,) * 4,
        scratch_shapes=[
            low(rows, d),
            low(rows, d),
            pltpu.VMEM(segments.shape, jnp.int32),
            full(*shards[0].shape),
            full(*shards[1].shape),
            full(len(vectors), *vectors[0].shape),
            full(len(vectors), 1, d),
            low(rows, d),
            full(rows, d),
            low(3, d, d),
            full(16, d),
            low(3 * n_mp * d, d),
            low(block_count, 2, 4 * piece, d),
            low(block_count, 2, 2 * piece, d),
            low(block_count, 2, piece, d),
            low(3, n_mp, 2, piece, d),
            low(len(NEAR), 2, 4 * piece, d),
            low(3 * pairs, rows, BLOCK),
            low(3 * d, rows),
            low(blocks * pairs, 2 * BLOCK, BLOCK),
            low(rows, d),
            low(d, rows),
            full(rows, d),
            full(rows, BLOCK),
            low(rows, d),
            low(d, rows),
            full(rows, d),
            low(rows, d),
            low(n_mp, rows, d),
            low(n_mp, d, rows),
            low(n_mp, rows, d),
            full(blocks, BLOCK, BLOCK),
            full(n_mp, 8, d),
            full(6, 1, d // 2),
            full(3, 16, d),
            full(3, 16, d),
            full(n_mp, 1, d),
            full(n_mp, 16, d),
            pltpu.SemaphoreType.DMA((32,)),
            pltpu.SemaphoreType.DMA((names,)),
            pltpu.SemaphoreType.DMA((names,)),
        ],
        compiler_params=pltpu.CompilerParams(
            collective_id=0, has_side_effects=True, vmem_limit_bytes=63 << 20
        ),
        cost_estimate=pl.CostEstimate(flops=flops, bytes_accessed=1 << 24, transcendentals=1 << 21),
    )(*operands)


def finish_kernel(
    out,
    grad_tok,
    grad_w,
    small,
    out_to,
    grad_tok_to,
    query_to,
    key_to,
    value_to,
    attn_to,
    up_to,
    down_to,
    b_query_to,
    b_value_to,
    *refs,

):
    vectors_to, refs = refs[:7], refs[7:]
    held, wide, lines, parts, vectors, low_rows, full_rows, sems = refs
    d = held.shape[-1]
    shard = query_to.shape[0]
    pieces = d // shard
    count = 0

    def fetch(src, dst):
        nonlocal count
        copy = pltpu.make_async_copy(src, dst, sems.at[count])
        count += 1
        copy.start()
        return copy

    first = fetch(small, lines)
    loads = {}
    for g in range(3):
        for k in range(pieces):
            here = pl.ds(k * shard, shard)
            loads[g, k] = fetch(grad_w.at[g, here], held.at[g, here])
    passing = [fetch(out, low_rows), fetch(grad_tok, full_rows)]
    first.wait()
    for k in range(2):
        parts[k] = lines[k : k + 1, :shard]
    for k in range(vectors.shape[0]):
        for j in range(d // BLOCK):
            vectors[k, j : j + 1, :] = lines[2 + k : 3 + k, j * BLOCK : (j + 1) * BLOCK]
    stores = [fetch(parts.at[0], b_query_to), fetch(parts.at[1], b_value_to)]
    stores += [fetch(vectors.at[k], ref) for k, ref in enumerate(vectors_to)]
    for g in range(3):
        for k in range(pieces):
            loads[g, k].wait()

            def widen(r, g=g, k=k):
                here = at(k * shard + r * 16, 16, 16)
                wide[g, here, :] = held[g, here, :].astype(F32)

            loop(shard // 16, widen, unroll=2)
            here = pl.ds(k * shard, shard)
            if g == 0:
                stores.append(fetch(wide.at[0, here], (query_to, key_to, value_to, attn_to)[k]))
            else:
                stores.append(fetch(wide.at[g, here], (up_to, down_to)[g - 1].at[here]))
        if g == 0:
            for copy in passing:
                copy.wait()
            stores += [fetch(low_rows, out_to), fetch(full_rows, grad_tok_to)]
    for copy in stores:
        copy.wait()


def run_finish(shard, out, grad_tok, grad_w, small):
    d = out.shape[1]
    anywhere = pl.BlockSpec(memory_space=pl.ANY)
    full = lambda *shape: jax.ShapeDtypeStruct(shape, F32)
    shapes = (
        [jax.ShapeDtypeStruct(out.shape, LOW), full(*grad_tok.shape)]
        + [full(shard, d)] * 4
        + [full(d, d)] * 2
        + [full(1, shard)] * 2
        + [full(d // BLOCK, BLOCK)] * 7
    )
    return pl.pallas_call(
        finish_kernel,
        out_shape=tuple(shapes),
        in_specs=[anywhere] * 4,
        out_specs=(anywhere,) * len(shapes),
        scratch_shapes=[
            pltpu.VMEM(grad_w.shape, grad_w.dtype),
            pltpu.VMEM(grad_w.shape, F32),
            pltpu.VMEM(small.shape, F32),
            pltpu.VMEM((2, 1, shard), F32),
            pltpu.VMEM((7, d // BLOCK, BLOCK), F32),
            pltpu.VMEM(out.shape, LOW),
            pltpu.VMEM(grad_tok.shape, F32),
            pltpu.SemaphoreType.DMA((64,)),
        ],
        compiler_params=pltpu.CompilerParams(vmem_limit_bytes=60 << 20),
        cost_estimate=pl.CostEstimate(flops=0, bytes_accessed=1 << 24, transcendentals=0),
    )(out, grad_tok, grad_w, small)


def per_device(
    n_dp,
    n_mp,
    tokens,
    segment_ids,
    w_query,
    b_query,
    w_key,
    w_value,
    b_value,
    w_out,
    b_out,
    gain_one,
    shift_one,
    w_up,
    b_up,
    w_down,
    b_down,
    gain_two,
    shift_two,
    cotangent,
):
    d = tokens.shape[1]
    shard = d // n_mp
    vectors = (b_up, b_out, gain_one, shift_one, b_down, gain_two, shift_two)
    out, grad_tokens, grad_w, small = run_kernel(
        n_mp,
        tokens,
        cotangent,
        segment_ids.reshape(-1, BLOCK),
        (w_query.T, w_key.T, w_value.T, w_out, w_up, w_down),
        (b_query.reshape(1, -1), b_value.reshape(1, -1)),
        tuple(v.reshape(-1, BLOCK) for v in vectors),
    )
    if n_dp > PLANE:
        groups = [[k + PLANE * h for h in range(n_dp // PLANE)] for k in range(PLANE)]
        grad_w, small = lax.psum(
            (grad_w.astype(F32), small), "dp", axis_index_groups=groups
        )
    (
        out,
        grad_tokens,
        grad_w_query,
        grad_w_key,
        grad_w_value,
        grad_w_out,
        grad_w_up,
        grad_w_down,
        grad_b_query,
        grad_b_value,
        *grad_vectors,
    ) = run_finish(shard, out, grad_tokens, grad_w, small)
    grad_b_out, grad_gain_one, grad_shift_one, grad_b_down, grad_gain_two, grad_shift_two = [
        grad_vectors[k].reshape(-1) for k in range(6)
    ]
    return (
        out,
        grad_tokens,
        grad_w_query.T,
        grad_b_query.reshape(-1),
        grad_w_key.T,
        grad_w_value.T,
        grad_b_value.reshape(-1),
        grad_w_out,
        grad_b_out,
        grad_gain_one,
        grad_shift_one,
        grad_w_up,
        grad_vectors[6].reshape(-1),
        grad_w_down,
        grad_b_down,
        grad_gain_two,
        grad_shift_two,
    )


def solution(mesh):
    n_dp, n_mp = mesh.shape["dp"], mesh.shape["mp"]
    return jax.shard_map(
        functools.partial(per_device, n_dp, n_mp),
        mesh=mesh,
        in_specs=(
            P(("dp", "mp"), None),
            P("dp"),
            P(None, "mp"),
            P("mp"),
            P(None, "mp"),
            P(None, "mp"),
            P("mp"),
            P("mp", None),
            P(),
            P(),
            P(),
            P(None, "mp"),
            P("mp"),
            P("mp", None),
            P(),
            P(),
            P(),
            P(("dp", "mp"), None),
        ),
        out_specs=(
            P(("dp", "mp"), None),
            P(("dp", "mp"), None),
            P(None, "mp"),
            P("mp"),
            P(None, "mp"),
            P(None, "mp"),
            P("mp"),
            P("mp", None),
            P(),
            P(),
            P(),
            P(None, "mp"),
            P("mp"),
            P("mp", None),
            P(),
            P(),
            P(),
        ),
        check_vma=False,
    )
```

```python
import functools

import jax
import jax.numpy as jnp
from jax import lax
from jax.experimental import pallas as pl
from jax.experimental.pallas import tpu as pltpu
from jax.sharding import PartitionSpec as P

HD = 64
BLOCK = 128
TILE = 256
ROWS = 64
PLANE = 8
ATTEND_PARTS = 2
ATTEND_BACK_PARTS = 6
DOUBLED = (0, 1, 2)
SENDS = ((0, 1, 2), (0, 1, 2), (0, 1, 2))
NEAR = (2,)
GELU = 0.7978845608028654
FORWARD = (
    ("send", 0), ("send_biases",), ("send", 1), ("two", 0, 0), ("one", 0, 1), ("three", 0, 0),
    ("one", 0, 2), ("send", 2), ("two", 0, 1), ("two", 0, 2), ("masks",), ("biases",),
    ("done", 0, 0), ("three", 0, 1), ("one", 1, 1), ("three", 0, 2), ("two", 1, 0),
    ("one", 1, 2), ("done", 0, 2), ("done", 0, 1), ("two", 1, 1), ("project", 0),
    ("attend", 0, 0), ("attend", 0, 1), ("project", 1), ("two", 1, 2), ("attend", 1, 0),
    ("three", 1, 0), ("three", 1, 1), ("one", 2, 1), ("two", 2, 0), ("attend", 1, 1),
    ("done", 1, 0), ("attn_out",), ("norm_one",), ("one", 2, 2), ("done", 1, 1), ("up", 3),
    ("two", 2, 1), ("three", 1, 2), ("up", 0), ("done", 1, 2), ("two", 2, 2), ("up", 1),
    ("three", 2, 0), ("up", 2), ("three", 2, 1), ("down", 3), ("done", 2, 0), ("three", 2, 2),
    ("done", 2, 1), ("down", 0), ("down", 1), ("done", 2, 2), ("down", 2),
)
BACKWARD = (
    ("down", 2), ("halve", 2, 2), ("down", 1), ("quarter", 2, 2), ("halve", 2, 1), ("down", 0),
    ("halve", 2, 0), ("quarter", 2, 1), ("down", 3), ("up", 1), ("near", 2), ("eighth", 2, 2),
    ("halve", 1, 1), ("up", 2), ("eighth", 2, 1), ("halve", 1, 2), ("quarter", 1, 1), ("up", 3),
    ("halve", 2, 3), ("up", 0), ("quarter", 1, 2), ("halve", 1, 0), ("norm",), ("out",),
    ("attend", 0), ("eighth", 1, 1), ("halve", 1, 3), ("quarter", 1, 0), ("attend", 1),
    ("plane", 2, 1), ("attend", 2), ("quarter", 1, 3), ("eighth", 1, 2), ("attend", 3),
    ("attend", 4), ("quarter", 2, 3), ("attend", 5), ("eighth", 1, 0), ("plane", 1, 1),
    ("token",), ("project",), ("plane", 2, 2), ("halve", 0, 2), ("eighth", 1, 3),
    ("small_send",), ("halve", 0, 1), ("quarter", 0, 2), ("small_next", 0), ("plane", 1, 2),
    ("halve", 0, 3), ("halve", 0, 0), ("quarter", 0, 1), ("eighth", 0, 2), ("quarter", 0, 0),
    ("eighth", 0, 1), ("plane", 1, 0), ("plane", 0, 2), ("eighth", 2, 3), ("eighth", 0, 0),
    ("quarter", 0, 3), ("finish", 2), ("plane", 0, 1), ("plane", 0, 0), ("finish", 1),
    ("eighth", 0, 3), ("two", 2), ("small_next", 1), ("finish", 0), ("two", 1), ("two", 0),
    ("small_next", 2), ("three", 2), ("three", 1), ("done", 1), ("done", 2), ("three", 0),
    ("small_done",), ("done", 0),
)
MASKED = -1000000000.0
MESH = pl.DeviceIdType.MESH
F32 = jnp.float32
LOW = jnp.bfloat16


def dot(left, right):
    return jnp.dot(left, right, preferred_element_type=F32)


def dot_nt(left, right):
    return lax.dot_general(left, right, (((1,), (1,)), ((), ())), preferred_element_type=F32)


def mean(value):
    return jnp.mean(value, axis=-1, keepdims=True)


def total(value):
    return jnp.sum(value, axis=0, keepdims=True)


def at(start, size, unit):
    return pl.ds(pl.multiple_of(start, unit), size)


def loop(count, body, unroll=1):
    def step(index, carry):
        body(index)
        return carry

    lax.fori_loop(0, count, step, 0, unroll=unroll)


class Links:
    def __init__(self, send, recv):
        self.send, self.recv = send, recv
        self.names = {}
        self.used = 0
        self.open = []

    def index(self, name, width):
        if name not in self.names:
            self.names[name] = self.used
            self.used += width
        return self.names[name]

    def copy(self, name, src, dst, device, there=None, here=None):
        first = self.index(name, 1 if there is None else 4)
        going, coming = (first, first) if there is None else (first + there, first + here)
        return pltpu.make_async_remote_copy(
            src_ref=src,
            dst_ref=dst,
            send_sem=self.send.at[going],
            recv_sem=self.recv.at[coming],
            device_id=device,
            device_id_type=MESH,
        )

    def start(self, *args):
        copy = self.copy(*args)
        copy.start()
        self.open.append(copy)

    def wait(self, name, dst, device, there=None):
        self.copy(name, dst, dst, device, there, there).wait_recv()

    def drain(self):
        for copy in self.open:
            copy.wait_send()
        self.open = []


def layer_kernel(
    n_mp,
    tok_in,
    cot_in,
    seg_in,
    w_query,
    w_key,
    w_value,
    w_out,
    w_up,
    w_down,
    b_query_in,
    b_value_in,
    *refs,
):
    vectors_in, refs = refs[:7], refs[7:]
    (
        out_to,
        grad_tok_to,
        grad_w_to,
        grad_small_to,
        tok,
        cot,
        seg,
        b_query,
        b_value,
        vectors,
        lines,
        out,
        grad_tok,
        grad_w,
        grad_small,
        w,
        half_in,
        quarter_in,
        eighth_in,
        plane_in,
        near_in,
        qkv,
        grad_qkv_t,
        prob,
        ctx,
        ctx_t,
        unit_one,
        inv_one,
        normed,
        normed_t,
        acc,
        grad_low,
        act,
        act_t,
        slope,
        mask,
        bias_in,
        qkv_bias,
        small,
        small_in,
        small_up,
        small_plane,
        local_sem,
        send_sem,
        recv_sem,
    ) = refs
    b_up, b_out, gain_one, shift_one, b_down, gain_two, shift_two = [lines.at[k] for k in range(7)]
    rows, d = tok.shape
    group = n_mp * d
    shard = d // n_mp
    piece = d // 16
    pairs = d // BLOCK
    blocks = rows // BLOCK

    dp, me = lax.axis_index("dp"), lax.axis_index("mp")
    c, x, y = dp % 2, dp // 2 % 2, dp // 4 % 2
    core = (dp + 1 - 2 * c, me)
    x_side = (dp + 2 - 4 * x, me)
    y_side = (dp + 4 - 8 * y, me)

    ranks = (me + 1 - 2 * (me % 2), 2 - me // 2, 3 - 3 * (me // 2), me)
    others = range(n_mp - 1)

    def rows_of(start, size):
        return at(start, size, 16)

    barrier = pltpu.get_barrier_semaphore()
    partners = [core, x_side, y_side] + [(dp, ranks[k]) for k in others]
    for partner in partners:
        pl.semaphore_signal(barrier, inc=1, device_id=partner, device_id_type=MESH)

    count = 0

    def fetch(src, dst):
        nonlocal count
        copy = pltpu.make_async_copy(src, dst, local_sem.at[count])
        count += 1
        copy.start()
        return copy

    own_zero = [
        fetch(ref, w.at[rows_of(kind * d + me * shard, shard)])
        for kind, ref in enumerate((w_query, w_key, w_value, w_out))
    ]
    own_one = [fetch(w_up, w.at[rows_of(group + me * d, d)])]
    own_two = [fetch(w_down, w.at[rows_of(2 * group + me * d, d)])]
    own_w = (own_zero, own_one, own_two)
    own_b = [fetch(b_query_in, b_query), fetch(b_value_in, b_value)]
    own_b += [fetch(ref, vectors.at[k]) for k, ref in enumerate(vectors_in)]
    own_rows = [fetch(seg_in, seg), fetch(tok_in, tok), fetch(cot_in, cot)]

    pl.semaphore_wait(barrier, len(partners))

    links = Links(send_sem, recv_sem)

    def region(g, m, core_of, side):
        if g == 0:
            return (2 * core_of + side) * d + m * shard
        return g * group + m * d + core_of * (d // 2) + side * (d // 4)

    class Gather:
        def __init__(self, name, ref, mine, theirs):
            self.name, self.ref = name, ref
            self.mine, self.theirs = mine, theirs

        def at(self, start, size):
            return self.ref.at[rows_of(start, size)]

        def one(self):
            a = self.at(self.mine[0] + (2 * x + y) * piece, piece)
            b = self.at(self.mine[1] + (2 * y + x) * piece, piece)
            links.start((self.name, 1, 0), a, a, y_side)
            links.start((self.name, 1, 1), b, b, x_side)

        def joined(self, side):
            if side == 0:
                start, device = self.mine[0] + (2 * x + 1 - y) * piece, y_side
            else:
                start, device = self.mine[1] + (2 * y + 1 - x) * piece, x_side
            links.wait((self.name, 1, side), self.at(start, piece), device)

        def two(self, joined=None):
            (joined or self.joined)(0)
            a = self.at(self.mine[0] + 2 * x * piece, 2 * piece)
            links.start((self.name, 2, 0), a, a, x_side)
            (joined or self.joined)(1)
            b = self.at(self.mine[1] + 2 * y * piece, 2 * piece)
            links.start((self.name, 2, 1), b, b, y_side)

        def three(self):
            links.wait(
                (self.name, 2, 0), self.at(self.mine[0] + 2 * (1 - x) * piece, 2 * piece), x_side
            )
            a = self.at(self.mine[0], 4 * piece)
            links.start((self.name, 3, 0), a, a, core)
            links.wait(
                (self.name, 2, 1), self.at(self.mine[1] + 2 * (1 - y) * piece, 2 * piece), y_side
            )
            b = self.at(self.mine[1], 4 * piece)
            links.start((self.name, 3, 1), b, b, core)

        def done(self):
            for side in range(2):
                links.wait((self.name, 3, side), self.at(self.theirs[side], 4 * piece), core)

    def share(g, k, m, side):
        start = region(g, m, c, side)
        high, bit = (x, y) if side == 0 else (y, x)
        if k == 0 and g in DOUBLED:
            return w.at[rows_of(start + 2 * high * piece, 2 * piece)]
        return w.at[rows_of(start + (2 * high + bit) * piece, piece)]

    def send(g):
        for copy in own_w[g]:
            copy.wait()
        for k in SENDS[g]:
            for side in range(2):
                rows_in = share(g, k, me, side)
                links.start(("w", g, side), rows_in, rows_in, (dp, ranks[k]), ranks[k], me)

    gathers = {}
    for g in range(3):
        for k in others:
            m = ranks[k]
            gathers[g, k] = Gather(
                ("in", g, k),
                w,
                [region(g, m, c, side) for side in range(2)],
                [region(g, m, 1 - c, side) for side in range(2)],
            )

    def landed(g, k, side):
        m = ranks[k]
        links.wait(("w", g, side), share(g, k, m, side), (dp, m), m)

    def one(g, k):
        for side in range(2):
            landed(g, k, side)
        gathers[g, k].one()

    def two(g, k):
        whole = k == 0 and g in DOUBLED
        gathers[g, k].two(functools.partial(landed, g, k) if whole else None)

    def three(g, k):
        gathers[g, k].three()

    def done(g, k):
        gathers[g, k].done()

    def masks():
        for copy in own_rows:
            copy.wait()
        for b in range(blocks):
            line = seg[pl.ds(me * blocks + b, 1), :]
            across = jnp.broadcast_to(line, (BLOCK, BLOCK))
            mask[b] = jnp.where(across == across.T, 0.0, MASKED)

    def send_biases():
        for copy in own_b:
            copy.wait()
        for k in range(len(vectors_in)):
            parts = [vectors[k, j : j + 1, :] for j in range(d // BLOCK)]
            lines[k] = jnp.concatenate(parts, axis=1)
        pad = jnp.zeros((1, d - shard), F32)
        for k, ref in enumerate((b_query, b_value)):
            placed = jnp.broadcast_to(jnp.concatenate([ref[...], pad], axis=1), (8, d))
            bias_in[me, k : k + 1, :] = pltpu.roll(placed, me * shard, 1)[0:1, :]
        bias_in[me, 2:3, :] = b_up[...]
        for k in others:
            m = ranks[k]
            links.start("bias", bias_in.at[me], bias_in.at[me], (dp, m), m, me)

    def biases():
        for k in others:
            m = ranks[k]
            links.wait("bias", bias_in.at[m], (dp, m), m)
        row = jnp.zeros((2, d), F32)
        for m in range(n_mp):
            row = row + bias_in[m, 0:2, :]
        for h in range(2):
            columns = slice(h * (d // 2), (h + 1) * (d // 2))
            qkv_bias[h] = row[0:1, columns]
            qkv_bias[2 + h] = jnp.zeros((1, d // 2), F32)
            qkv_bias[4 + h] = row[1:2, columns]

    half_pairs = pairs // 2

    def half_of(k):
        return me // 2 if k == 0 else 1 - me // 2

    def project(k):
        half = half_of(k)

        def one_kind(kind):
            here = rows_of(kind * d + half * (d // 2), d // 2)
            part = dot_nt(tok[...], w[here, :]) + qkv_bias[2 * kind + half]
            for j in range(half_pairs):
                columns = part[:, j * BLOCK : (j + 1) * BLOCK]
                qkv[kind * pairs + half * half_pairs + j] = columns.astype(LOW)

        loop(3, one_kind, unroll=3)

    lane = lax.broadcasted_iota(jnp.int32, (1, BLOCK), 1)
    first = jnp.where(lane < HD, 1.0, 0.0).astype(LOW)
    second = jnp.where(lane < HD, 0.0, 1.0).astype(LOW)
    none = jnp.zeros((HD, BLOCK), LOW)

    def two_heads(value):
        return jnp.concatenate([value * first, value * second], axis=0)

    def two_heads_t(value):
        turned = value.T
        upper = jnp.concatenate([turned[:HD], none], axis=1)
        lower = jnp.concatenate([none, turned[HD:]], axis=1)
        return jnp.concatenate([upper, lower], axis=0)

    def softmax(score):
        expo = jnp.exp(score - jnp.max(score, axis=0, keepdims=True))
        return expo * (1.0 / jnp.sum(expo, axis=0, keepdims=True))

    def attend(b, p):
        here = at(b * BLOCK, BLOCK, BLOCK)
        columns = at(p * BLOCK, BLOCK, BLOCK)
        query = qkv[p, here, :]
        key = qkv[pairs + p, here, :]
        value = qkv[2 * pairs + p, here, :]
        score = dot_nt(two_heads(key), query) * HD**-0.5
        hidden = mask[b]
        both = jnp.concatenate(
            [softmax(score[:BLOCK] + hidden), softmax(score[BLOCK:] + hidden)], axis=0
        ).astype(LOW)
        prob[b * pairs + p] = both
        context = dot(two_heads_t(value), both).astype(LOW)
        ctx_t[columns, here] = context
        ctx[here, columns] = context.T

    def attend_part(k, part):
        count = blocks * half_pairs // ATTEND_PARTS

        def step(i):
            i = i + part * count
            attend(i % blocks, half_of(k) * half_pairs + i // blocks)

        loop(count, step, unroll=count)

    def attn_out():
        acc[...] = dot(ctx[...], w[3 * d : 4 * d, :])

    def norm_one():
        def step(r):
            here = at(r * ROWS, ROWS, ROWS)
            value = tok[here, :].astype(F32) + acc[here, :] + b_out[...]
            center = value - mean(value)
            inverse = lax.rsqrt(mean(center * center) + 1e-05)
            unit = center * inverse
            unit_one[here, :] = unit
            inv_one[here, :] = jnp.broadcast_to(inverse, (ROWS, BLOCK))
            normed[here, :] = (unit * gain_one[...] + shift_one[...]).astype(LOW)

        loop(rows // ROWS, step)

        def turn(r):
            here = at(r * BLOCK, BLOCK, BLOCK)
            normed_t[:, here] = normed[here, :].T

        loop(blocks, turn)

    def feed_up(k):
        m = ranks[k]
        acc[...] = dot(normed[...], w[rows_of(group + m * d, d), :]) + bias_in[m, 2:3, :]

        def gelu(r):
            here = at(r * 16, 16, 16)
            u = acc[here, :]
            square = u * u
            inner = jnp.tanh(u * (GELU + GELU * 0.044715 * square))
            cdf = 0.5 + 0.5 * inner
            act[m, here, :] = (u * cdf).astype(LOW)
            slope_in = 0.5 * GELU + (1.5 * 0.044715 * GELU) * square
            slope[m, here, :] = (cdf + u * (1.0 - inner * inner) * slope_in).astype(LOW)

        loop(rows // 16, gelu)

        def turn(r):
            here = at(r * BLOCK, BLOCK, BLOCK)
            act_t[m, :, here] = act[m, here, :].T

        loop(blocks, turn)

    def feed_down(k):
        m = ranks[k]
        part = dot(act[m], w[rows_of(2 * group + m * d, d), :])
        acc[...] = part if k == n_mp - 1 else acc[...] + part

    forward = {
        "send": send,
        "one": one,
        "two": two,
        "three": three,
        "done": done,
        "masks": masks,
        "send_biases": send_biases,
        "biases": biases,
        "project": project,
        "attend": attend_part,
        "attn_out": attn_out,
        "norm_one": norm_one,
        "up": feed_up,
        "down": feed_down,
    }
    for name, *args in FORWARD:
        forward[name](*args)
    links.drain()

    small[...] = jnp.zeros(small.shape, F32)

    def add_small(row, value):
        small[0, row : row + 1, :] = small[0, row : row + 1, :] + value

    def norm_two(r):
        here = at(r * ROWS, ROWS, ROWS)
        unit = unit_one[here, :]
        value = unit * gain_one[...] + shift_one[...] + acc[here, :] + b_down[...]
        center = value - mean(value)
        inverse = lax.rsqrt(mean(center * center) + 1e-05)
        unit = center * inverse
        out[here, :] = (unit * gain_two[...] + shift_two[...]).astype(LOW)
        grad = cot[here, :].astype(F32)
        scaled = grad * gain_two[...]
        grad_resid = inverse * (scaled - mean(scaled) - unit * mean(scaled * unit))
        acc[here, :] = grad_resid
        grad_low[here, :] = grad_resid.astype(LOW)
        add_small(5, total(grad_resid))
        add_small(6, total(grad * unit))
        add_small(7, total(grad))

    loop(rows // ROWS, norm_two)
    leaving = [fetch(out, out_to)]

    def block_of(g, s):
        return g * n_mp + s

    def add_rows(start, sources, offset, size):
        def one(k):
            here = rows_of(start + k * 16, 16)
            there = rows_of(offset + k * 16, 16)
            value = w[here, :].astype(F32)
            for source in sources:
                value = value + source[there, :].astype(F32)
            w[here, :] = value.astype(LOW)

        loop(size // 16, one)

    def halve(g, s):
        m, k = ranks[s], block_of(g, s)
        for side in range(2):
            links.start(
                ("half", k, side),
                w.at[rows_of(region(g, m, 1 - c, side), 4 * piece)],
                half_in.at[k, side],
                core,
            )

    def near(g):
        k = block_of(g, 0)
        for side in range(2):
            start = region(g, ranks[0], c, side)
            links.wait(("half", k, side), half_in.at[k, side], core)
            add_rows(start, (half_in.at[k, side],), 0, 4 * piece)
            links.start(
                ("near", g, side),
                w.at[rows_of(start, 4 * piece)],
                near_in.at[NEAR.index(g), side],
                (dp, ranks[0]),
            )

    def quarter(g, s):
        m, k = ranks[s], block_of(g, s)
        sources = []
        for side, (bit, device) in enumerate(((x, x_side), (y, y_side))):
            start = region(g, m, c, side)
            links.wait(("half", k, side), half_in.at[k, side], core)
            sources.append([half_in.at[k, side]])
            if s == n_mp - 1 and g in NEAR:
                arrived = near_in.at[NEAR.index(g), side]
                links.wait(("near", g, side), arrived, (dp, ranks[0]))
                sources[side].append(arrived)
            other = 2 * (1 - bit) * piece
            add_rows(start + other, sources[side], other, 2 * piece)
            links.start(
                ("quarter", k, side),
                w.at[rows_of(start + other, 2 * piece)],
                quarter_in.at[k, side],
                device,
            )
        for side, bit in enumerate((x, y)):
            start = region(g, m, c, side)
            own = 2 * bit * piece
            add_rows(start + own, sources[side], own, 2 * piece)

    def eighth(g, s):
        m, k = ranks[s], block_of(g, s)
        sides = ((x, y, x_side, y_side), (y, x, y_side, x_side))
        for side, (high, bit, before, device) in enumerate(sides):
            start = region(g, m, c, side) + 2 * high * piece
            links.wait(("quarter", k, side), quarter_in.at[k, side], before)
            other = (1 - bit) * piece
            add_rows(start + other, (quarter_in.at[k, side],), other, piece)
            links.start(
                ("eighth", k, side),
                w.at[rows_of(start + other, piece)],
                eighth_in.at[k, side],
                device,
            )
        for side, (high, bit, before, device) in enumerate(sides):
            start = region(g, m, c, side) + 2 * high * piece
            own = bit * piece
            add_rows(start + own, (quarter_in.at[k, side],), own, piece)

    def to_plane(g, s):
        m, k = ranks[s], block_of(g, s)
        for side, (high, bit, device) in enumerate(((x, y, y_side), (y, x, x_side))):
            start = region(g, m, c, side) + (2 * high + bit) * piece
            links.wait(("eighth", k, side), eighth_in.at[k, side], device)
            add_rows(start, (eighth_in.at[k, side],), 0, piece)
            if s < n_mp - 1:
                links.start(
                    ("plane", g, side),
                    w.at[rows_of(start, piece)],
                    plane_in.at[g, me, side],
                    (dp, m),
                    m,
                    me,
                )

    outs = [
        Gather(
            ("out", g),
            grad_w.at[g],
            [c * (d // 2) + side * (d // 4) for side in range(2)],
            [(1 - c) * (d // 2) + side * (d // 4) for side in range(2)],
        )
        for g in range(3)
    ]

    def finish(g):
        to_plane(g, n_mp - 1)
        senders = [ranks[k] for k in others if k or g not in NEAR]
        for side, (high, bit) in enumerate(((x, y), (y, x))):
            start = region(g, me, c, side) + (2 * high + bit) * piece
            goal = c * (d // 2) + side * (d // 4) + (2 * high + bit) * piece
            for m in senders:
                links.wait(("plane", g, side), plane_in.at[g, m, side], (dp, m), m)

            def step(k):
                value = w[rows_of(start + k * 16, 16), :].astype(F32)
                for m in senders:
                    value = value + plane_in[g, m, side, rows_of(k * 16, 16), :].astype(F32)
                grad_w[g, rows_of(goal + k * 16, 16), :] = value.astype(LOW)

            loop(piece // 16, step)
        outs[g].one()

    def spread(g):
        outs[g].two()

    def pair(g):
        outs[g].three()

    def leave(g):
        outs[g].done()
        leaving.append(fetch(grad_w.at[g], grad_w_to.at[g]))

    def down_back(k):
        m = ranks[k]
        here = rows_of(2 * group + m * d, d)
        small_up[m] = jnp.zeros((1, d), F32)

        def step(r):
            tile = rows_of(r * TILE, TILE)
            grad_up = dot_nt(grad_low[tile, :], w[here, :]) * slope[m, tile, :].astype(F32)
            act[m, tile, :] = grad_up.astype(LOW)
            small_up[m] = small_up[m] + total(grad_up)

        loop(rows // TILE, step, unroll=2)

        def weight(r):
            tile = rows_of(r * (d // 2), d // 2)
            there = rows_of(2 * group + m * d + r * (d // 2), d // 2)
            w[there, :] = dot(act_t[m, tile, :], grad_low[...]).astype(LOW)

        loop(2, weight, unroll=2)

    def up_back(k):
        m = ranks[k]
        here = rows_of(group + m * d, d)

        def step(r):
            tile = rows_of(r * TILE, TILE)
            acc[tile, :] = acc[tile, :] + dot_nt(act[m, tile, :], w[here, :])

        loop(rows // TILE, step, unroll=2)

        def weight(r):
            tile = rows_of(r * (d // 2), d // 2)
            there = rows_of(group + m * d + r * (d // 2), d // 2)
            w[there, :] = dot(normed_t[tile, :], act[m]).astype(LOW)

        loop(2, weight, unroll=2)

    def norm_back():
        def step(r):
            here = at(r * ROWS, ROWS, ROWS)
            grad = acc[here, :]
            unit = unit_one[here, :]
            scaled = grad * gain_one[...]
            inverse = inv_one[here, 0:1]
            grad_resid = inverse * (scaled - mean(scaled) - unit * mean(scaled * unit))
            grad_tok[here, :] = grad_resid
            grad_low[here, :] = grad_resid.astype(LOW)
            add_small(2, total(grad_resid))
            add_small(3, total(grad * unit))
            add_small(4, total(grad))

        loop(rows // ROWS, step)

    def out_back():
        def step(r):
            tile = rows_of(r * TILE, TILE)
            ctx[tile, :] = dot_nt(grad_low[tile, :], w[3 * d : 4 * d, :]).astype(LOW)

        loop(rows // TILE, step, unroll=2)

        def weight(r):
            tile = rows_of(r * (d // 2), d // 2)
            there = rows_of(3 * d + r * (d // 2), d // 2)
            w[there, :] = dot(ctx_t[tile, :], grad_low[...]).astype(LOW)

        loop(2, weight, unroll=2)

    def attend_back(index):
        b, p = index // pairs, index % pairs
        here = at(b * BLOCK, BLOCK, BLOCK)
        query = qkv[p, here, :]
        key = qkv[pairs + p, here, :]
        value = qkv[2 * pairs + p, here, :]
        grad = ctx[here, at(p * BLOCK, BLOCK, BLOCK)]
        both = prob[index]
        grad_prob = dot_nt(two_heads(value), grad)
        wide = both.astype(F32)

        def score_back(part, grad_part):
            return part * (grad_part - jnp.sum(part * grad_part, axis=0, keepdims=True))

        low_score = jnp.concatenate(
            [
                score_back(wide[:BLOCK], grad_prob[:BLOCK]),
                score_back(wide[BLOCK:], grad_prob[BLOCK:]),
            ],
            axis=0,
        ).astype(LOW)

        def beside(stack):
            return jnp.concatenate([stack[:BLOCK], stack[BLOCK:]], axis=1)

        def keep(kind, natural, turned):
            qkv[kind * pairs + p, here, :] = natural
            grad_qkv_t[at((kind * pairs + p) * BLOCK, BLOCK, BLOCK), here] = turned

        grad_query = (dot(two_heads_t(key), low_score) * HD**-0.5).astype(LOW)
        grad_key = (dot(beside(low_score), two_heads(query)) * HD**-0.5).astype(LOW)
        grad_value = dot(beside(both), two_heads(grad)).astype(LOW)
        keep(0, grad_query.T, grad_query)
        keep(1, grad_key, grad_key.T)
        keep(2, grad_value, grad_value.T)

    def attend_back_part(part):
        count = blocks * pairs // ATTEND_BACK_PARTS
        loop(count, lambda i: attend_back(part * count + i), unroll=count)

    def small_send():
        for k in range(pairs):
            columns = slice(k * BLOCK, (k + 1) * BLOCK)
            small[0, 0:1, columns] = total(qkv[k].astype(F32))
            small[0, 1:2, columns] = total(qkv[2 * pairs + k].astype(F32))
        for m in range(n_mp):
            small[0, 8 + m : 9 + m, :] = small_up[m]
        links.start(("small", 0), small.at[0], small_in.at[0], core)

    def small_next(k):
        before, device = ((core, x_side), (x_side, y_side), (y_side, None))[k]
        links.wait(("small", k), small_in.at[k], before)
        if device is None:
            small_plane[me] = small[k] + small_in[k]
            for s in others:
                m = ranks[s]
                links.start("small", small_plane.at[me], small_plane.at[me], (dp, m), m, me)
        else:
            small[k + 1] = small[k] + small_in[k]
            links.start(("small", k + 1), small.at[k + 1], small_in.at[k + 1], device)

    def small_done():
        for s in others:
            m = ranks[s]
            links.wait("small", small_plane.at[m], (dp, m), m)
        value = small_plane[0]
        for m in range(1, n_mp):
            value = value + small_plane[m]
        grad_small[...] = value
        ups = value[8:16, :]
        own = total(jnp.where(lax.broadcasted_iota(jnp.int32, ups.shape, 0) == me, ups, 0.0))
        grad_small[8:9, :] = own
        turned = pltpu.roll(value[0:8, :], (n_mp - me) % n_mp * shard, 1)
        grad_small[0:2, :] = turned[0:2, :]
        leaving.append(fetch(grad_small, grad_small_to))

    def token_back():
        def step(kind):
            whole = jnp.concatenate([qkv[kind * pairs + k] for k in range(pairs)], axis=1)
            grad_tok[...] = grad_tok[...] + dot(whole, w[rows_of(kind * d, d), :])

        loop(3, step)
        leaving.append(fetch(grad_tok, grad_tok_to))

    def project_back():
        def step(r):
            here = rows_of(r * (d // 2), d // 2)
            w[here, :] = dot(grad_qkv_t[here, :], tok[...]).astype(LOW)

        loop(6, step, unroll=2)

    backward = {
        "down": down_back,
        "up": up_back,
        "norm": norm_back,
        "out": out_back,
        "attend": attend_back_part,
        "token": token_back,
        "project": project_back,
        "halve": halve,
        "near": near,
        "quarter": quarter,
        "eighth": eighth,
        "plane": to_plane,
        "finish": finish,
        "two": spread,
        "three": pair,
        "done": leave,
        "small_send": small_send,
        "small_next": small_next,
        "small_done": small_done,
    }
    for name, *args in BACKWARD:
        backward[name](*args)
    links.drain()
    for copy in leaving:
        copy.wait()


def run_kernel(n_mp, tokens, cotangent, segments, weights, shards, vectors):
    rows, d = tokens.shape
    anywhere = pl.BlockSpec(memory_space=pl.ANY)
    blocks = rows // BLOCK
    pairs = d // BLOCK
    piece = d // 16
    low = lambda *shape: pltpu.VMEM(shape, LOW)
    full = lambda *shape: pltpu.VMEM(shape, F32)
    block_count = 3 * n_mp
    names = 256
    flops = 2 * rows * d * d * 12 * 3
    operands = (tokens, cotangent, segments, *weights, *shards, *vectors)
    return pl.pallas_call(
        functools.partial(layer_kernel, n_mp),
        out_shape=(
            jax.ShapeDtypeStruct((rows, d), LOW),
            jax.ShapeDtypeStruct((rows, d), F32),
            jax.ShapeDtypeStruct((3, d, d), LOW),
            jax.ShapeDtypeStruct((16, d), F32),
        ),
        in_specs=[anywhere] * len(operands),
        out_specs=(anywhere,) * 4,
        scratch_shapes=[
            low(rows, d),
            low(rows, d),
            pltpu.VMEM(segments.shape, jnp.int32),
            full(*shards[0].shape),
            full(*shards[1].shape),
            full(len(vectors), *vectors[0].shape),
            full(len(vectors), 1, d),
            low(rows, d),
            full(rows, d),
            low(3, d, d),
            full(16, d),
            low(3 * n_mp * d, d),
            low(block_count, 2, 4 * piece, d),
            low(block_count, 2, 2 * piece, d),
            low(block_count, 2, piece, d),
            low(3, n_mp, 2, piece, d),
            low(len(NEAR), 2, 4 * piece, d),
            low(3 * pairs, rows, BLOCK),
            low(3 * d, rows),
            low(blocks * pairs, 2 * BLOCK, BLOCK),
            low(rows, d),
            low(d, rows),
            full(rows, d),
            full(rows, BLOCK),
            low(rows, d),
            low(d, rows),
            full(rows, d),
            low(rows, d),
            low(n_mp, rows, d),
            low(n_mp, d, rows),
            low(n_mp, rows, d),
            full(blocks, BLOCK, BLOCK),
            full(n_mp, 8, d),
            full(6, 1, d // 2),
            full(3, 16, d),
            full(3, 16, d),
            full(n_mp, 1, d),
            full(n_mp, 16, d),
            pltpu.SemaphoreType.DMA((32,)),
            pltpu.SemaphoreType.DMA((names,)),
            pltpu.SemaphoreType.DMA((names,)),
        ],
        compiler_params=pltpu.CompilerParams(
            collective_id=0, has_side_effects=True, vmem_limit_bytes=63 << 20
        ),
        cost_estimate=pl.CostEstimate(flops=flops, bytes_accessed=1 << 24, transcendentals=1 << 21),
    )(*operands)


def finish_kernel(
    out,
    grad_tok,
    grad_w,
    small,
    out_to,
    grad_tok_to,
    query_to,
    key_to,
    value_to,
    attn_to,
    up_to,
    down_to,
    b_query_to,
    b_value_to,
    *refs,

):
    vectors_to, refs = refs[:7], refs[7:]
    held, wide, lines, parts, vectors, low_rows, full_rows, sems = refs
    d = held.shape[-1]
    shard = query_to.shape[0]
    pieces = d // shard
    count = 0

    def fetch(src, dst):
        nonlocal count
        copy = pltpu.make_async_copy(src, dst, sems.at[count])
        count += 1
        copy.start()
        return copy

    first = fetch(small, lines)
    loads = {}
    for g in range(3):
        for k in range(pieces):
            here = pl.ds(k * shard, shard)
            loads[g, k] = fetch(grad_w.at[g, here], held.at[g, here])
    passing = [fetch(out, low_rows), fetch(grad_tok, full_rows)]
    first.wait()
    for k in range(2):
        parts[k] = lines[k : k + 1, :shard]
    for k in range(vectors.shape[0]):
        for j in range(d // BLOCK):
            vectors[k, j : j + 1, :] = lines[2 + k : 3 + k, j * BLOCK : (j + 1) * BLOCK]
    stores = [fetch(parts.at[0], b_query_to), fetch(parts.at[1], b_value_to)]
    stores += [fetch(vectors.at[k], ref) for k, ref in enumerate(vectors_to)]
    for g in range(3):
        for k in range(pieces):
            loads[g, k].wait()

            def widen(r, g=g, k=k):
                here = at(k * shard + r * 16, 16, 16)
                wide[g, here, :] = held[g, here, :].astype(F32)

            loop(shard // 16, widen, unroll=2)
            here = pl.ds(k * shard, shard)
            if g == 0:
                stores.append(fetch(wide.at[0, here], (query_to, key_to, value_to, attn_to)[k]))
            else:
                stores.append(fetch(wide.at[g, here], (up_to, down_to)[g - 1].at[here]))
        if g == 0:
            for copy in passing:
                copy.wait()
            stores += [fetch(low_rows, out_to), fetch(full_rows, grad_tok_to)]
    for copy in stores:
        copy.wait()


def run_finish(shard, out, grad_tok, grad_w, small):
    d = out.shape[1]
    anywhere = pl.BlockSpec(memory_space=pl.ANY)
    full = lambda *shape: jax.ShapeDtypeStruct(shape, F32)
    shapes = (
        [jax.ShapeDtypeStruct(out.shape, LOW), full(*grad_tok.shape)]
        + [full(shard, d)] * 4
        + [full(d, d)] * 2
        + [full(1, shard)] * 2
        + [full(d // BLOCK, BLOCK)] * 7
    )
    return pl.pallas_call(
        finish_kernel,
        out_shape=tuple(shapes),
        in_specs=[anywhere] * 4,
        out_specs=(anywhere,) * len(shapes),
        scratch_shapes=[
            pltpu.VMEM(grad_w.shape, grad_w.dtype),
            pltpu.VMEM(grad_w.shape, F32),
            pltpu.VMEM(small.shape, F32),
            pltpu.VMEM((2, 1, shard), F32),
            pltpu.VMEM((7, d // BLOCK, BLOCK), F32),
            pltpu.VMEM(out.shape, LOW),
            pltpu.VMEM(grad_tok.shape, F32),
            pltpu.SemaphoreType.DMA((64,)),
        ],
        compiler_params=pltpu.CompilerParams(vmem_limit_bytes=60 << 20),
        cost_estimate=pl.CostEstimate(flops=0, bytes_accessed=1 << 24, transcendentals=0),
    )(out, grad_tok, grad_w, small)


def per_device(
    n_dp,
    n_mp,
    tokens,
    segment_ids,
    w_query,
    b_query,
    w_key,
    w_value,
    b_value,
    w_out,
    b_out,
    gain_one,
    shift_one,
    w_up,
    b_up,
    w_down,
    b_down,
    gain_two,
    shift_two,
    cotangent,
):
    d = tokens.shape[1]
    shard = d // n_mp
    vectors = (b_up, b_out, gain_one, shift_one, b_down, gain_two, shift_two)
    out, grad_tokens, grad_w, small = run_kernel(
        n_mp,
        tokens,
        cotangent,
        segment_ids.reshape(-1, BLOCK),
        (w_query.T, w_key.T, w_value.T, w_out, w_up, w_down),
        (b_query.reshape(1, -1), b_value.reshape(1, -1)),
        tuple(v.reshape(-1, BLOCK) for v in vectors),
    )
    if n_dp > PLANE:
        groups = [[k + PLANE * h for h in range(n_dp // PLANE)] for k in range(PLANE)]
        grad_w, small = lax.psum(
            (grad_w.astype(F32), small), "dp", axis_index_groups=groups
        )
    (
        out,
        grad_tokens,
        grad_w_query,
        grad_w_key,
        grad_w_value,
        grad_w_out,
        grad_w_up,
        grad_w_down,
        grad_b_query,
        grad_b_value,
        *grad_vectors,
    ) = run_finish(shard, out, grad_tokens, grad_w, small)
    grad_b_out, grad_gain_one, grad_shift_one, grad_b_down, grad_gain_two, grad_shift_two = [
        grad_vectors[k].reshape(-1) for k in range(6)
    ]
    return (
        out,
        grad_tokens,
        grad_w_query.T,
        grad_b_query.reshape(-1),
        grad_w_key.T,
        grad_w_value.T,
        grad_b_value.reshape(-1),
        grad_w_out,
        grad_b_out,
        grad_gain_one,
        grad_shift_one,
        grad_w_up,
        grad_vectors[6].reshape(-1),
        grad_w_down,
        grad_b_down,
        grad_gain_two,
        grad_shift_two,
    )


def solution(mesh):
    n_dp, n_mp = mesh.shape["dp"], mesh.shape["mp"]
    return jax.shard_map(
        functools.partial(per_device, n_dp, n_mp),
        mesh=mesh,
        in_specs=(
            P(("dp", "mp"), None),
            P("dp"),
            P(None, "mp"),
            P("mp"),
            P(None, "mp"),
            P(None, "mp"),
            P("mp"),
            P("mp", None),
            P(),
            P(),
            P(),
            P(None, "mp"),
            P("mp"),
            P("mp", None),
            P(),
            P(),
            P(),
            P(("dp", "mp"), None),
        ),
        out_specs=(
            P(("dp", "mp"), None),
            P(("dp", "mp"), None),
            P(None, "mp"),
            P("mp"),
            P(None, "mp"),
            P(None, "mp"),
            P("mp"),
            P("mp", None),
            P(),
            P(),
            P(),
            P(None, "mp"),
            P("mp"),
            P("mp", None),
            P(),
            P(),
            P(),
        ),
        check_vma=False,
    )
```

```python
import functools

import jax
import jax.numpy as jnp
from jax import lax
from jax.experimental import pallas as pl
from jax.experimental.pallas import tpu as pltpu
from jax.sharding import PartitionSpec as P

HD = 64
BLOCK = 128
TILE = 256
ROWS = 64
PLANE = 8
ATTEND_PARTS = 2
ATTEND_BACK_PARTS = 6
DOUBLED = (0, 1, 2)
SENDS = ((0, 1, 2), (0, 1, 2), (0, 1, 2))
NEAR = (2,)
SEMI = (1, 0)
GELU = 0.7978845608028654
FORWARD = (
    ("send", 0), ("send_biases",), ("send", 1), ("two", 0, 0), ("one", 0, 1), ("three", 0, 0),
    ("one", 0, 2), ("send", 2), ("two", 0, 1), ("two", 0, 2), ("masks",), ("biases",),
    ("done", 0, 0), ("three", 0, 1), ("one", 1, 1), ("three", 0, 2), ("two", 1, 0),
    ("one", 1, 2), ("done", 0, 2), ("done", 0, 1), ("two", 1, 1), ("project", 0),
    ("attend", 0, 0), ("attend", 0, 1), ("project", 1), ("two", 1, 2), ("attend", 1, 0),
    ("three", 1, 0), ("three", 1, 1), ("one", 2, 1), ("two", 2, 0), ("attend", 1, 1),
    ("done", 1, 0), ("attn_out",), ("norm_one",), ("one", 2, 2), ("done", 1, 1), ("up", 3),
    ("two", 2, 1), ("three", 1, 2), ("up", 0), ("done", 1, 2), ("two", 2, 2), ("up", 1),
    ("three", 2, 0), ("up", 2), ("three", 2, 1), ("down", 3), ("done", 2, 0), ("three", 2, 2),
    ("done", 2, 1), ("down", 0), ("down", 1), ("done", 2, 2), ("down", 2),
)
BACKWARD = (
    ("down", 1), ("halve", 2, 1), ("down", 0), ("halve", 2, 0), ("quarter", 2, 1), ("down", 2),
    ("halve", 2, 2), ("down", 3), ("quarter", 2, 2), ("near", 2), ("up", 1), ("halve", 1, 1),
    ("eighth", 2, 1), ("up", 0), ("halve", 1, 0), ("quarter", 1, 1), ("halve", 2, 3), ("up", 2),
    ("halve", 1, 2), ("eighth", 2, 2), ("up", 3), ("norm",), ("quarter", 1, 2),
    ("quarter", 1, 0), ("out",), ("halve", 1, 3), ("eighth", 1, 1), ("attend", 0),
    ("plane", 2, 2), ("attend", 1), ("attend", 2), ("attend", 3), ("attend", 4),
    ("quarter", 2, 3), ("attend", 5), ("eighth", 1, 2), ("quarter", 1, 3), ("plane", 2, 1),
    ("token",), ("project",), ("halve", 0, 1), ("small_send",), ("eighth", 2, 3),
    ("halve", 0, 0), ("plane", 1, 1), ("semi", 1), ("halve", 0, 2), ("quarter", 0, 1),
    ("plane", 1, 2), ("small_next", 0), ("quarter", 0, 0), ("eighth", 0, 1), ("quarter", 0, 2),
    ("halve", 0, 3), ("finish", 2), ("small_next", 1), ("plane", 0, 1), ("semi", 0),
    ("eighth", 0, 2), ("quarter", 0, 3), ("eighth", 1, 3), ("two", 2), ("plane", 0, 2),
    ("small_next", 2), ("eighth", 0, 3), ("finish", 1), ("finish", 0), ("two", 1), ("two", 0),
    ("small_done",), ("three", 1), ("three", 2), ("three", 0), ("done", 1), ("done", 2),
    ("done", 0),
)
MASKED = -1000000000.0
MESH = pl.DeviceIdType.MESH
F32 = jnp.float32
LOW = jnp.bfloat16


def dot(left, right):
    return jnp.dot(left, right, preferred_element_type=F32)


def dot_nt(left, right):
    return lax.dot_general(left, right, (((1,), (1,)), ((), ())), preferred_element_type=F32)


def mean(value):
    return jnp.mean(value, axis=-1, keepdims=True)


def total(value):
    return jnp.sum(value, axis=0, keepdims=True)


def at(start, size, unit):
    return pl.ds(pl.multiple_of(start, unit), size)


def loop(count, body, unroll=1):
    def step(index, carry):
        body(index)
        return carry

    lax.fori_loop(0, count, step, 0, unroll=unroll)


class Links:
    def __init__(self, send, recv):
        self.send, self.recv = send, recv
        self.names = {}
        self.used = 0
        self.open = []

    def index(self, name, width):
        if name not in self.names:
            self.names[name] = self.used
            self.used += width
        return self.names[name]

    def copy(self, name, src, dst, device, there=None, here=None):
        first = self.index(name, 1 if there is None else 4)
        going, coming = (first, first) if there is None else (first + there, first + here)
        return pltpu.make_async_remote_copy(
            src_ref=src,
            dst_ref=dst,
            send_sem=self.send.at[going],
            recv_sem=self.recv.at[coming],
            device_id=device,
            device_id_type=MESH,
        )

    def start(self, *args):
        copy = self.copy(*args)
        copy.start()
        self.open.append(copy)

    def wait(self, name, dst, device, there=None):
        self.copy(name, dst, dst, device, there, there).wait_recv()

    def drain(self):
        for copy in self.open:
            copy.wait_send()
        self.open = []


def layer_kernel(
    n_mp,
    tok_in,
    cot_in,
    seg_in,
    w_query,
    w_key,
    w_value,
    w_out,
    w_up,
    w_down,
    b_query_in,
    b_value_in,
    *refs,
):
    vectors_in, refs = refs[:7], refs[7:]
    (
        out_to,
        grad_tok_to,
        grad_w_to,
        grad_small_to,
        tok,
        cot,
        seg,
        b_query,
        b_value,
        vectors,
        lines,
        out,
        grad_tok,
        grad_w,
        grad_small,
        w,
        half_in,
        quarter_in,
        eighth_in,
        plane_in,
        near_in,
        semi_in,
        qkv,
        grad_qkv_t,
        prob,
        ctx,
        ctx_t,
        unit_one,
        inv_one,
        normed,
        normed_t,
        acc,
        grad_low,
        act,
        act_t,
        slope,
        mask,
        bias_in,
        qkv_bias,
        small,
        small_in,
        small_up,
        small_plane,
        local_sem,
        send_sem,
        recv_sem,
    ) = refs
    b_up, b_out, gain_one, shift_one, b_down, gain_two, shift_two = [lines.at[k] for k in range(7)]
    rows, d = tok.shape
    group = n_mp * d
    shard = d // n_mp
    piece = d // 16
    pairs = d // BLOCK
    blocks = rows // BLOCK

    dp, me = lax.axis_index("dp"), lax.axis_index("mp")
    c, x, y = dp % 2, dp // 2 % 2, dp // 4 % 2
    core = (dp + 1 - 2 * c, me)
    x_side = (dp + 2 - 4 * x, me)
    y_side = (dp + 4 - 8 * y, me)

    ranks = (me + 1 - 2 * (me % 2), 2 - me // 2, 3 - 3 * (me // 2), me)
    others = range(n_mp - 1)

    def rows_of(start, size):
        return at(start, size, 16)

    barrier = pltpu.get_barrier_semaphore()
    partners = [core, x_side, y_side] + [(dp, ranks[k]) for k in others]
    for partner in partners:
        pl.semaphore_signal(barrier, inc=1, device_id=partner, device_id_type=MESH)

    count = 0

    def fetch(src, dst):
        nonlocal count
        copy = pltpu.make_async_copy(src, dst, local_sem.at[count])
        count += 1
        copy.start()
        return copy

    own_zero = [
        fetch(ref, w.at[rows_of(kind * d + me * shard, shard)])
        for kind, ref in enumerate((w_query, w_key, w_value, w_out))
    ]
    own_one = [fetch(w_up, w.at[rows_of(group + me * d, d)])]
    own_two = [fetch(w_down, w.at[rows_of(2 * group + me * d, d)])]
    own_w = (own_zero, own_one, own_two)
    own_b = [fetch(b_query_in, b_query), fetch(b_value_in, b_value)]
    own_b += [fetch(ref, vectors.at[k]) for k, ref in enumerate(vectors_in)]
    own_rows = [fetch(seg_in, seg), fetch(tok_in, tok), fetch(cot_in, cot)]

    pl.semaphore_wait(barrier, len(partners))

    links = Links(send_sem, recv_sem)

    def region(g, m, core_of, side):
        if g == 0:
            return (2 * core_of + side) * d + m * shard
        return g * group + m * d + core_of * (d // 2) + side * (d // 4)

    class Gather:
        def __init__(self, name, ref, mine, theirs):
            self.name, self.ref = name, ref
            self.mine, self.theirs = mine, theirs

        def at(self, start, size):
            return self.ref.at[rows_of(start, size)]

        def one(self):
            a = self.at(self.mine[0] + (2 * x + y) * piece, piece)
            b = self.at(self.mine[1] + (2 * y + x) * piece, piece)
            links.start((self.name, 1, 0), a, a, y_side)
            links.start((self.name, 1, 1), b, b, x_side)

        def joined(self, side):
            if side == 0:
                start, device = self.mine[0] + (2 * x + 1 - y) * piece, y_side
            else:
                start, device = self.mine[1] + (2 * y + 1 - x) * piece, x_side
            links.wait((self.name, 1, side), self.at(start, piece), device)

        def two(self, joined=None):
            (joined or self.joined)(0)
            a = self.at(self.mine[0] + 2 * x * piece, 2 * piece)
            links.start((self.name, 2, 0), a, a, x_side)
            (joined or self.joined)(1)
            b = self.at(self.mine[1] + 2 * y * piece, 2 * piece)
            links.start((self.name, 2, 1), b, b, y_side)

        def three(self):
            links.wait(
                (self.name, 2, 0), self.at(self.mine[0] + 2 * (1 - x) * piece, 2 * piece), x_side
            )
            a = self.at(self.mine[0], 4 * piece)
            links.start((self.name, 3, 0), a, a, core)
            links.wait(
                (self.name, 2, 1), self.at(self.mine[1] + 2 * (1 - y) * piece, 2 * piece), y_side
            )
            b = self.at(self.mine[1], 4 * piece)
            links.start((self.name, 3, 1), b, b, core)

        def done(self):
            for side in range(2):
                links.wait((self.name, 3, side), self.at(self.theirs[side], 4 * piece), core)

    def share(g, k, m, side):
        start = region(g, m, c, side)
        high, bit = (x, y) if side == 0 else (y, x)
        if k == 0 and g in DOUBLED:
            return w.at[rows_of(start + 2 * high * piece, 2 * piece)]
        return w.at[rows_of(start + (2 * high + bit) * piece, piece)]

    def send(g):
        for copy in own_w[g]:
            copy.wait()
        for k in SENDS[g]:
            for side in range(2):
                rows_in = share(g, k, me, side)
                links.start(("w", g, side), rows_in, rows_in, (dp, ranks[k]), ranks[k], me)

    gathers = {}
    for g in range(3):
        for k in others:
            m = ranks[k]
            gathers[g, k] = Gather(
                ("in", g, k),
                w,
                [region(g, m, c, side) for side in range(2)],
                [region(g, m, 1 - c, side) for side in range(2)],
            )

    def landed(g, k, side):
        m = ranks[k]
        links.wait(("w", g, side), share(g, k, m, side), (dp, m), m)

    def one(g, k):
        for side in range(2):
            landed(g, k, side)
        gathers[g, k].one()

    def two(g, k):
        whole = k == 0 and g in DOUBLED
        gathers[g, k].two(functools.partial(landed, g, k) if whole else None)

    def three(g, k):
        gathers[g, k].three()

    def done(g, k):
        gathers[g, k].done()

    def masks():
        for copy in own_rows:
            copy.wait()
        for b in range(blocks):
            line = seg[pl.ds(me * blocks + b, 1), :]
            across = jnp.broadcast_to(line, (BLOCK, BLOCK))
            mask[b] = jnp.where(across == across.T, 0.0, MASKED)

    def send_biases():
        for copy in own_b:
            copy.wait()
        for k in range(len(vectors_in)):
            parts = [vectors[k, j : j + 1, :] for j in range(d // BLOCK)]
            lines[k] = jnp.concatenate(parts, axis=1)
        pad = jnp.zeros((1, d - shard), F32)
        for k, ref in enumerate((b_query, b_value)):
            placed = jnp.broadcast_to(jnp.concatenate([ref[...], pad], axis=1), (8, d))
            bias_in[me, k : k + 1, :] = pltpu.roll(placed, me * shard, 1)[0:1, :]
        bias_in[me, 2:3, :] = b_up[...]
        for k in others:
            m = ranks[k]
            links.start("bias", bias_in.at[me], bias_in.at[me], (dp, m), m, me)

    def biases():
        for k in others:
            m = ranks[k]
            links.wait("bias", bias_in.at[m], (dp, m), m)
        row = jnp.zeros((2, d), F32)
        for m in range(n_mp):
            row = row + bias_in[m, 0:2, :]
        for h in range(2):
            columns = slice(h * (d // 2), (h + 1) * (d // 2))
            qkv_bias[h] = row[0:1, columns]
            qkv_bias[2 + h] = jnp.zeros((1, d // 2), F32)
            qkv_bias[4 + h] = row[1:2, columns]

    half_pairs = pairs // 2

    def half_of(k):
        return me // 2 if k == 0 else 1 - me // 2

    def project(k):
        half = half_of(k)

        def one_kind(kind):
            here = rows_of(kind * d + half * (d // 2), d // 2)
            part = dot_nt(tok[...], w[here, :]) + qkv_bias[2 * kind + half]
            for j in range(half_pairs):
                columns = part[:, j * BLOCK : (j + 1) * BLOCK]
                qkv[kind * pairs + half * half_pairs + j] = columns.astype(LOW)

        loop(3, one_kind, unroll=3)

    lane = lax.broadcasted_iota(jnp.int32, (1, BLOCK), 1)
    first = jnp.where(lane < HD, 1.0, 0.0).astype(LOW)
    second = jnp.where(lane < HD, 0.0, 1.0).astype(LOW)
    none = jnp.zeros((HD, BLOCK), LOW)

    def two_heads(value):
        return jnp.concatenate([value * first, value * second], axis=0)

    def two_heads_t(value):
        turned = value.T
        upper = jnp.concatenate([turned[:HD], none], axis=1)
        lower = jnp.concatenate([none, turned[HD:]], axis=1)
        return jnp.concatenate([upper, lower], axis=0)

    def softmax(score):
        expo = jnp.exp(score - jnp.max(score, axis=0, keepdims=True))
        return expo * (1.0 / jnp.sum(expo, axis=0, keepdims=True))

    def attend(b, p):
        here = at(b * BLOCK, BLOCK, BLOCK)
        columns = at(p * BLOCK, BLOCK, BLOCK)
        query = qkv[p, here, :]
        key = qkv[pairs + p, here, :]
        value = qkv[2 * pairs + p, here, :]
        score = dot_nt(two_heads(key), query) * HD**-0.5
        hidden = mask[b]
        both = jnp.concatenate(
            [softmax(score[:BLOCK] + hidden), softmax(score[BLOCK:] + hidden)], axis=0
        ).astype(LOW)
        prob[b * pairs + p] = both
        context = dot(two_heads_t(value), both).astype(LOW)
        ctx_t[columns, here] = context
        ctx[here, columns] = context.T

    def attend_part(k, part):
        count = blocks * half_pairs // ATTEND_PARTS

        def step(i):
            i = i + part * count
            attend(i % blocks, half_of(k) * half_pairs + i // blocks)

        loop(count, step, unroll=count)

    def attn_out():
        acc[...] = dot(ctx[...], w[3 * d : 4 * d, :])

    def norm_one():
        def step(r):
            here = at(r * ROWS, ROWS, ROWS)
            value = tok[here, :].astype(F32) + acc[here, :] + b_out[...]
            center = value - mean(value)
            inverse = lax.rsqrt(mean(center * center) + 1e-05)
            unit = center * inverse
            unit_one[here, :] = unit
            inv_one[here, :] = jnp.broadcast_to(inverse, (ROWS, BLOCK))
            normed[here, :] = (unit * gain_one[...] + shift_one[...]).astype(LOW)

        loop(rows // ROWS, step, unroll=4)

        def turn(r):
            here = at(r * BLOCK, BLOCK, BLOCK)
            normed_t[:, here] = normed[here, :].T

        loop(blocks, turn)

    def feed_up(k):
        m = ranks[k]
        acc[...] = dot(normed[...], w[rows_of(group + m * d, d), :]) + bias_in[m, 2:3, :]

        def gelu(r):
            here = at(r * 16, 16, 16)
            u = acc[here, :]
            square = u * u
            inner = jnp.tanh(u * (GELU + GELU * 0.044715 * square))
            cdf = 0.5 + 0.5 * inner
            act[m, here, :] = (u * cdf).astype(LOW)
            slope_in = 0.5 * GELU + (1.5 * 0.044715 * GELU) * square
            slope[m, here, :] = (cdf + u * (1.0 - inner * inner) * slope_in).astype(LOW)

        loop(rows // 16, gelu, unroll=2)

        def turn(r):
            here = at(r * BLOCK, BLOCK, BLOCK)
            act_t[m, :, here] = act[m, here, :].T

        loop(blocks, turn)

    def feed_down(k):
        m = ranks[k]
        part = dot(act[m], w[rows_of(2 * group + m * d, d), :])
        acc[...] = part if k == n_mp - 1 else acc[...] + part

    forward = {
        "send": send,
        "one": one,
        "two": two,
        "three": three,
        "done": done,
        "masks": masks,
        "send_biases": send_biases,
        "biases": biases,
        "project": project,
        "attend": attend_part,
        "attn_out": attn_out,
        "norm_one": norm_one,
        "up": feed_up,
        "down": feed_down,
    }
    for name, *args in FORWARD:
        forward[name](*args)
    links.drain()

    small[...] = jnp.zeros(small.shape, F32)

    def add_small(row, value):
        small[0, row : row + 1, :] = small[0, row : row + 1, :] + value

    def norm_two(r):
        here = at(r * ROWS, ROWS, ROWS)
        unit = unit_one[here, :]
        value = unit * gain_one[...] + shift_one[...] + acc[here, :] + b_down[...]
        center = value - mean(value)
        inverse = lax.rsqrt(mean(center * center) + 1e-05)
        unit = center * inverse
        out[here, :] = (unit * gain_two[...] + shift_two[...]).astype(LOW)
        grad = cot[here, :].astype(F32)
        scaled = grad * gain_two[...]
        grad_resid = inverse * (scaled - mean(scaled) - unit * mean(scaled * unit))
        acc[here, :] = grad_resid
        grad_low[here, :] = grad_resid.astype(LOW)
        add_small(5, total(grad_resid))
        add_small(6, total(grad * unit))
        add_small(7, total(grad))

    loop(rows // ROWS, norm_two, unroll=8)
    leaving = [fetch(out, out_to)]

    def block_of(g, s):
        return g * n_mp + s

    def add_rows(start, sources, offset, size):
        def one(k):
            here = rows_of(start + k * 16, 16)
            there = rows_of(offset + k * 16, 16)
            value = w[here, :].astype(F32)
            for source in sources:
                value = value + source[there, :].astype(F32)
            w[here, :] = value.astype(LOW)

        loop(size // 16, one, unroll=3)

    def halve(g, s):
        m, k = ranks[s], block_of(g, s)
        for side in range(2):
            links.start(
                ("half", k, side),
                w.at[rows_of(region(g, m, 1 - c, side), 4 * piece)],
                half_in.at[k, side],
                core,
            )

    def near(g):
        k = block_of(g, 0)
        for side in range(2):
            start = region(g, ranks[0], c, side)
            links.wait(("half", k, side), half_in.at[k, side], core)
            add_rows(start, (half_in.at[k, side],), 0, 4 * piece)
            links.start(
                ("near", g, side),
                w.at[rows_of(start, 4 * piece)],
                near_in.at[NEAR.index(g), side],
                (dp, ranks[0]),
            )

    def quarter(g, s):
        m, k = ranks[s], block_of(g, s)
        sources = []
        for side, (bit, device) in enumerate(((x, x_side), (y, y_side))):
            start = region(g, m, c, side)
            links.wait(("half", k, side), half_in.at[k, side], core)
            sources.append([half_in.at[k, side]])
            if s == n_mp - 1 and g in NEAR:
                arrived = near_in.at[NEAR.index(g), side]
                links.wait(("near", g, side), arrived, (dp, ranks[0]))
                sources[side].append(arrived)
            other = 2 * (1 - bit) * piece
            add_rows(start + other, sources[side], other, 2 * piece)
            links.start(
                ("quarter", k, side),
                w.at[rows_of(start + other, 2 * piece)],
                quarter_in.at[k, side],
                device,
            )
        for side, bit in enumerate((x, y)):
            start = region(g, m, c, side)
            own = 2 * bit * piece
            add_rows(start + own, sources[side], own, 2 * piece)

    def semi(g):
        k = block_of(g, 0)
        for side, (bit, device) in enumerate(((x, x_side), (y, y_side))):
            start = region(g, ranks[0], c, side) + 2 * bit * piece
            links.wait(("quarter", k, side), quarter_in.at[k, side], device)
            add_rows(start, (quarter_in.at[k, side],), 0, 2 * piece)
            links.start(
                ("semi", g, side),
                w.at[rows_of(start, 2 * piece)],
                semi_in.at[SEMI.index(g), side],
                (dp, ranks[0]),
            )

    def eighth(g, s):
        m, k = ranks[s], block_of(g, s)
        sources = []
        sides = ((x, y, x_side, y_side), (y, x, y_side, x_side))
        for side, (high, bit, before, device) in enumerate(sides):
            start = region(g, m, c, side) + 2 * high * piece
            links.wait(("quarter", k, side), quarter_in.at[k, side], before)
            sources.append([quarter_in.at[k, side]])
            if s == n_mp - 1 and g in SEMI:
                arrived = semi_in.at[SEMI.index(g), side]
                links.wait(("semi", g, side), arrived, (dp, ranks[0]))
                sources[side].append(arrived)
            other = (1 - bit) * piece
            add_rows(start + other, sources[side], other, piece)
            links.start(
                ("eighth", k, side),
                w.at[rows_of(start + other, piece)],
                eighth_in.at[k, side],
                device,
            )
        for side, (high, bit, before, device) in enumerate(sides):
            start = region(g, m, c, side) + 2 * high * piece
            own = bit * piece
            add_rows(start + own, sources[side], own, piece)

    def to_plane(g, s):
        m, k = ranks[s], block_of(g, s)
        for side, (high, bit, device) in enumerate(((x, y, y_side), (y, x, x_side))):
            start = region(g, m, c, side) + (2 * high + bit) * piece
            links.wait(("eighth", k, side), eighth_in.at[k, side], device)
            add_rows(start, (eighth_in.at[k, side],), 0, piece)
            if s < n_mp - 1:
                links.start(
                    ("plane", g, side),
                    w.at[rows_of(start, piece)],
                    plane_in.at[g, me, side],
                    (dp, m),
                    m,
                    me,
                )

    outs = [
        Gather(
            ("out", g),
            grad_w.at[g],
            [c * (d // 2) + side * (d // 4) for side in range(2)],
            [(1 - c) * (d // 2) + side * (d // 4) for side in range(2)],
        )
        for g in range(3)
    ]

    def finish(g):
        to_plane(g, n_mp - 1)
        senders = [ranks[k] for k in others if k or g not in NEAR + SEMI]
        for side, (high, bit) in enumerate(((x, y), (y, x))):
            start = region(g, me, c, side) + (2 * high + bit) * piece
            goal = c * (d // 2) + side * (d // 4) + (2 * high + bit) * piece
            for m in senders:
                links.wait(("plane", g, side), plane_in.at[g, m, side], (dp, m), m)

            def step(k):
                value = w[rows_of(start + k * 16, 16), :].astype(F32)
                for m in senders:
                    value = value + plane_in[g, m, side, rows_of(k * 16, 16), :].astype(F32)
                grad_w[g, rows_of(goal + k * 16, 16), :] = value.astype(LOW)

            loop(piece // 16, step, unroll=3)
        outs[g].one()

    def spread(g):
        outs[g].two()

    def pair(g):
        outs[g].three()

    def leave(g):
        outs[g].done()
        leaving.append(fetch(grad_w.at[g], grad_w_to.at[g]))

    def down_back(k):
        m = ranks[k]
        here = rows_of(2 * group + m * d, d)
        small_up[m] = jnp.zeros((1, d), F32)

        def step(r):
            tile = rows_of(r * TILE, TILE)
            grad_up = dot_nt(grad_low[tile, :], w[here, :]) * slope[m, tile, :].astype(F32)
            act[m, tile, :] = grad_up.astype(LOW)
            small_up[m] = small_up[m] + total(grad_up)

        loop(rows // TILE, step, unroll=2)

        def weight(r):
            tile = rows_of(r * (d // 2), d // 2)
            there = rows_of(2 * group + m * d + r * (d // 2), d // 2)
            w[there, :] = dot(act_t[m, tile, :], grad_low[...]).astype(LOW)

        loop(2, weight, unroll=2)

    def up_back(k):
        m = ranks[k]
        here = rows_of(group + m * d, d)

        def step(r):
            tile = rows_of(r * TILE, TILE)
            acc[tile, :] = acc[tile, :] + dot_nt(act[m, tile, :], w[here, :])

        loop(rows // TILE, step, unroll=2)

        def weight(r):
            tile = rows_of(r * (d // 2), d // 2)
            there = rows_of(group + m * d + r * (d // 2), d // 2)
            w[there, :] = dot(normed_t[tile, :], act[m]).astype(LOW)

        loop(2, weight, unroll=2)

    def norm_back():
        def step(r):
            here = at(r * ROWS, ROWS, ROWS)
            grad = acc[here, :]
            unit = unit_one[here, :]
            scaled = grad * gain_one[...]
            inverse = inv_one[here, 0:1]
            grad_resid = inverse * (scaled - mean(scaled) - unit * mean(scaled * unit))
            grad_tok[here, :] = grad_resid
            grad_low[here, :] = grad_resid.astype(LOW)
            add_small(2, total(grad_resid))
            add_small(3, total(grad * unit))
            add_small(4, total(grad))

        loop(rows // ROWS, step, unroll=4)

    def out_back():
        def step(r):
            tile = rows_of(r * TILE, TILE)
            ctx[tile, :] = dot_nt(grad_low[tile, :], w[3 * d : 4 * d, :]).astype(LOW)

        loop(rows // TILE, step, unroll=2)

        def weight(r):
            tile = rows_of(r * (d // 2), d // 2)
            there = rows_of(3 * d + r * (d // 2), d // 2)
            w[there, :] = dot(ctx_t[tile, :], grad_low[...]).astype(LOW)

        loop(2, weight, unroll=2)

    def attend_back(index):
        b, p = index // pairs, index % pairs
        here = at(b * BLOCK, BLOCK, BLOCK)
        query = qkv[p, here, :]
        key = qkv[pairs + p, here, :]
        value = qkv[2 * pairs + p, here, :]
        grad = ctx[here, at(p * BLOCK, BLOCK, BLOCK)]
        both = prob[index]
        grad_prob = dot_nt(two_heads(value), grad)
        wide = both.astype(F32)

        def score_back(part, grad_part):
            return part * (grad_part - jnp.sum(part * grad_part, axis=0, keepdims=True))

        low_score = jnp.concatenate(
            [
                score_back(wide[:BLOCK], grad_prob[:BLOCK]),
                score_back(wide[BLOCK:], grad_prob[BLOCK:]),
            ],
            axis=0,
        ).astype(LOW)

        def beside(stack):
            return jnp.concatenate([stack[:BLOCK], stack[BLOCK:]], axis=1)

        def keep(kind, natural, turned):
            qkv[kind * pairs + p, here, :] = natural
            grad_qkv_t[at((kind * pairs + p) * BLOCK, BLOCK, BLOCK), here] = turned

        grad_query = (dot(two_heads_t(key), low_score) * HD**-0.5).astype(LOW)
        grad_key = (dot(beside(low_score), two_heads(query)) * HD**-0.5).astype(LOW)
        grad_value = dot(beside(both), two_heads(grad)).astype(LOW)
        keep(0, grad_query.T, grad_query)
        keep(1, grad_key, grad_key.T)
        keep(2, grad_value, grad_value.T)

    def attend_back_part(part):
        count = blocks * pairs // ATTEND_BACK_PARTS
        loop(count, lambda i: attend_back(part * count + i), unroll=count)

    def small_send():
        for k in range(pairs):
            columns = slice(k * BLOCK, (k + 1) * BLOCK)
            small[0, 0:1, columns] = total(qkv[k].astype(F32))
            small[0, 1:2, columns] = total(qkv[2 * pairs + k].astype(F32))
        for m in range(n_mp):
            small[0, 8 + m : 9 + m, :] = small_up[m]
        links.start(("small", 0), small.at[0], small_in.at[0], core)

    def small_next(k):
        before, device = ((core, x_side), (x_side, y_side), (y_side, None))[k]
        links.wait(("small", k), small_in.at[k], before)
        if device is None:
            small_plane[me] = small[k] + small_in[k]
            for s in others:
                m = ranks[s]
                links.start("small", small_plane.at[me], small_plane.at[me], (dp, m), m, me)
        else:
            small[k + 1] = small[k] + small_in[k]
            links.start(("small", k + 1), small.at[k + 1], small_in.at[k + 1], device)

    def small_done():
        for s in others:
            m = ranks[s]
            links.wait("small", small_plane.at[m], (dp, m), m)
        value = small_plane[0]
        for m in range(1, n_mp):
            value = value + small_plane[m]
        grad_small[...] = value
        ups = value[8:16, :]
        own = total(jnp.where(lax.broadcasted_iota(jnp.int32, ups.shape, 0) == me, ups, 0.0))
        grad_small[8:9, :] = own
        turned = pltpu.roll(value[0:8, :], (n_mp - me) % n_mp * shard, 1)
        grad_small[0:2, :] = turned[0:2, :]
        leaving.append(fetch(grad_small, grad_small_to))

    def token_back():
        def step(kind):
            whole = jnp.concatenate([qkv[kind * pairs + k] for k in range(pairs)], axis=1)
            grad_tok[...] = grad_tok[...] + dot(whole, w[rows_of(kind * d, d), :])

        loop(3, step)
        leaving.append(fetch(grad_tok, grad_tok_to))

    def project_back():
        def step(r):
            here = rows_of(r * (d // 2), d // 2)
            w[here, :] = dot(grad_qkv_t[here, :], tok[...]).astype(LOW)

        loop(6, step, unroll=2)

    backward = {
        "down": down_back,
        "up": up_back,
        "norm": norm_back,
        "out": out_back,
        "attend": attend_back_part,
        "token": token_back,
        "project": project_back,
        "halve": halve,
        "near": near,
        "semi": semi,
        "quarter": quarter,
        "eighth": eighth,
        "plane": to_plane,
        "finish": finish,
        "two": spread,
        "three": pair,
        "done": leave,
        "small_send": small_send,
        "small_next": small_next,
        "small_done": small_done,
    }
    for name, *args in BACKWARD:
        backward[name](*args)
    links.drain()
    for copy in leaving:
        copy.wait()


def run_kernel(n_mp, tokens, cotangent, segments, weights, shards, vectors):
    rows, d = tokens.shape
    anywhere = pl.BlockSpec(memory_space=pl.ANY)
    blocks = rows // BLOCK
    pairs = d // BLOCK
    piece = d // 16
    low = lambda *shape: pltpu.VMEM(shape, LOW)
    full = lambda *shape: pltpu.VMEM(shape, F32)
    block_count = 3 * n_mp
    names = 256
    flops = 2 * rows * d * d * 12 * 3
    operands = (tokens, cotangent, segments, *weights, *shards, *vectors)
    return pl.pallas_call(
        functools.partial(layer_kernel, n_mp),
        out_shape=(
            jax.ShapeDtypeStruct((rows, d), LOW),
            jax.ShapeDtypeStruct((rows, d), F32),
            jax.ShapeDtypeStruct((3, d, d), LOW),
            jax.ShapeDtypeStruct((16, d), F32),
        ),
        in_specs=[anywhere] * len(operands),
        out_specs=(anywhere,) * 4,
        scratch_shapes=[
            low(rows, d),
            low(rows, d),
            pltpu.VMEM(segments.shape, jnp.int32),
            full(*shards[0].shape),
            full(*shards[1].shape),
            full(len(vectors), *vectors[0].shape),
            full(len(vectors), 1, d),
            low(rows, d),
            full(rows, d),
            low(3, d, d),
            full(16, d),
            low(3 * n_mp * d, d),
            low(block_count, 2, 4 * piece, d),
            low(block_count, 2, 2 * piece, d),
            low(block_count, 2, piece, d),
            low(3, n_mp, 2, piece, d),
            low(len(NEAR), 2, 4 * piece, d),
            low(max(len(SEMI), 1), 2, 2 * piece, d),
            low(3 * pairs, rows, BLOCK),
            low(3 * d, rows),
            low(blocks * pairs, 2 * BLOCK, BLOCK),
            low(rows, d),
            low(d, rows),
            full(rows, d),
            full(rows, BLOCK),
            low(rows, d),
            low(d, rows),
            full(rows, d),
            low(rows, d),
            low(n_mp, rows, d),
            low(n_mp, d, rows),
            low(n_mp, rows, d),
            full(blocks, BLOCK, BLOCK),
            full(n_mp, 8, d),
            full(6, 1, d // 2),
            full(3, 16, d),
            full(3, 16, d),
            full(n_mp, 1, d),
            full(n_mp, 16, d),
            pltpu.SemaphoreType.DMA((32,)),
            pltpu.SemaphoreType.DMA((names,)),
            pltpu.SemaphoreType.DMA((names,)),
        ],
        compiler_params=pltpu.CompilerParams(
            collective_id=0, has_side_effects=True, vmem_limit_bytes=63 << 20
        ),
        cost_estimate=pl.CostEstimate(flops=flops, bytes_accessed=1 << 24, transcendentals=1 << 21),
    )(*operands)


def finish_kernel(
    out,
    grad_tok,
    grad_w,
    small,
    out_to,
    grad_tok_to,
    query_to,
    key_to,
    value_to,
    attn_to,
    up_to,
    down_to,
    b_query_to,
    b_value_to,
    *refs,

):
    vectors_to, refs = refs[:7], refs[7:]
    held, wide, lines, parts, vectors, low_rows, full_rows, sems = refs
    d = held.shape[-1]
    shard = query_to.shape[0]
    pieces = d // shard
    count = 0

    def fetch(src, dst):
        nonlocal count
        copy = pltpu.make_async_copy(src, dst, sems.at[count])
        count += 1
        copy.start()
        return copy

    first = fetch(small, lines)
    loads = {}
    for g in range(3):
        for k in range(pieces):
            here = pl.ds(k * shard, shard)
            loads[g, k] = fetch(grad_w.at[g, here], held.at[g, here])
    passing = [fetch(out, low_rows), fetch(grad_tok, full_rows)]
    first.wait()
    for k in range(2):
        parts[k] = lines[k : k + 1, :shard]
    for k in range(vectors.shape[0]):
        for j in range(d // BLOCK):
            vectors[k, j : j + 1, :] = lines[2 + k : 3 + k, j * BLOCK : (j + 1) * BLOCK]
    stores = [fetch(parts.at[0], b_query_to), fetch(parts.at[1], b_value_to)]
    stores += [fetch(vectors.at[k], ref) for k, ref in enumerate(vectors_to)]
    for g in range(3):
        for k in range(pieces):
            loads[g, k].wait()

            def widen(r, g=g, k=k):
                here = at(k * shard + r * 16, 16, 16)
                wide[g, here, :] = held[g, here, :].astype(F32)

            loop(shard // 16, widen, unroll=2)
            here = pl.ds(k * shard, shard)
            if g == 0:
                stores.append(fetch(wide.at[0, here], (query_to, key_to, value_to, attn_to)[k]))
            else:
                stores.append(fetch(wide.at[g, here], (up_to, down_to)[g - 1].at[here]))
        if g == 0:
            for copy in passing:
                copy.wait()
            stores += [fetch(low_rows, out_to), fetch(full_rows, grad_tok_to)]
    for copy in stores:
        copy.wait()


def run_finish(shard, out, grad_tok, grad_w, small):
    d = out.shape[1]
    anywhere = pl.BlockSpec(memory_space=pl.ANY)
    full = lambda *shape: jax.ShapeDtypeStruct(shape, F32)
    shapes = (
        [jax.ShapeDtypeStruct(out.shape, LOW), full(*grad_tok.shape)]
        + [full(shard, d)] * 4
        + [full(d, d)] * 2
        + [full(1, shard)] * 2
        + [full(d // BLOCK, BLOCK)] * 7
    )
    return pl.pallas_call(
        finish_kernel,
        out_shape=tuple(shapes),
        in_specs=[anywhere] * 4,
        out_specs=(anywhere,) * len(shapes),
        scratch_shapes=[
            pltpu.VMEM(grad_w.shape, grad_w.dtype),
            pltpu.VMEM(grad_w.shape, F32),
            pltpu.VMEM(small.shape, F32),
            pltpu.VMEM((2, 1, shard), F32),
            pltpu.VMEM((7, d // BLOCK, BLOCK), F32),
            pltpu.VMEM(out.shape, LOW),
            pltpu.VMEM(grad_tok.shape, F32),
            pltpu.SemaphoreType.DMA((64,)),
        ],
        compiler_params=pltpu.CompilerParams(vmem_limit_bytes=60 << 20),
        cost_estimate=pl.CostEstimate(flops=0, bytes_accessed=1 << 24, transcendentals=0),
    )(out, grad_tok, grad_w, small)


def per_device(
    n_dp,
    n_mp,
    tokens,
    segment_ids,
    w_query,
    b_query,
    w_key,
    w_value,
    b_value,
    w_out,
    b_out,
    gain_one,
    shift_one,
    w_up,
    b_up,
    w_down,
    b_down,
    gain_two,
    shift_two,
    cotangent,
):
    d = tokens.shape[1]
    shard = d // n_mp
    vectors = (b_up, b_out, gain_one, shift_one, b_down, gain_two, shift_two)
    out, grad_tokens, grad_w, small = run_kernel(
        n_mp,
        tokens,
        cotangent,
        segment_ids.reshape(-1, BLOCK),
        (w_query.T, w_key.T, w_value.T, w_out, w_up, w_down),
        (b_query.reshape(1, -1), b_value.reshape(1, -1)),
        tuple(v.reshape(-1, BLOCK) for v in vectors),
    )
    if n_dp > PLANE:
        groups = [[k + PLANE * h for h in range(n_dp // PLANE)] for k in range(PLANE)]
        grad_w, small = lax.psum(
            (grad_w.astype(F32), small), "dp", axis_index_groups=groups
        )
    (
        out,
        grad_tokens,
        grad_w_query,
        grad_w_key,
        grad_w_value,
        grad_w_out,
        grad_w_up,
        grad_w_down,
        grad_b_query,
        grad_b_value,
        *grad_vectors,
    ) = run_finish(shard, out, grad_tokens, grad_w, small)
    grad_b_out, grad_gain_one, grad_shift_one, grad_b_down, grad_gain_two, grad_shift_two = [
        grad_vectors[k].reshape(-1) for k in range(6)
    ]
    return (
        out,
        grad_tokens,
        grad_w_query.T,
        grad_b_query.reshape(-1),
        grad_w_key.T,
        grad_w_value.T,
        grad_b_value.reshape(-1),
        grad_w_out,
        grad_b_out,
        grad_gain_one,
        grad_shift_one,
        grad_w_up,
        grad_vectors[6].reshape(-1),
        grad_w_down,
        grad_b_down,
        grad_gain_two,
        grad_shift_two,
    )


def solution(mesh):
    n_dp, n_mp = mesh.shape["dp"], mesh.shape["mp"]
    return jax.shard_map(
        functools.partial(per_device, n_dp, n_mp),
        mesh=mesh,
        in_specs=(
            P(("dp", "mp"), None),
            P("dp"),
            P(None, "mp"),
            P("mp"),
            P(None, "mp"),
            P(None, "mp"),
            P("mp"),
            P("mp", None),
            P(),
            P(),
            P(),
            P(None, "mp"),
            P("mp"),
            P("mp", None),
            P(),
            P(),
            P(),
            P(("dp", "mp"), None),
        ),
        out_specs=(
            P(("dp", "mp"), None),
            P(("dp", "mp"), None),
            P(None, "mp"),
            P("mp"),
            P(None, "mp"),
            P(None, "mp"),
            P("mp"),
            P("mp", None),
            P(),
            P(),
            P(),
            P(None, "mp"),
            P("mp"),
            P("mp", None),
            P(),
            P(),
            P(),
        ),
        check_vma=False,
    )
```

```python
import functools

import jax
import jax.numpy as jnp
from jax import lax
from jax.experimental import pallas as pl
from jax.experimental.pallas import tpu as pltpu
from jax.sharding import PartitionSpec as P

HD = 64
BLOCK = 128
TILE = 256
ROWS = 64
PLANE = 8
ATTEND_PARTS = 2
ATTEND_BACK_PARTS = 6
DOUBLED = (0, 1, 2)
SENDS = ((0, 1, 2), (0, 1, 2), (0, 1, 2))
NEAR = (2,)
SEMI = (1, 0)
GELU = 0.7978845608028654
FORWARD = (
    ("send", 0), ("send_biases",), ("send", 1), ("two", 0, 0), ("one", 0, 1), ("one", 0, 2),
    ("two", 0, 1), ("send", 2), ("two", 0, 2), ("one", 1, 1), ("two", 1, 0), ("three", 0, 1),
    ("three", 0, 2), ("three", 0, 0), ("one", 1, 2), ("two", 1, 1), ("masks",), ("done", 0, 0),
    ("biases",), ("project", 0), ("attend", 0, 0), ("two", 1, 2), ("done", 0, 2),
    ("attend", 0, 1), ("done", 0, 1), ("project", 1), ("attend", 1, 0), ("three", 1, 0),
    ("attend", 1, 1), ("one", 2, 1), ("attn_out",), ("two", 2, 0), ("norm_one",), ("one", 2, 2),
    ("three", 1, 2), ("done", 1, 0), ("three", 1, 1), ("two", 2, 1), ("up", 3), ("done", 1, 1),
    ("done", 1, 2), ("up", 0), ("three", 2, 0), ("two", 2, 2), ("up", 1), ("up", 2),
    ("down", 3), ("three", 2, 1), ("done", 2, 0), ("down", 0), ("three", 2, 2), ("done", 2, 1),
    ("down", 1), ("done", 2, 2), ("down", 2),
)
BACKWARD = (
    ("down", 1), ("halve", 2, 1), ("down", 2), ("halve", 2, 2), ("quarter", 2, 1), ("down", 0),
    ("halve", 2, 0), ("down", 3), ("quarter", 2, 2), ("up", 1), ("halve", 1, 1), ("near", 2),
    ("eighth", 2, 1), ("up", 2), ("halve", 1, 2), ("quarter", 1, 1), ("up", 0),
    ("quarter", 1, 2), ("up", 3), ("halve", 1, 0), ("eighth", 2, 2), ("norm",), ("out",),
    ("attend", 0), ("eighth", 1, 1), ("halve", 2, 3), ("plane", 2, 1), ("quarter", 1, 0),
    ("attend", 1), ("attend", 2), ("attend", 3), ("attend", 4), ("plane", 2, 2),
    ("halve", 1, 3), ("eighth", 1, 2), ("attend", 5), ("quarter", 2, 3), ("quarter", 1, 3),
    ("token",), ("project",), ("halve", 0, 1), ("plane", 1, 1), ("semi", 1), ("eighth", 2, 3),
    ("plane", 1, 2), ("small_send",), ("quarter", 0, 1), ("halve", 0, 0), ("halve", 0, 2),
    ("small_next", 0), ("quarter", 0, 0), ("eighth", 0, 1), ("quarter", 0, 2), ("plane", 0, 1),
    ("halve", 0, 3), ("semi", 0), ("small_next", 1), ("eighth", 1, 3), ("eighth", 0, 2),
    ("quarter", 0, 3), ("finish", 1), ("plane", 0, 2), ("small_next", 2), ("finish", 2),
    ("eighth", 0, 3), ("two", 1), ("finish", 0), ("two", 2), ("three", 1), ("two", 0),
    ("three", 2), ("small_done",), ("done", 1), ("done", 2), ("three", 0), ("done", 0),
)
MASKED = -1000000000.0
MESH = pl.DeviceIdType.MESH
F32 = jnp.float32
LOW = jnp.bfloat16


def dot(left, right):
    return jnp.dot(left, right, preferred_element_type=F32)


def dot_nt(left, right):
    return lax.dot_general(left, right, (((1,), (1,)), ((), ())), preferred_element_type=F32)


def mean(value):
    return jnp.mean(value, axis=-1, keepdims=True)


def total(value):
    return jnp.sum(value, axis=0, keepdims=True)


def at(start, size, unit):
    return pl.ds(pl.multiple_of(start, unit), size)


def loop(count, body, unroll=1):
    def step(index, carry):
        body(index)
        return carry

    lax.fori_loop(0, count, step, 0, unroll=unroll)


class Links:
    def __init__(self, send, recv):
        self.send, self.recv = send, recv
        self.names = {}
        self.used = 0
        self.open = []

    def index(self, name, width):
        if name not in self.names:
            self.names[name] = self.used
            self.used += width
        return self.names[name]

    def copy(self, name, src, dst, device, there=None, here=None):
        first = self.index(name, 1 if there is None else 4)
        going, coming = (first, first) if there is None else (first + there, first + here)
        return pltpu.make_async_remote_copy(
            src_ref=src,
            dst_ref=dst,
            send_sem=self.send.at[going],
            recv_sem=self.recv.at[coming],
            device_id=device,
            device_id_type=MESH,
        )

    def start(self, *args):
        copy = self.copy(*args)
        copy.start()
        self.open.append(copy)

    def wait(self, name, dst, device, there=None):
        self.copy(name, dst, dst, device, there, there).wait_recv()

    def drain(self):
        for copy in self.open:
            copy.wait_send()
        self.open = []


def layer_kernel(
    n_mp,
    tok_in,
    cot_in,
    seg_in,
    w_query,
    w_key,
    w_value,
    w_out,
    w_up,
    w_down,
    b_query_in,
    b_value_in,
    *refs,
):
    vectors_in, refs = refs[:7], refs[7:]
    (
        out_to,
        grad_tok_to,
        grad_w_to,
        grad_small_to,
        tok,
        cot,
        seg,
        b_query,
        b_value,
        vectors,
        lines,
        out,
        grad_tok,
        grad_w,
        grad_small,
        w,
        half_in,
        quarter_in,
        eighth_in,
        plane_in,
        near_in,
        semi_in,
        qkv,
        grad_qkv_t,
        prob,
        ctx,
        ctx_t,
        unit_one,
        inv_one,
        normed,
        normed_t,
        acc,
        grad_low,
        act,
        act_t,
        slope,
        mask,
        bias_in,
        qkv_bias,
        small,
        small_in,
        small_up,
        small_plane,
        local_sem,
        send_sem,
        recv_sem,
    ) = refs
    b_up, b_out, gain_one, shift_one, b_down, gain_two, shift_two = [lines.at[k] for k in range(7)]
    rows, d = tok.shape
    group = n_mp * d
    shard = d // n_mp
    piece = d // 16
    pairs = d // BLOCK
    blocks = rows // BLOCK

    dp, me = lax.axis_index("dp"), lax.axis_index("mp")
    c, x, y = dp % 2, dp // 2 % 2, dp // 4 % 2
    core = (dp + 1 - 2 * c, me)
    x_side = (dp + 2 - 4 * x, me)
    y_side = (dp + 4 - 8 * y, me)

    ranks = (me + 1 - 2 * (me % 2), 2 - me // 2, 3 - 3 * (me // 2), me)
    others = range(n_mp - 1)

    def rows_of(start, size):
        return at(start, size, 16)

    barrier = pltpu.get_barrier_semaphore()
    partners = [core, x_side, y_side] + [(dp, ranks[k]) for k in others]
    for partner in partners:
        pl.semaphore_signal(barrier, inc=1, device_id=partner, device_id_type=MESH)

    count = 0

    def fetch(src, dst):
        nonlocal count
        copy = pltpu.make_async_copy(src, dst, local_sem.at[count])
        count += 1
        copy.start()
        return copy

    own_zero = [
        fetch(ref, w.at[rows_of(kind * d + me * shard, shard)])
        for kind, ref in enumerate((w_query, w_key, w_value, w_out))
    ]
    own_one = [fetch(w_up, w.at[rows_of(group + me * d, d)])]
    own_two = [fetch(w_down, w.at[rows_of(2 * group + me * d, d)])]
    own_w = (own_zero, own_one, own_two)
    own_b = [fetch(b_query_in, b_query), fetch(b_value_in, b_value)]
    own_b += [fetch(ref, vectors.at[k]) for k, ref in enumerate(vectors_in)]
    own_rows = [fetch(seg_in, seg), fetch(tok_in, tok), fetch(cot_in, cot)]

    pl.semaphore_wait(barrier, len(partners))

    links = Links(send_sem, recv_sem)

    def region(g, m, core_of, side):
        if g == 0:
            return (2 * core_of + side) * d + m * shard
        return g * group + m * d + core_of * (d // 2) + side * (d // 4)

    class Gather:
        def __init__(self, name, ref, mine, theirs):
            self.name, self.ref = name, ref
            self.mine, self.theirs = mine, theirs

        def at(self, start, size):
            return self.ref.at[rows_of(start, size)]

        def one(self):
            a = self.at(self.mine[0] + (2 * x + y) * piece, piece)
            b = self.at(self.mine[1] + (2 * y + x) * piece, piece)
            links.start((self.name, 1, 0), a, a, y_side)
            links.start((self.name, 1, 1), b, b, x_side)

        def joined(self, side):
            if side == 0:
                start, device = self.mine[0] + (2 * x + 1 - y) * piece, y_side
            else:
                start, device = self.mine[1] + (2 * y + 1 - x) * piece, x_side
            links.wait((self.name, 1, side), self.at(start, piece), device)

        def two(self, joined=None):
            (joined or self.joined)(0)
            a = self.at(self.mine[0] + 2 * x * piece, 2 * piece)
            links.start((self.name, 2, 0), a, a, x_side)
            (joined or self.joined)(1)
            b = self.at(self.mine[1] + 2 * y * piece, 2 * piece)
            links.start((self.name, 2, 1), b, b, y_side)

        def three(self):
            links.wait(
                (self.name, 2, 0), self.at(self.mine[0] + 2 * (1 - x) * piece, 2 * piece), x_side
            )
            a = self.at(self.mine[0], 4 * piece)
            links.start((self.name, 3, 0), a, a, core)
            links.wait(
                (self.name, 2, 1), self.at(self.mine[1] + 2 * (1 - y) * piece, 2 * piece), y_side
            )
            b = self.at(self.mine[1], 4 * piece)
            links.start((self.name, 3, 1), b, b, core)

        def done(self):
            for side in range(2):
                links.wait((self.name, 3, side), self.at(self.theirs[side], 4 * piece), core)

    def share(g, k, m, side):
        start = region(g, m, c, side)
        high, bit = (x, y) if side == 0 else (y, x)
        if k == 0 and g in DOUBLED:
            return w.at[rows_of(start + 2 * high * piece, 2 * piece)]
        return w.at[rows_of(start + (2 * high + bit) * piece, piece)]

    def send(g):
        for copy in own_w[g]:
            copy.wait()
        for k in SENDS[g]:
            for side in range(2):
                rows_in = share(g, k, me, side)
                links.start(("w", g, side), rows_in, rows_in, (dp, ranks[k]), ranks[k], me)

    gathers = {}
    for g in range(3):
        for k in others:
            m = ranks[k]
            gathers[g, k] = Gather(
                ("in", g, k),
                w,
                [region(g, m, c, side) for side in range(2)],
                [region(g, m, 1 - c, side) for side in range(2)],
            )

    def landed(g, k, side):
        m = ranks[k]
        links.wait(("w", g, side), share(g, k, m, side), (dp, m), m)

    def one(g, k):
        for side in range(2):
            landed(g, k, side)
        gathers[g, k].one()

    def two(g, k):
        whole = k == 0 and g in DOUBLED
        gathers[g, k].two(functools.partial(landed, g, k) if whole else None)

    def three(g, k):
        gathers[g, k].three()

    def done(g, k):
        gathers[g, k].done()

    def masks():
        for copy in own_rows:
            copy.wait()
        for b in range(blocks):
            line = seg[pl.ds(me * blocks + b, 1), :]
            across = jnp.broadcast_to(line, (BLOCK, BLOCK))
            mask[b] = jnp.where(across == across.T, 0.0, MASKED)

    def send_biases():
        for copy in own_b:
            copy.wait()
        for k in range(len(vectors_in)):
            parts = [vectors[k, j : j + 1, :] for j in range(d // BLOCK)]
            lines[k] = jnp.concatenate(parts, axis=1)
        pad = jnp.zeros((1, d - shard), F32)
        for k, ref in enumerate((b_query, b_value)):
            placed = jnp.broadcast_to(jnp.concatenate([ref[...], pad], axis=1), (8, d))
            bias_in[me, k : k + 1, :] = pltpu.roll(placed, me * shard, 1)[0:1, :]
        bias_in[me, 2:3, :] = b_up[...]
        for k in others:
            m = ranks[k]
            links.start("bias", bias_in.at[me], bias_in.at[me], (dp, m), m, me)

    def biases():
        for k in others:
            m = ranks[k]
            links.wait("bias", bias_in.at[m], (dp, m), m)
        row = jnp.zeros((2, d), F32)
        for m in range(n_mp):
            row = row + bias_in[m, 0:2, :]
        for h in range(2):
            columns = slice(h * (d // 2), (h + 1) * (d // 2))
            qkv_bias[h] = row[0:1, columns]
            qkv_bias[2 + h] = jnp.zeros((1, d // 2), F32)
            qkv_bias[4 + h] = row[1:2, columns]

    half_pairs = pairs // 2

    def half_of(k):
        return me // 2 if k == 0 else 1 - me // 2

    def project(k):
        half = half_of(k)

        def one_kind(kind):
            here = rows_of(kind * d + half * (d // 2), d // 2)
            part = dot_nt(tok[...], w[here, :]) + qkv_bias[2 * kind + half]
            for j in range(half_pairs):
                columns = part[:, j * BLOCK : (j + 1) * BLOCK]
                qkv[kind * pairs + half * half_pairs + j] = columns.astype(LOW)

        loop(3, one_kind, unroll=3)

    lane = lax.broadcasted_iota(jnp.int32, (1, BLOCK), 1)
    first = jnp.where(lane < HD, 1.0, 0.0).astype(LOW)
    second = jnp.where(lane < HD, 0.0, 1.0).astype(LOW)
    none = jnp.zeros((HD, BLOCK), LOW)

    def two_heads(value):
        return jnp.concatenate([value * first, value * second], axis=0)

    def two_heads_t(value):
        turned = value.T
        upper = jnp.concatenate([turned[:HD], none], axis=1)
        lower = jnp.concatenate([none, turned[HD:]], axis=1)
        return jnp.concatenate([upper, lower], axis=0)

    def softmax(score):
        expo = jnp.exp(score - jnp.max(score, axis=0, keepdims=True))
        return expo * (1.0 / jnp.sum(expo, axis=0, keepdims=True))

    def attend(b, p):
        here = at(b * BLOCK, BLOCK, BLOCK)
        columns = at(p * BLOCK, BLOCK, BLOCK)
        query = qkv[p, here, :]
        key = qkv[pairs + p, here, :]
        value = qkv[2 * pairs + p, here, :]
        score = dot_nt(two_heads(key), query) * HD**-0.5
        hidden = mask[b]
        both = jnp.concatenate(
            [softmax(score[:BLOCK] + hidden), softmax(score[BLOCK:] + hidden)], axis=0
        ).astype(LOW)
        prob[b * pairs + p] = both
        context = dot(two_heads_t(value), both).astype(LOW)
        ctx_t[columns, here] = context
        ctx[here, columns] = context.T

    def attend_part(k, part):
        count = blocks * half_pairs // ATTEND_PARTS

        def step(i):
            i = i + part * count
            attend(i % blocks, half_of(k) * half_pairs + i // blocks)

        loop(count, step, unroll=count)

    def attn_out():
        acc[...] = dot(ctx[...], w[3 * d : 4 * d, :])

    def norm_one():
        def step(r):
            here = at(r * ROWS, ROWS, ROWS)
            value = tok[here, :].astype(F32) + acc[here, :] + b_out[...]
            center = value - mean(value)
            inverse = lax.rsqrt(mean(center * center) + 1e-05)
            unit = center * inverse
            unit_one[here, :] = unit
            inv_one[here, :] = jnp.broadcast_to(inverse, (ROWS, BLOCK))
            normed[here, :] = (unit * gain_one[...] + shift_one[...]).astype(LOW)

        loop(rows // ROWS, step, unroll=4)

        def turn(r):
            here = at(r * BLOCK, BLOCK, BLOCK)
            normed_t[:, here] = normed[here, :].T

        loop(blocks, turn)

    def feed_up(k):
        m = ranks[k]
        acc[...] = dot(normed[...], w[rows_of(group + m * d, d), :]) + bias_in[m, 2:3, :]

        def gelu(r):
            here = at(r * 16, 16, 16)
            u = acc[here, :]
            square = u * u
            inner = jnp.tanh(u * (GELU + GELU * 0.044715 * square))
            cdf = 0.5 + 0.5 * inner
            act[m, here, :] = (u * cdf).astype(LOW)
            slope_in = 0.5 * GELU + (1.5 * 0.044715 * GELU) * square
            slope[m, here, :] = (cdf + u * (1.0 - inner * inner) * slope_in).astype(LOW)

        loop(rows // 16, gelu, unroll=2)

        def turn(r):
            here = at(r * BLOCK, BLOCK, BLOCK)
            act_t[m, :, here] = act[m, here, :].T

        loop(blocks, turn)

    def feed_down(k):
        m = ranks[k]
        part = dot(act[m], w[rows_of(2 * group + m * d, d), :])
        acc[...] = part if k == n_mp - 1 else acc[...] + part

    forward = {
        "send": send,
        "one": one,
        "two": two,
        "three": three,
        "done": done,
        "masks": masks,
        "send_biases": send_biases,
        "biases": biases,
        "project": project,
        "attend": attend_part,
        "attn_out": attn_out,
        "norm_one": norm_one,
        "up": feed_up,
        "down": feed_down,
    }
    for name, *args in FORWARD:
        forward[name](*args)

    small[...] = jnp.zeros(small.shape, F32)

    def add_small(row, value):
        small[0, row : row + 1, :] = small[0, row : row + 1, :] + value

    def norm_two(r):
        here = at(r * ROWS, ROWS, ROWS)
        unit = unit_one[here, :]
        value = unit * gain_one[...] + shift_one[...] + acc[here, :] + b_down[...]
        center = value - mean(value)
        inverse = lax.rsqrt(mean(center * center) + 1e-05)
        unit = center * inverse
        out[here, :] = (unit * gain_two[...] + shift_two[...]).astype(LOW)
        grad = cot[here, :].astype(F32)
        scaled = grad * gain_two[...]
        grad_resid = inverse * (scaled - mean(scaled) - unit * mean(scaled * unit))
        acc[here, :] = grad_resid
        grad_low[here, :] = grad_resid.astype(LOW)
        add_small(5, total(grad_resid))
        add_small(6, total(grad * unit))
        add_small(7, total(grad))

    loop(rows // ROWS, norm_two, unroll=8)
    links.drain()
    leaving = [fetch(out, out_to)]

    def block_of(g, s):
        return g * n_mp + s

    def add_rows(start, sources, offset, size):
        def one(k):
            here = rows_of(start + k * 16, 16)
            there = rows_of(offset + k * 16, 16)
            value = w[here, :].astype(F32)
            for source in sources:
                value = value + source[there, :].astype(F32)
            w[here, :] = value.astype(LOW)

        loop(size // 16, one, unroll=3)

    def halve(g, s):
        m, k = ranks[s], block_of(g, s)
        for side in range(2):
            links.start(
                ("half", k, side),
                w.at[rows_of(region(g, m, 1 - c, side), 4 * piece)],
                half_in.at[k, side],
                core,
            )

    def near(g):
        k = block_of(g, 0)
        for side in range(2):
            start = region(g, ranks[0], c, side)
            links.wait(("half", k, side), half_in.at[k, side], core)
            add_rows(start, (half_in.at[k, side],), 0, 4 * piece)
            links.start(
                ("near", g, side),
                w.at[rows_of(start, 4 * piece)],
                near_in.at[NEAR.index(g), side],
                (dp, ranks[0]),
            )

    def quarter(g, s):
        m, k = ranks[s], block_of(g, s)
        sources = []
        for side, (bit, device) in enumerate(((x, x_side), (y, y_side))):
            start = region(g, m, c, side)
            links.wait(("half", k, side), half_in.at[k, side], core)
            sources.append([half_in.at[k, side]])
            if s == n_mp - 1 and g in NEAR:
                arrived = near_in.at[NEAR.index(g), side]
                links.wait(("near", g, side), arrived, (dp, ranks[0]))
                sources[side].append(arrived)
            other = 2 * (1 - bit) * piece
            add_rows(start + other, sources[side], other, 2 * piece)
            links.start(
                ("quarter", k, side),
                w.at[rows_of(start + other, 2 * piece)],
                quarter_in.at[k, side],
                device,
            )
        for side, bit in enumerate((x, y)):
            start = region(g, m, c, side)
            own = 2 * bit * piece
            add_rows(start + own, sources[side], own, 2 * piece)

    def semi(g):
        k = block_of(g, 0)
        for side, (bit, device) in enumerate(((x, x_side), (y, y_side))):
            start = region(g, ranks[0], c, side) + 2 * bit * piece
            links.wait(("quarter", k, side), quarter_in.at[k, side], device)
            add_rows(start, (quarter_in.at[k, side],), 0, 2 * piece)
            links.start(
                ("semi", g, side),
                w.at[rows_of(start, 2 * piece)],
                semi_in.at[SEMI.index(g), side],
                (dp, ranks[0]),
            )

    def eighth(g, s):
        m, k = ranks[s], block_of(g, s)
        sources = []
        sides = ((x, y, x_side, y_side), (y, x, y_side, x_side))
        for side, (high, bit, before, device) in enumerate(sides):
            start = region(g, m, c, side) + 2 * high * piece
            links.wait(("quarter", k, side), quarter_in.at[k, side], before)
            sources.append([quarter_in.at[k, side]])
            if s == n_mp - 1 and g in SEMI:
                arrived = semi_in.at[SEMI.index(g), side]
                links.wait(("semi", g, side), arrived, (dp, ranks[0]))
                sources[side].append(arrived)
            other = (1 - bit) * piece
            add_rows(start + other, sources[side], other, piece)
            links.start(
                ("eighth", k, side),
                w.at[rows_of(start + other, piece)],
                eighth_in.at[g * (n_mp - 1) + s - 1, side],
                device,
            )
        for side, (high, bit, before, device) in enumerate(sides):
            start = region(g, m, c, side) + 2 * high * piece
            own = bit * piece
            add_rows(start + own, sources[side], own, piece)

    def to_plane(g, s):
        m, k = ranks[s], block_of(g, s)
        for side, (high, bit, device) in enumerate(((x, y, y_side), (y, x, x_side))):
            start = region(g, m, c, side) + (2 * high + bit) * piece
            arrived = eighth_in.at[g * (n_mp - 1) + s - 1, side]
            links.wait(("eighth", k, side), arrived, device)
            add_rows(start, (arrived,), 0, piece)
            if s < n_mp - 1:
                links.start(
                    ("plane", g, side),
                    w.at[rows_of(start, piece)],
                    plane_in.at[g, me % 2, side],
                    (dp, m),
                    m,
                    me,
                )

    outs = [
        Gather(
            ("out", g),
            grad_w.at[g],
            [c * (d // 2) + side * (d // 4) for side in range(2)],
            [(1 - c) * (d // 2) + side * (d // 4) for side in range(2)],
        )
        for g in range(3)
    ]

    def finish(g):
        to_plane(g, n_mp - 1)
        senders = [ranks[k] for k in others if k or g not in NEAR + SEMI]
        for side, (high, bit) in enumerate(((x, y), (y, x))):
            start = region(g, me, c, side) + (2 * high + bit) * piece
            goal = c * (d // 2) + side * (d // 4) + (2 * high + bit) * piece
            for m in senders:
                links.wait(("plane", g, side), plane_in.at[g, m % 2, side], (dp, m), m)

            def step(k):
                value = w[rows_of(start + k * 16, 16), :].astype(F32)
                for m in senders:
                    value = value + plane_in[g, m % 2, side, rows_of(k * 16, 16), :].astype(F32)
                grad_w[g, rows_of(goal + k * 16, 16), :] = value.astype(LOW)

            loop(piece // 16, step, unroll=3)
        outs[g].one()

    def spread(g):
        outs[g].two()

    def pair(g):
        outs[g].three()

    def leave(g):
        outs[g].done()
        leaving.append(fetch(grad_w.at[g], grad_w_to.at[g]))

    def down_back(k):
        m = ranks[k]
        here = rows_of(2 * group + m * d, d)
        small_up[m] = jnp.zeros((1, d), F32)

        def step(r):
            tile = rows_of(r * TILE, TILE)
            grad_up = dot_nt(grad_low[tile, :], w[here, :]) * slope[m, tile, :].astype(F32)
            act[m, tile, :] = grad_up.astype(LOW)
            small_up[m] = small_up[m] + total(grad_up)

        loop(rows // TILE, step, unroll=2)

        def weight(r):
            tile = rows_of(r * (d // 2), d // 2)
            there = rows_of(2 * group + m * d + r * (d // 2), d // 2)
            w[there, :] = dot(act_t[m, tile, :], grad_low[...]).astype(LOW)

        loop(2, weight, unroll=2)

    def up_back(k):
        m = ranks[k]
        here = rows_of(group + m * d, d)

        def step(r):
            tile = rows_of(r * TILE, TILE)
            acc[tile, :] = acc[tile, :] + dot_nt(act[m, tile, :], w[here, :])

        loop(rows // TILE, step, unroll=2)

        def weight(r):
            tile = rows_of(r * (d // 2), d // 2)
            there = rows_of(group + m * d + r * (d // 2), d // 2)
            w[there, :] = dot(normed_t[tile, :], act[m]).astype(LOW)

        loop(2, weight, unroll=2)

    def norm_back():
        def step(r):
            here = at(r * ROWS, ROWS, ROWS)
            grad = acc[here, :]
            unit = unit_one[here, :]
            scaled = grad * gain_one[...]
            inverse = inv_one[here, 0:1]
            grad_resid = inverse * (scaled - mean(scaled) - unit * mean(scaled * unit))
            grad_tok[here, :] = grad_resid
            grad_low[here, :] = grad_resid.astype(LOW)
            add_small(2, total(grad_resid))
            add_small(3, total(grad * unit))
            add_small(4, total(grad))

        loop(rows // ROWS, step, unroll=4)

    def out_back():
        def step(r):
            tile = rows_of(r * TILE, TILE)
            ctx[tile, :] = dot_nt(grad_low[tile, :], w[3 * d : 4 * d, :]).astype(LOW)

        loop(rows // TILE, step, unroll=2)

        def weight(r):
            tile = rows_of(r * (d // 2), d // 2)
            there = rows_of(3 * d + r * (d // 2), d // 2)
            w[there, :] = dot(ctx_t[tile, :], grad_low[...]).astype(LOW)

        loop(2, weight, unroll=2)

    def attend_back(index):
        b, p = index // pairs, index % pairs
        here = at(b * BLOCK, BLOCK, BLOCK)
        query = qkv[p, here, :]
        key = qkv[pairs + p, here, :]
        value = qkv[2 * pairs + p, here, :]
        grad = ctx[here, at(p * BLOCK, BLOCK, BLOCK)]
        both = prob[index]
        grad_prob = dot_nt(two_heads(value), grad)
        wide = both.astype(F32)

        def score_back(part, grad_part):
            return part * (grad_part - jnp.sum(part * grad_part, axis=0, keepdims=True))

        low_score = jnp.concatenate(
            [
                score_back(wide[:BLOCK], grad_prob[:BLOCK]),
                score_back(wide[BLOCK:], grad_prob[BLOCK:]),
            ],
            axis=0,
        ).astype(LOW)

        def beside(stack):
            return jnp.concatenate([stack[:BLOCK], stack[BLOCK:]], axis=1)

        def keep(kind, natural, turned):
            qkv[kind * pairs + p, here, :] = natural
            grad_qkv_t[at((kind * pairs + p) * BLOCK, BLOCK, BLOCK), here] = turned

        grad_query = (dot(two_heads_t(key), low_score) * HD**-0.5).astype(LOW)
        grad_key = (dot(beside(low_score), two_heads(query)) * HD**-0.5).astype(LOW)
        grad_value = dot(beside(both), two_heads(grad)).astype(LOW)
        keep(0, grad_query.T, grad_query)
        keep(1, grad_key, grad_key.T)
        keep(2, grad_value, grad_value.T)

    def attend_back_part(part):
        count = blocks * pairs // ATTEND_BACK_PARTS
        loop(count, lambda i: attend_back(part * count + i), unroll=count)

    def small_send():
        for k in range(pairs):
            columns = slice(k * BLOCK, (k + 1) * BLOCK)
            small[0, 0:1, columns] = total(qkv[k].astype(F32))
            small[0, 1:2, columns] = total(qkv[2 * pairs + k].astype(F32))
        for m in range(n_mp):
            small[0, 8 + m : 9 + m, :] = small_up[m]
        links.start(("small", 0), small.at[0], small_in.at[0], core)

    def small_next(k):
        before, device = ((core, x_side), (x_side, y_side), (y_side, None))[k]
        links.wait(("small", k), small_in.at[k], before)
        if device is None:
            small_plane[me] = small[k] + small_in[k]
            for s in others:
                m = ranks[s]
                links.start("small", small_plane.at[me], small_plane.at[me], (dp, m), m, me)
        else:
            small[k + 1] = small[k] + small_in[k]
            links.start(("small", k + 1), small.at[k + 1], small_in.at[k + 1], device)

    def small_done():
        for s in others:
            m = ranks[s]
            links.wait("small", small_plane.at[m], (dp, m), m)
        value = small_plane[0]
        for m in range(1, n_mp):
            value = value + small_plane[m]
        grad_small[...] = value
        ups = value[8:16, :]
        own = total(jnp.where(lax.broadcasted_iota(jnp.int32, ups.shape, 0) == me, ups, 0.0))
        grad_small[8:9, :] = own
        turned = pltpu.roll(value[0:8, :], (n_mp - me) % n_mp * shard, 1)
        grad_small[0:2, :] = turned[0:2, :]
        leaving.append(fetch(grad_small, grad_small_to))

    def token_back():
        def step(kind):
            whole = jnp.concatenate([qkv[kind * pairs + k] for k in range(pairs)], axis=1)
            grad_tok[...] = grad_tok[...] + dot(whole, w[rows_of(kind * d, d), :])

        loop(3, step)
        leaving.append(fetch(grad_tok, grad_tok_to))

    def project_back():
        def step(r):
            here = rows_of(r * (d // 2), d // 2)
            w[here, :] = dot(grad_qkv_t[here, :], tok[...]).astype(LOW)

        loop(6, step, unroll=2)

    backward = {
        "down": down_back,
        "up": up_back,
        "norm": norm_back,
        "out": out_back,
        "attend": attend_back_part,
        "token": token_back,
        "project": project_back,
        "halve": halve,
        "near": near,
        "semi": semi,
        "quarter": quarter,
        "eighth": eighth,
        "plane": to_plane,
        "finish": finish,
        "two": spread,
        "three": pair,
        "done": leave,
        "small_send": small_send,
        "small_next": small_next,
        "small_done": small_done,
    }
    for name, *args in BACKWARD:
        backward[name](*args)
    links.drain()
    for copy in leaving:
        copy.wait()


def run_kernel(n_mp, tokens, cotangent, segments, weights, shards, vectors):
    rows, d = tokens.shape
    anywhere = pl.BlockSpec(memory_space=pl.ANY)
    blocks = rows // BLOCK
    pairs = d // BLOCK
    piece = d // 16
    low = lambda *shape: pltpu.VMEM(shape, LOW)
    full = lambda *shape: pltpu.VMEM(shape, F32)
    block_count = 3 * n_mp
    names = 256
    flops = 2 * rows * d * d * 12 * 3
    operands = (tokens, cotangent, segments, *weights, *shards, *vectors)
    return pl.pallas_call(
        functools.partial(layer_kernel, n_mp),
        out_shape=(
            jax.ShapeDtypeStruct((rows, d), LOW),
            jax.ShapeDtypeStruct((rows, d), F32),
            jax.ShapeDtypeStruct((3, d, d), LOW),
            jax.ShapeDtypeStruct((16, d), F32),
        ),
        in_specs=[anywhere] * len(operands),
        out_specs=(anywhere,) * 4,
        scratch_shapes=[
            low(rows, d),
            low(rows, d),
            pltpu.VMEM(segments.shape, jnp.int32),
            full(*shards[0].shape),
            full(*shards[1].shape),
            full(len(vectors), *vectors[0].shape),
            full(len(vectors), 1, d),
            low(rows, d),
            full(rows, d),
            low(3, d, d),
            full(16, d),
            low(3 * n_mp * d, d),
            low(block_count, 2, 4 * piece, d),
            low(block_count, 2, 2 * piece, d),
            low(block_count - 3, 2, piece, d),
            low(3, 2, 2, piece, d),
            low(len(NEAR), 2, 4 * piece, d),
            low(max(len(SEMI), 1), 2, 2 * piece, d),
            low(3 * pairs, rows, BLOCK),
            low(3 * d, rows),
            low(blocks * pairs, 2 * BLOCK, BLOCK),
            low(rows, d),
            low(d, rows),
            full(rows, d),
            full(rows, BLOCK),
            low(rows, d),
            low(d, rows),
            full(rows, d),
            low(rows, d),
            low(n_mp, rows, d),
            low(n_mp, d, rows),
            low(n_mp, rows, d),
            full(blocks, BLOCK, BLOCK),
            full(n_mp, 8, d),
            full(6, 1, d // 2),
            full(3, 16, d),
            full(3, 16, d),
            full(n_mp, 1, d),
            full(n_mp, 16, d),
            pltpu.SemaphoreType.DMA((32,)),
            pltpu.SemaphoreType.DMA((names,)),
            pltpu.SemaphoreType.DMA((names,)),
        ],
        compiler_params=pltpu.CompilerParams(
            collective_id=0, has_side_effects=True, vmem_limit_bytes=63 << 20
        ),
        cost_estimate=pl.CostEstimate(flops=flops, bytes_accessed=1 << 24, transcendentals=1 << 21),
    )(*operands)


def finish_kernel(
    out,
    grad_tok,
    grad_w,
    small,
    out_to,
    grad_tok_to,
    query_to,
    key_to,
    value_to,
    attn_to,
    up_to,
    down_to,
    b_query_to,
    b_value_to,
    *refs,

):
    vectors_to, refs = refs[:7], refs[7:]
    held, wide, lines, parts, vectors, low_rows, full_rows, sems = refs
    d = held.shape[-1]
    shard = query_to.shape[0]
    pieces = d // shard
    count = 0

    def fetch(src, dst):
        nonlocal count
        copy = pltpu.make_async_copy(src, dst, sems.at[count])
        count += 1
        copy.start()
        return copy

    first = fetch(small, lines)
    loads = {}
    for g in range(3):
        for k in range(pieces):
            here = pl.ds(k * shard, shard)
            loads[g, k] = fetch(grad_w.at[g, here], held.at[g, here])
    passing = [fetch(out, low_rows), fetch(grad_tok, full_rows)]
    first.wait()
    for k in range(2):
        parts[k] = lines[k : k + 1, :shard]
    for k in range(vectors.shape[0]):
        for j in range(d // BLOCK):
            vectors[k, j : j + 1, :] = lines[2 + k : 3 + k, j * BLOCK : (j + 1) * BLOCK]
    stores = [fetch(parts.at[0], b_query_to), fetch(parts.at[1], b_value_to)]
    stores += [fetch(vectors.at[k], ref) for k, ref in enumerate(vectors_to)]
    for g in range(3):
        for k in range(pieces):
            loads[g, k].wait()

            def widen(r, g=g, k=k):
                here = at(k * shard + r * 16, 16, 16)
                wide[g, here, :] = held[g, here, :].astype(F32)

            loop(shard // 16, widen, unroll=2)
            here = pl.ds(k * shard, shard)
            if g == 0:
                stores.append(fetch(wide.at[0, here], (query_to, key_to, value_to, attn_to)[k]))
            else:
                stores.append(fetch(wide.at[g, here], (up_to, down_to)[g - 1].at[here]))
        if g == 0:
            for copy in passing:
                copy.wait()
            stores += [fetch(low_rows, out_to), fetch(full_rows, grad_tok_to)]
    for copy in stores:
        copy.wait()


def run_finish(shard, out, grad_tok, grad_w, small):
    d = out.shape[1]
    anywhere = pl.BlockSpec(memory_space=pl.ANY)
    full = lambda *shape: jax.ShapeDtypeStruct(shape, F32)
    shapes = (
        [jax.ShapeDtypeStruct(out.shape, LOW), full(*grad_tok.shape)]
        + [full(shard, d)] * 4
        + [full(d, d)] * 2
        + [full(1, shard)] * 2
        + [full(d // BLOCK, BLOCK)] * 7
    )
    return pl.pallas_call(
        finish_kernel,
        out_shape=tuple(shapes),
        in_specs=[anywhere] * 4,
        out_specs=(anywhere,) * len(shapes),
        scratch_shapes=[
            pltpu.VMEM(grad_w.shape, grad_w.dtype),
            pltpu.VMEM(grad_w.shape, F32),
            pltpu.VMEM(small.shape, F32),
            pltpu.VMEM((2, 1, shard), F32),
            pltpu.VMEM((7, d // BLOCK, BLOCK), F32),
            pltpu.VMEM(out.shape, LOW),
            pltpu.VMEM(grad_tok.shape, F32),
            pltpu.SemaphoreType.DMA((64,)),
        ],
        compiler_params=pltpu.CompilerParams(vmem_limit_bytes=60 << 20),
        cost_estimate=pl.CostEstimate(flops=0, bytes_accessed=1 << 24, transcendentals=0),
    )(out, grad_tok, grad_w, small)


def per_device(
    n_dp,
    n_mp,
    tokens,
    segment_ids,
    w_query,
    b_query,
    w_key,
    w_value,
    b_value,
    w_out,
    b_out,
    gain_one,
    shift_one,
    w_up,
    b_up,
    w_down,
    b_down,
    gain_two,
    shift_two,
    cotangent,
):
    d = tokens.shape[1]
    shard = d // n_mp
    vectors = (b_up, b_out, gain_one, shift_one, b_down, gain_two, shift_two)
    out, grad_tokens, grad_w, small = run_kernel(
        n_mp,
        tokens,
        cotangent,
        segment_ids.reshape(-1, BLOCK),
        (w_query.T, w_key.T, w_value.T, w_out, w_up, w_down),
        (b_query.reshape(1, -1), b_value.reshape(1, -1)),
        tuple(v.reshape(-1, BLOCK) for v in vectors),
    )
    if n_dp > PLANE:
        groups = [[k + PLANE * h for h in range(n_dp // PLANE)] for k in range(PLANE)]
        grad_w, small = lax.psum(
            (grad_w.astype(F32), small), "dp", axis_index_groups=groups
        )
    (
        out,
        grad_tokens,
        grad_w_query,
        grad_w_key,
        grad_w_value,
        grad_w_out,
        grad_w_up,
        grad_w_down,
        grad_b_query,
        grad_b_value,
        *grad_vectors,
    ) = run_finish(shard, out, grad_tokens, grad_w, small)
    grad_b_out, grad_gain_one, grad_shift_one, grad_b_down, grad_gain_two, grad_shift_two = [
        grad_vectors[k].reshape(-1) for k in range(6)
    ]
    return (
        out,
        grad_tokens,
        grad_w_query.T,
        grad_b_query.reshape(-1),
        grad_w_key.T,
        grad_w_value.T,
        grad_b_value.reshape(-1),
        grad_w_out,
        grad_b_out,
        grad_gain_one,
        grad_shift_one,
        grad_w_up,
        grad_vectors[6].reshape(-1),
        grad_w_down,
        grad_b_down,
        grad_gain_two,
        grad_shift_two,
    )


def solution(mesh):
    n_dp, n_mp = mesh.shape["dp"], mesh.shape["mp"]
    return jax.shard_map(
        functools.partial(per_device, n_dp, n_mp),
        mesh=mesh,
        in_specs=(
            P(("dp", "mp"), None),
            P("dp"),
            P(None, "mp"),
            P("mp"),
            P(None, "mp"),
            P(None, "mp"),
            P("mp"),
            P("mp", None),
            P(),
            P(),
            P(),
            P(None, "mp"),
            P("mp"),
            P("mp", None),
            P(),
            P(),
            P(),
            P(("dp", "mp"), None),
        ),
        out_specs=(
            P(("dp", "mp"), None),
            P(("dp", "mp"), None),
            P(None, "mp"),
            P("mp"),
            P(None, "mp"),
            P(None, "mp"),
            P("mp"),
            P("mp", None),
            P(),
            P(),
            P(),
            P(None, "mp"),
            P("mp"),
            P("mp", None),
            P(),
            P(),
            P(),
        ),
        check_vma=False,
    )
```
